32 devices in a mesh: dp: 8 (over z, y), head: 4 (over x, core).
Axes of the slice: x: 2, y: 2, z: 4, core: 2. Of those that a mesh axis runs over, the one named last changes fastest.
Arguments:
- features: bfloat16 [32768, 768], P('dp'), may hold values from -6 to 6
- laplacian: float32 [8192, 16], P('dp'), may hold values from -4 to 4
- endpoints: int32 [32768, 2], P('dp'), may hold values from 0 to 31
- lengths: int32 [16, 16], P('dp'), may hold values from 1 to 128, 1536 in all within a row
- pairing: int32 [8, 16], P('dp'), may hold values from 0 to 15, each once within a row
- ident_weight: float32 [32, 768], P(None, ('dp', 'head')), may hold values from -1 to 1
- qkv_weight: float32 [768, 3, 768], P('dp', None, 'head'), may hold values from -0.21875 to 0.21875
- out_weight: float32 [768, 768], P('head', 'dp'), may hold values from -1.75 to 1.75
- ffn_weight: float32 [2, 768, 768], P(None, ('dp', 'head')), may hold values from -0.21875 to 0.21875
- norm_gains: float32 [3, 768], P(None, ('dp', 'head')), may hold values from 0.5 to 1.5
- ident_first: float32 [32, 768], P(None, ('dp', 'head')), may hold values from -0.015625 to 0.015625
- qkv_first: float32 [768, 3, 768], P('dp', None, 'head'), may hold values from -0.015625 to 0.015625
- out_first: float32 [768, 768], P('head', 'dp'), may hold values from -0.015625 to 0.015625
- ffn_first: float32 [2, 768, 768], P(None, ('dp', 'head')), may hold values from -0.015625 to 0.015625
- gains_first: float32 [3, 768], P(None, ('dp', 'head')), may hold values from -0.0625 to 0.0625
- ident_second: float32 [32, 768], P(None, ('dp', 'head')), may hold values from 7.0110023e-06 to 2.8044009e-05
- qkv_second: float32 [768, 3, 768], P('dp', None, 'head'), may hold values from 7.0110023e-06 to 2.8044009e-05
- out_second: float32 [768, 768], P('head', 'dp'), may hold values from 7.0110023e-06 to 2.8044009e-05
- ffn_second: float32 [2, 768, 768], P(None, ('dp', 'head')), may hold values from 7.0110023e-06 to 2.8044009e-05
- gains_second: float32 [3, 768], P(None, ('dp', 'head')), may hold values from 0.000112176036 to 0.00044870414
Outputs:
- grad_norm: float32 [], replicated
- total_loss: float32 [], replicated
- new_ident: float32 [32, 768], P(None, ('dp', 'head'))
- new_qkv: float32 [768, 3, 768], P('dp', None, 'head')
- new_out: float32 [768, 768], P('head', 'dp')
- new_ffn: float32 [2, 768, 768], P(None, ('dp', 'head'))
- new_gains: float32 [3, 768], P(None, ('dp', 'head'))
- first_ident: float32 [32, 768], P(None, ('dp', 'head'))
- first_qkv: float32 [768, 3, 768], P('dp', None, 'head')
- first_out: float32 [768, 768], P('head', 'dp')
- first_ffn: float32 [2, 768, 768], P(None, ('dp', 'head'))
- first_gains: float32 [3, 768], P(None, ('dp', 'head'))
- second_ident: float32 [32, 768], P(None, ('dp', 'head'))
- second_qkv: float32 [768, 3, 768], P('dp', None, 'head')
- second_out: float32 [768, 768], P('head', 'dp')
- second_ffn: float32 [2, 768, 768], P(None, ('dp', 'head'))
- second_gains: float32 [3, 768], P(None, ('dp', 'head'))
The draws below stay inside these ranges and needn't reach their ends.
All inputs are finite; a program needn't handle non-finite values.
Results may differ from the reference program's by a relative error of at most 0.0099.
Values may be sent and summed in bfloat16 or wider, within the bound.
No kernel may reach another device: no remote copies, remote signals or barrier semaphores. Data moves between devices by JAX's collectives and lax.ppermute only.
A program may use at most 192 MiB of HBM per device.

```python
import math
import jax
import jax.numpy as jnp
import numpy as np
from jax import lax

D = 768
HEADS = 32
HEAD_DIM = 24
FF = 768
LAP = 16
LEN = 128
NODE = 32
STEPS = 3
GRAPHS_DEV = 16
TOKG = 4096
TOKENS = 32768
GRAPHS = 128
N_DP = 8


def with_ends(entries, stream_key, low, top_value):
    longest = entries.shape.index(max(entries.shape))
    spots = []
    for shift in (0, 1):
        where = [jax.random.randint(jax.random.fold_in(stream_key, axis), (), 0, length) for axis, length in enumerate(entries.shape)]
        where[longest] = (where[longest] + shift) % entries.shape[longest]
        spots.append(tuple(where))
    return entries.at[spots[0]].set(low).at[spots[1]].set(top_value)


def level_of(rng, extent, shards, least, high):
    level, own = 1.0, jax.random.fold_in(rng, 6)
    for dim, blocks in shards:
        steps = jnp.exp(jax.random.uniform(jax.random.fold_in(own, dim), (blocks,), jnp.float32, least / len(shards), high / len(shards)))
        level = level * jnp.repeat(steps, extent[dim] // blocks).reshape([-1 if axis == dim else 1 for axis in range(len(extent))])
    return level


def profile(count, total, limit, skew):
    weights = [(1 << 20) // math.isqrt(grade ** skew) + 1 for grade in range(2, count + 1)]
    spare, given = total - limit - (count - 1), [1] * (count - 1)
    while spare > 0:
        free = [i for i in range(count - 1) if given[i] < limit]
        mass, left = sum([weights[i] for i in free]), spare
        for i in free:
            extra = min(limit - given[i], max(1, left * weights[i] // mass), spare)
            given[i] = given[i] + extra
            spare = spare - extra
    return np.array([limit] + given)


def uneven(key, number_of, total, most, skew):
    if number_of == 2:
        one = jax.random.randint(key, (), max(1, total - most), min(most, total - 1) + 1)
        return jnp.stack([one, total - one])
    sizes = jnp.asarray(profile(number_of, total, most, skew), jnp.int32)
    twos = (number_of - 1) // 2
    giver, receiver = sizes[1:1 + 2 * twos:2], sizes[2:2 + 2 * twos:2]
    room = jnp.minimum(giver - 1, most - receiver)
    passed = jax.random.randint(jax.random.fold_in(key, 1), (twos,), 0, 1 << 20) % (room + 1)
    sizes = sizes.at[1:1 + 2 * twos:2].set(giver - passed).at[2:2 + 2 * twos:2].set(receiver + passed)
    return sizes[jax.random.permutation(jax.random.fold_in(key, 2), number_of)]


def normal_values(rng, dims, scale, bound, split=(), kind=jnp.bfloat16):
    entries = scale * jax.random.normal(rng, dims, jnp.float32)
    if split:
        entries = entries * level_of(rng, dims, split, -0.22, 0.18)
    return jnp.clip(entries, -bound, bound).astype(kind)


def setup_inputs(seed: int = 0) -> dict:
    arg_keys = jax.random.split(jax.random.key(seed), 21)
    features = normal_values(arg_keys[0], (TOKENS, D), 1.0, 6.0, ((0, 8),))
    laplacian = normal_values(arg_keys[1], (2 * GRAPHS * NODE, LAP), 1.0, 4.0, ((0, 8),), jnp.float32)
    endpoints = with_ends(jax.random.randint(arg_keys[2], (TOKENS, 2), 0, NODE), jax.random.fold_in(arg_keys[2], 1), 0, NODE - 1).astype(jnp.int32)
    lengths = jax.vmap(lambda own: uneven(own, GRAPHS_DEV, GRAPHS_DEV * LEN * 3 // 4, LEN, 1))(jax.random.split(arg_keys[3], (2 * N_DP))).reshape((2 * N_DP, GRAPHS_DEV)).astype(jnp.int32)
    pairing = jax.vmap(lambda own: jax.random.permutation(own, GRAPHS_DEV))(jax.random.split(arg_keys[4], N_DP)).reshape((N_DP, GRAPHS_DEV)).astype(jnp.int32)
    ident_weight = normal_values(arg_keys[5], (2 * LAP, D), (2 * LAP) ** -0.5, 1.0, ((1, 32),), jnp.float32)
    qkv_weight = normal_values(arg_keys[6], (D, 3, D), D ** -0.5, 0.21875, ((0, 8), (2, 4)), jnp.float32)
    out_weight = normal_values(arg_keys[7], (D, D), (D // 64) ** -0.5, 1.75, ((0, 4), (1, 8)), jnp.float32)
    ffn_weight = normal_values(arg_keys[8], (2, D, FF), D ** -0.5, 0.21875, ((1, 32),), jnp.float32)
    norm_gains = jnp.clip(1.0 + 0.1 * jax.random.normal(arg_keys[9], (3, D), jnp.float32), 0.5, 1.5)
    ident_first = normal_values(arg_keys[10], (2 * LAP, D), (5.0 / (2 * LAP * D + 4 * D * D + 2 * D * FF + 3 * D) ** 0.5), 0.015625, ((1, 32),), jnp.float32)
    qkv_first = normal_values(arg_keys[11], (D, 3, D), (5.0 / (2 * LAP * D + 4 * D * D + 2 * D * FF + 3 * D) ** 0.5), 0.015625, ((0, 8), (2, 4)), jnp.float32)
    out_first = normal_values(arg_keys[12], (D, D), (5.0 / (2 * LAP * D + 4 * D * D + 2 * D * FF + 3 * D) ** 0.5), 0.015625, ((0, 4), (1, 8)), jnp.float32)
    ffn_first = normal_values(arg_keys[13], (2, D, FF), (5.0 / (2 * LAP * D + 4 * D * D + 2 * D * FF + 3 * D) ** 0.5), 0.015625, ((1, 32),), jnp.float32)
    gains_first = normal_values(arg_keys[14], (3, D), (20.0 / (2 * LAP * D + 4 * D * D + 2 * D * FF + 3 * D) ** 0.5), 0.0625, ((1, 32),), jnp.float32)
    ident_second = jnp.clip(jnp.exp(math.log(2.8044009013683535e-05) - 1.3862944 * jax.random.uniform(arg_keys[15], (2 * LAP, D), jnp.float32) ** level_of(arg_keys[15], (2 * LAP, D), ((1, 32),), -0.2, 0.2)), 7.011002253420884e-06, 2.8044009013683535e-05)
    qkv_second = jnp.clip(jnp.exp(math.log(2.8044009013683535e-05) - 1.3862944 * jax.random.uniform(arg_keys[16], (D, 3, D), jnp.float32) ** level_of(arg_keys[16], (D, 3, D), ((0, 8), (2, 4)), -0.2, 0.2)), 7.011002253420884e-06, 2.8044009013683535e-05)
    out_second = jnp.clip(jnp.exp(math.log(2.8044009013683535e-05) - 1.3862944 * jax.random.uniform(arg_keys[17], (D, D), jnp.float32) ** level_of(arg_keys[17], (D, D), ((0, 4), (1, 8)), -0.2, 0.2)), 7.011002253420884e-06, 2.8044009013683535e-05)
    ffn_second = jnp.clip(jnp.exp(math.log(2.8044009013683535e-05) - 1.3862944 * jax.random.uniform(arg_keys[18], (2, D, FF), jnp.float32) ** level_of(arg_keys[18], (2, D, FF), ((1, 32),), -0.2, 0.2)), 7.011002253420884e-06, 2.8044009013683535e-05)
    gains_second = jnp.clip(jnp.exp(math.log(0.00044870414) - 1.3862944 * jax.random.uniform(arg_keys[19], (3, D), jnp.float32) ** level_of(arg_keys[19], (3, D), ((1, 32),), -0.2, 0.2)), 0.000112176036, 0.00044870414)
    return dict(features=features, laplacian=laplacian, endpoints=endpoints, lengths=lengths, pairing=pairing, ident_weight=ident_weight, qkv_weight=qkv_weight, out_weight=out_weight, ffn_weight=ffn_weight, norm_gains=norm_gains, ident_first=ident_first, qkv_first=qkv_first, out_first=out_first, ffn_first=ffn_first, gains_first=gains_first, ident_second=ident_second, qkv_second=qkv_second, out_second=out_second, ffn_second=ffn_second, gains_second=gains_second)


HIGHEST = lax.Precision.HIGHEST
NORM_EPS = 1e-05
CLIP_AT = 5.0
STEP_RATES = (0.08, 0.02, 0.15, 0.02, 0.5)
BETA_ONE = 0.5
BETA_TWO = 0.5
DECAY = 0.01
ADAM_EPS = 1e-08
MASKED = -1e+30

@jax.custom_vjp
def low(v):
    return lax.optimization_barrier(v.astype(jnp.bfloat16)).astype(jnp.float32)

@jax.custom_vjp
def low_back(v):
    return v

def low_keep(v):
    return (low(v), None)

def low_pass(kept, grad):
    return (grad,)

def back_keep(v):
    return (v, None)

def back_low(kept, grad):
    return (low(grad),)
low.defvjp(low_keep, low_pass)
low_back.defvjp(back_keep, back_low)

def matmul(left, right):
    return jnp.dot(left, right, precision=HIGHEST)

def layer_norm(values, gain):
    centred = values - lax.optimization_barrier(jnp.mean(values, axis=-1, keepdims=True))
    spread = lax.optimization_barrier(jnp.mean(centred * centred, axis=-1, keepdims=True))
    return centred * lax.rsqrt(spread + NORM_EPS) * gain

def log_total(values, axis):
    top = lax.optimization_barrier(jnp.max(values, axis=axis, keepdims=True))
    return jnp.squeeze(top, axis) + jnp.log(lax.optimization_barrier(jnp.sum(jnp.exp(values - top), axis=axis)))

def identifiers(table, endpoints):
    graphs = endpoints.shape[0] // LEN
    nodes = table.reshape(graphs, NODE, LAP)
    picks = (endpoints.reshape(graphs, LEN, 2)[..., None] == jnp.arange(NODE, dtype=jnp.int32)).astype(jnp.float32)
    found = jnp.einsum('glan,gnc->glac', picks, nodes, precision=HIGHEST)
    return found.reshape(graphs * LEN, 2 * LAP)

def summarize(params, features, table, endpoints, lens):
    ident_weight, qkv_weight, out_weight, ffn_weight, norm_gains = params
    graphs = lens.shape[0]
    ident = identifiers(table, endpoints)
    embedded = features + low_back(matmul(low(ident), low(ident_weight)))
    normed_one = low(layer_norm(embedded, norm_gains[0]))
    projected = low(low_back(jnp.einsum('td,dcf->tcf', normed_one, low(qkv_weight), precision=HIGHEST)))
    parts = projected.reshape(graphs, LEN, 3, HEADS, HEAD_DIM)
    query, keys, values = (parts[:, :, 0], parts[:, :, 1], parts[:, :, 2])
    scores = low_back(jnp.einsum('gqhe,gkhe->ghqk', query, keys, precision=HIGHEST) * HEAD_DIM ** (-0.5))
    live = jnp.arange(LEN, dtype=jnp.int32)[None, :] < lens[:, None]
    scores = jnp.where(live[:, None, None, :], scores, MASKED)
    top = lax.optimization_barrier(jnp.max(scores, axis=-1, keepdims=True))
    expo = jnp.exp(scores - top)
    probs = expo / lax.optimization_barrier(jnp.sum(expo, axis=-1, keepdims=True))
    heads_out = low(low_back(jnp.einsum('ghqk,gkhe->gqhe', low(probs), values, precision=HIGHEST)))
    heads_out = heads_out.reshape(graphs * LEN, D)
    middle = embedded + low_back(matmul(heads_out, low(out_weight)))
    normed_two = low(layer_norm(middle, norm_gains[1]))
    up_pre = low_back(matmul(normed_two, low(ffn_weight[0])))
    hidden = low(jax.nn.gelu(up_pre, approximate=False))
    output_rows = middle + low_back(matmul(hidden, low(ffn_weight[1]).T))
    weights_live = live.astype(jnp.float32)
    pooled = lax.optimization_barrier(jnp.sum(output_rows.reshape(graphs, LEN, D) * weights_live[:, :, None], axis=1)) / lens[:, None].astype(jnp.float32)
    return layer_norm(pooled, norm_gains[2])

def adam_step(weight, gradient, first, second, factor, rate):
    clipped = gradient * factor
    first_new = BETA_ONE * first + (1.0 - BETA_ONE) * clipped
    second_new = BETA_TWO * second + (1.0 - BETA_TWO) * clipped * clipped
    first_hat = first_new / (1.0 - BETA_ONE ** STEPS)
    second_hat = second_new / (1.0 - BETA_TWO ** STEPS)
    weight_new = weight - rate * (first_hat / (jnp.sqrt(second_hat) + ADAM_EPS) + DECAY * weight)
    return (weight_new, first_new, second_new)

def reference(features, laplacian, endpoints, lengths, pairing, ident_weight, qkv_weight, out_weight, ffn_weight, norm_gains, ident_first, qkv_first, out_first, ffn_first, gains_first, ident_second, qkv_second, out_second, ffn_second, gains_second):
    params = (ident_weight, qkv_weight, out_weight, ffn_weight, norm_gains)
    group_feats = features.astype(jnp.float32).reshape(N_DP, TOKG, D)
    group_tables = laplacian.reshape(N_DP, 2 * GRAPHS_DEV * NODE, LAP)
    group_ends = endpoints.reshape(N_DP, TOKG, 2)
    group_lens = lengths.reshape(N_DP, 2 * GRAPHS_DEV)
    partner = (jnp.arange(N_DP, dtype=jnp.int32)[:, None] * GRAPHS_DEV + pairing).reshape(-1)

    def loss_of(weights):

        def one_group(inputs):
            return summarize(weights, inputs[0], inputs[1], inputs[2], inputs[3])
        summaries = lax.map(jax.checkpoint(one_group), (group_feats, group_tables, group_ends, group_lens))
        by_view = summaries.reshape(N_DP, 2, GRAPHS_DEV, D)
        left_side = by_view[:, 0].reshape(-1, D)
        right_side = by_view[:, 1].reshape(-1, D)
        logits = matmul(left_side, right_side.T) / D ** 0.5
        positive = jnp.take_along_axis(logits, partner[:, None], axis=1)
        return jnp.sum(log_total(logits, 1)) + jnp.sum(log_total(logits, 0)) - 2.0 * jnp.sum(positive)
    total_loss, back = jax.vjp(loss_of, params)
    grads = back(jnp.ones_like(total_loss))[0]
    squares = sum((jnp.sum(gradient * gradient) for gradient in grads))
    grad_norm = jnp.sqrt(squares)
    factor = CLIP_AT / jnp.maximum(grad_norm, CLIP_AT)
    ident_res = adam_step(ident_weight, grads[0], ident_first, ident_second, factor, STEP_RATES[0])
    qkv_res = adam_step(qkv_weight, grads[1], qkv_first, qkv_second, factor, STEP_RATES[1])
    out_res = adam_step(out_weight, grads[2], out_first, out_second, factor, STEP_RATES[2])
    ffn_res = adam_step(ffn_weight, grads[3], ffn_first, ffn_second, factor, STEP_RATES[3])
    gains_res = adam_step(norm_gains, grads[4], gains_first, gains_second, factor, STEP_RATES[4])
    return (grad_norm, total_loss, ident_res[0], qkv_res[0], out_res[0], ffn_res[0], gains_res[0], ident_res[1], qkv_res[1], out_res[1], ffn_res[1], gains_res[1], ident_res[2], qkv_res[2], out_res[2], ffn_res[2], gains_res[2])
```

```python
import functools

import jax
import jax.numpy as jnp
from jax import lax
from jax.experimental import pallas as pl
from jax.experimental.pallas import tpu as pltpu
from jax.sharding import PartitionSpec as P

D = 768
HEAD_DIM = 24
LAP = 16
LEN = 128
NODE = 32
STEPS = 3
GRAPHS_DEV = 16

HIGHEST = lax.Precision.HIGHEST
NORM_EPS = 1e-05
CLIP_AT = 5.0
STEP_RATES = (0.08, 0.02, 0.15, 0.02, 0.5)
BETA_ONE = 0.5
BETA_TWO = 0.5
DECAY = 0.01
ADAM_EPS = 1e-08
MASKED = -1e30

BF = jnp.bfloat16
F32 = jnp.float32
SUB = 4
SW = SUB * HEAD_DIM
PACK = 4 * SW
V_AT = 128 - SW
SCALE = HEAD_DIM ** (-0.5)
VMEM_LIMIT = 56 * 2**20


def nn(a, b):
    return lax.dot_general(a, b, (((1,), (0,)), ((), ())), preferred_element_type=F32)


def nt(a, b):
    return lax.dot_general(a, b, (((1,), (1,)), ((), ())), preferred_element_type=F32)


def tn(a, b):
    return lax.dot_general(a, b, (((0,), (0,)), ((), ())), preferred_element_type=F32)


def lanes():
    return lax.broadcasted_iota(jnp.int32, (1, 128), 1)


def head_lanes(h, at):
    lane = lanes()
    return (lane >= at + h * HEAD_DIM) & (lane < at + (h + 1) * HEAD_DIM)


def by_head(v, at):
    zero = jnp.zeros_like(v)
    return jnp.concatenate([jnp.where(head_lanes(h, at), v, zero) for h in range(SUB)], axis=0)


def stack_heads(v):
    return jnp.concatenate([v[:, h * LEN : (h + 1) * LEN] for h in range(SUB)], axis=0)


def attend_kernel(lens_ref, x_ref, w_ref, qkv_ref, p_ref, o_ref, rinv_ref, *, graphs):
    y = nn(x_ref[...], w_ref[0])
    qkv_ref[0, 0] = y[:, :128].astype(BF)
    qkv_ref[0, 1] = pltpu.roll(y, PACK - SW, 1)[:, :128].astype(BF)
    qkv_ref[0, 2] = pltpu.roll(y, SW, 1)[:, 256:].astype(BF)
    col = lanes()
    ones = by_head(jnp.ones((LEN, 128), BF), V_AT)
    for g in range(graphs):
        rows = slice(g * LEN, (g + 1) * LEN)
        query, keys, values = qkv_ref[0, 0, rows, :], qkv_ref[0, 1, rows, :], qkv_ref[0, 2, rows, :]
        live = col < lens_ref[g]
        scores = nt(query, by_head(keys, 0))
        parts = []
        for h in range(SUB):
            own = jnp.where(live, scores[:, h * LEN : (h + 1) * LEN] * SCALE, MASKED)
            parts.append(jnp.exp(own - jnp.max(own, axis=1, keepdims=True)).astype(BF))
        expo = jnp.concatenate(parts, axis=1)
        both = nn(expo, jnp.concatenate([by_head(values, V_AT), ones], axis=1))
        rinv = jnp.where(col >= V_AT, 1.0 / both[:, 128:], 0.0)
        p_ref[0, rows, :] = expo
        rinv_ref[0, rows, :] = rinv
        o_ref[0, rows, :] = jnp.where(col >= V_AT, both[:, :128] * rinv, 0.0).astype(BF)


def attend(lens, x, w):
    tokens, groups = x.shape[0], w.shape[0]
    block = lambda *tail: pl.BlockSpec((1,) + tail, lambda i: (i,) + (0,) * len(tail))
    return pl.pallas_call(
        functools.partial(attend_kernel, graphs=tokens // LEN),
        grid=(groups,),
        in_specs=[
            pl.BlockSpec(memory_space=pltpu.SMEM),
            pl.BlockSpec((tokens, D), lambda i: (0, 0)),
            block(D, PACK),
        ],
        out_specs=[block(3, tokens, 128), block(tokens, 512), block(tokens, 128), block(tokens, 128)],
        out_shape=[
            jax.ShapeDtypeStruct((groups, 3, tokens, 128), BF),
            jax.ShapeDtypeStruct((groups, tokens, 512), BF),
            jax.ShapeDtypeStruct((groups, tokens, 128), BF),
            jax.ShapeDtypeStruct((groups, tokens, 128), F32),
        ],
        compiler_params=pltpu.CompilerParams(vmem_limit_bytes=VMEM_LIMIT),
        cost_estimate=pl.CostEstimate(
            flops=groups * 2_500_000_000, bytes_accessed=groups * 3_000_000, transcendentals=0
        ),
        name="attend",
    )(lens, x, w)


def attend_back_kernel(
    x_ref, da_ref, w_ref, qkv_ref, p_ref, o_ref, rinv_ref, g_ref, dn_ref, xt, dt, dqkv, aug, *, graphs
):
    step = pl.program_id(0)

    @pl.when(step == 0)
    def _():
        xt[...] = x_ref[...].T
        dt[...] = da_ref[...].T

    w = w_ref[0]
    lane = lanes()
    d_out = jnp.where(lane >= V_AT, nn(da_ref[...], w[:, 256:]) * rinv_ref[0], 0.0)
    heads_out = o_ref[0]
    terms = d_out * heads_out.astype(F32)
    high = terms.astype(BF)
    low = (terms - high.astype(F32)).astype(BF)
    row = lax.broadcasted_iota(jnp.int32, (128, 128), 0)
    column = lax.broadcasted_iota(jnp.int32, (128, 128), 1)
    pick = jnp.zeros((128, 128), BF)
    for h in range(SUB):
        inside = (row >= V_AT + h * HEAD_DIM) & (row < V_AT + (h + 1) * HEAD_DIM)
        pick = jnp.where(inside & ((column == h) | (column == SUB + h)), jnp.ones_like(pick), pick)
    delta = nn(high, pick) + nn(low, pick)
    rounded = delta.astype(BF).astype(F32)
    aug[...] = jnp.where(
        lane >= V_AT, d_out, jnp.where(lane < SUB, -rounded, rounded - delta)
    ).astype(BF)
    for g in range(graphs):
        rows = slice(g * LEN, (g + 1) * LEN)
        query, keys, values = qkv_ref[0, 0, rows, :], qkv_ref[0, 1, rows, :], qkv_ref[0, 2, rows, :]
        d_rows, expo = aug[rows, :], p_ref[0, rows, :]
        one, zero = jnp.ones_like(values), jnp.zeros_like(values)
        spread = jnp.concatenate(
            [
                jnp.where(
                    head_lanes(h, V_AT), values, jnp.where((lane == h) | (lane == SUB + h), one, zero)
                )
                for h in range(SUB)
            ],
            axis=0,
        )
        d_scores = (expo.astype(F32) * nt(d_rows, spread)).astype(BF)
        d_query = nn(d_scores, by_head(keys, 0)) * SCALE
        d_keys = tn(stack_heads(d_scores), by_head(query, 0)) * SCALE
        d_values = tn(stack_heads(expo), by_head(d_rows, V_AT))
        rolled_keys, rolled_values = pltpu.roll(d_keys, SW, 1), pltpu.roll(d_values, V_AT, 1)
        dqkv[rows, 0:128] = jnp.where(lane < SW, d_query, rolled_keys).astype(BF)
        dqkv[rows, 128:256] = jnp.where(lane < 64, rolled_keys, rolled_values).astype(BF)
        dqkv[rows, 256:384] = jnp.where(lane < V_AT, rolled_values, 0.0).astype(BF)
    d_packed = dqkv[...]
    grad = nn(xt[...], d_packed)
    grad_out = nn(dt[...], heads_out)
    g_ref[0, :, 0:256] = grad[:, 0:256].astype(BF)
    g_ref[0, :, 256:384] = (grad[:, 256:384] + grad_out).astype(BF)
    d_normed = nt(d_packed, w)

    @pl.when(step == 0)
    def _():
        dn_ref[...] = d_normed

    @pl.when(step > 0)
    def _():
        dn_ref[...] += d_normed


def attend_back(x, d_attn, w, saved):
    qkv, expo, heads_out, rinv = saved
    tokens, groups = x.shape[0], w.shape[0]
    block = lambda *tail: pl.BlockSpec((1,) + tail, lambda i: (i,) + (0,) * len(tail))
    whole = pl.BlockSpec((tokens, D), lambda i: (0, 0))
    return pl.pallas_call(
        functools.partial(attend_back_kernel, graphs=tokens // LEN),
        grid=(groups,),
        in_specs=[
            whole,
            whole,
            block(D, PACK),
            block(3, tokens, 128),
            block(tokens, 512),
            block(tokens, 128),
            block(tokens, 128),
        ],
        out_specs=[block(D, PACK), whole],
        out_shape=[
            jax.ShapeDtypeStruct((groups, D, PACK), BF),
            jax.ShapeDtypeStruct((tokens, D), F32),
        ],
        scratch_shapes=[
            pltpu.VMEM((D, tokens), BF),
            pltpu.VMEM((D, tokens), BF),
            pltpu.VMEM((tokens, PACK), BF),
            pltpu.VMEM((tokens, 128), BF),
        ],
        compiler_params=pltpu.CompilerParams(vmem_limit_bytes=VMEM_LIMIT),
        cost_estimate=pl.CostEstimate(
            flops=groups * 7_000_000_000, bytes_accessed=groups * 3_000_000, transcendentals=0
        ),
        name="attend_back",
    )(x, d_attn, w, qkv, expo, heads_out, rinv)


def erf(x):
    x = jnp.clip(x, -3.832506856900711, 3.832506856900711)
    x2 = x * x
    top = 0.00022905065861350646
    for c in (
        0.0034082910107109506,
        0.050955695062380861,
        0.18520832239976145,
        1.128379143519084,
    ):
        top = top * x2 + c
    bottom = -1.1791602954361697e-7
    for c in (
        0.000023547966471313185,
        0.0010179625278914885,
        0.014070470171167667,
        0.11098505178285362,
        0.49746925110067538,
        1.0,
    ):
        bottom = bottom * x2 + c
    return x * top / bottom


def normalize(values):
    centred = values - jnp.mean(values, axis=-1, keepdims=True)
    spread = jnp.mean(centred * centred, axis=-1, keepdims=True)
    rstd = lax.rsqrt(spread + NORM_EPS)
    return centred * rstd, rstd


def two_parts(v):
    high = v.astype(BF)
    return high, (v - high.astype(F32)).astype(BF)


def forward_kernel(
    lens_ref, e_ref, gain_ref, up_ref, down_ref, *refs, tile_graphs, waves, groups
):
    o_refs, w_refs = refs[:waves], refs[waves : 2 * waves]
    mid_ref, slope_ref, hsum_ref, pay_ref, hsum, msum = refs[2 * waves :]
    step, steps = pl.program_id(0), pl.num_programs(0)
    middle = e_ref[...]
    for wave in range(waves):
        left = jnp.concatenate([o_refs[wave][j] for j in range(groups)], axis=1)
        right = jnp.concatenate([w_refs[wave][j][:, 256:] for j in range(groups)], axis=1)
        middle = middle + nt(left, right)
    mid_ref[...] = middle
    xhat, _ = normalize(middle)
    up = nn((xhat * gain_ref[1:2, :]).astype(BF), up_ref[...])
    cdf = 0.5 + 0.5 * erf(up * (0.5**0.5))
    hidden = (up * cdf).astype(BF).astype(F32)
    slope_ref[...] = (cdf + up * (0.3989422804014327 * jnp.exp(-0.5 * up * up))).astype(BF)
    place = lax.broadcasted_iota(jnp.int32, (LEN, 1), 0)
    for j in range(tile_graphs):
        g = step * tile_graphs + j
        live = place < lens_ref[g]
        rows = slice(j * LEN, (j + 1) * LEN)
        hsum[pl.ds(g, 1), :] = jnp.sum(jnp.where(live, hidden[rows], 0.0), axis=0, keepdims=True)
        msum[pl.ds(g, 1), :] = jnp.sum(jnp.where(live, middle[rows], 0.0), axis=0, keepdims=True)

    @pl.when(step == steps - 1)
    def _():
        graphs = hsum.shape[0]
        high, low = two_parts(hsum[...])
        which = lax.broadcasted_iota(jnp.int32, (graphs, 1), 0)
        length = jnp.ones((graphs, 1), F32)
        for g in range(graphs):
            length = jnp.where(which == g, lens_ref[g].astype(F32), length)
        pooled = (msum[...] + (nt(high, down_ref[...]) + nt(low, down_ref[...]))) / length
        xhat_pool, rstd = normalize(pooled)
        hsum_ref[...] = hsum[...].astype(BF)
        pay_ref[:, :D] = xhat_pool
        lane = lanes()
        pay_ref[:, D:] = jnp.where(lane == 0, rstd, jnp.where(lane == 1, 1.0 / length, 0.0))


def forward_rest(lens, embedded, gains, w_up, w_down, outs, weights):
    tokens = embedded.shape[0]
    graphs = tokens // LEN
    tile_graphs = min(2, graphs)
    rows = tile_graphs * LEN
    waves, groups = len(outs), outs[0].shape[0]
    full = lambda a: pl.BlockSpec(a.shape, lambda i: (0,) * a.ndim)
    tile = pl.BlockSpec((rows, D), lambda i: (i, 0))
    return pl.pallas_call(
        functools.partial(forward_kernel, tile_graphs=tile_graphs, waves=waves, groups=groups),
        grid=(tokens // rows,),
        in_specs=[pl.BlockSpec(memory_space=pltpu.SMEM), tile, full(gains), full(w_up), full(w_down)]
        + [pl.BlockSpec((groups, rows, 128), lambda i: (0, i, 0)) for _ in outs]
        + [full(w) for w in weights],
        out_specs=[
            tile,
            tile,
            pl.BlockSpec((graphs, D), lambda i: (0, 0)),
            pl.BlockSpec((graphs, D + 128), lambda i: (0, 0)),
        ],
        out_shape=[
            jax.ShapeDtypeStruct((tokens, D), F32),
            jax.ShapeDtypeStruct((tokens, D), BF),
            jax.ShapeDtypeStruct((graphs, D), BF),
            jax.ShapeDtypeStruct((graphs, D + 128), F32),
        ],
        scratch_shapes=[pltpu.VMEM((graphs, D), F32), pltpu.VMEM((graphs, D), F32)],
        compiler_params=pltpu.CompilerParams(vmem_limit_bytes=VMEM_LIMIT),
        cost_estimate=pl.CostEstimate(
            flops=10_000_000_000, bytes_accessed=20_000_000, transcendentals=0
        ),
        name="forward_rest",
    )(lens, embedded, gains, w_up, w_down, *outs, *weights)


def norm_back(d_normed, xhat, rstd, gain):
    d_hat = d_normed * gain
    return rstd * (
        d_hat
        - jnp.mean(d_hat, axis=-1, keepdims=True)
        - xhat * jnp.mean(d_hat * xhat, axis=-1, keepdims=True)
    )


def ffn_back_kernel(
    lens_ref, mid_ref, slope_ref, dout_ref, dhid_ref, gain_ref, up_ref,
    dmid_ref, dattn_ref, grad_ref, dgain_ref, grad, dgain, *, tile_graphs
):
    step, steps = pl.program_id(0), pl.num_programs(0)
    xhat, rstd = normalize(mid_ref[...])
    gain = gain_ref[1:2, :]
    place = lax.broadcasted_iota(jnp.int32, (LEN, 1), 0)
    d_up, d_out = [], []
    for j in range(tile_graphs):
        g = step * tile_graphs + j
        live = place < lens_ref[g]
        rows = slice(j * LEN, (j + 1) * LEN)
        d_hidden = jnp.where(live, dhid_ref[pl.ds(g, 1), :], 0.0)
        d_up.append((slope_ref[rows, :].astype(F32) * d_hidden).astype(BF))
        d_out.append(jnp.where(live, dout_ref[pl.ds(g, 1), :], 0.0))
    d_up, d_out = jnp.concatenate(d_up, axis=0), jnp.concatenate(d_out, axis=0)
    d_normed = nt(d_up, up_ref[...])
    d_mid = d_out + norm_back(d_normed, xhat, rstd, gain)
    dmid_ref[...] = d_mid
    dattn_ref[...] = d_mid.astype(BF)
    part = tn((xhat * gain).astype(BF), d_up)
    part_gain = jnp.sum((d_normed * xhat).reshape(-1, 8, D), axis=0)

    @pl.when(step == 0)
    def _():
        grad[...] = part
        dgain[...] = part_gain

    @pl.when(step > 0)
    def _():
        grad[...] += part
        dgain[...] += part_gain

    @pl.when(step == steps - 1)
    def _():
        grad_ref[...] = grad[...].astype(BF)
        dgain_ref[...] = dgain[...]


def ffn_back(lens, middle, slope, d_out, d_hidden, gains, w_up):
    tokens = middle.shape[0]
    tile_graphs = min(2, tokens // LEN)
    rows = tile_graphs * LEN
    full = lambda a: pl.BlockSpec(a.shape, lambda i: (0,) * a.ndim)
    tile = pl.BlockSpec((rows, D), lambda i: (i, 0))
    return pl.pallas_call(
        functools.partial(ffn_back_kernel, tile_graphs=tile_graphs),
        grid=(tokens // rows,),
        in_specs=[pl.BlockSpec(memory_space=pltpu.SMEM), tile, tile]
        + [full(a) for a in (d_out, d_hidden, gains, w_up)],
        out_specs=[
            tile,
            tile,
            pl.BlockSpec((D, D), lambda i: (0, 0)),
            pl.BlockSpec((8, D), lambda i: (0, 0)),
        ],
        out_shape=[
            jax.ShapeDtypeStruct((tokens, D), F32),
            jax.ShapeDtypeStruct((tokens, D), BF),
            jax.ShapeDtypeStruct((D, D), BF),
            jax.ShapeDtypeStruct((8, D), F32),
        ],
        scratch_shapes=[pltpu.VMEM((D, D), F32), pltpu.VMEM((8, D), F32)],
        compiler_params=pltpu.CompilerParams(vmem_limit_bytes=VMEM_LIMIT),
        cost_estimate=pl.CostEstimate(
            flops=10_000_000_000, bytes_accessed=15_000_000, transcendentals=0
        ),
        name="ffn_back",
    )(lens, middle, slope, d_out, d_hidden, gains, w_up)


class Place:
    def __init__(self):
        self.n, self.heads = lax.axis_size("dp"), lax.axis_size("head")
        self.inner = 1 << ((self.n.bit_length() - 1) // 2)
        self.outer = self.n // self.inner
        self.dp, self.head = lax.axis_index("dp"), lax.axis_index("head")
        self.bits = [1 << b for b in range(self.heads.bit_length() - 1)]

    def swap(self, v, bit):
        return lax.ppermute(v, "head", [(i, i ^ bit) for i in range(self.heads)])

    def digit(self, which):
        size, stride = (self.outer, self.inner) if which == "outer" else (self.inner, 1)
        return size, stride, (self.dp // stride) % size

    def shift(self, v, which, by):
        size, stride, _ = self.digit(which)
        pairs = []
        for i in range(self.n):
            own = (i // stride) % size
            pairs.append((i, i + ((own + by) % size - own) * stride))
        return lax.ppermute(v, "dp", pairs)

    def gather_digit(self, v, which, axis=0):
        size, _, own = self.digit(which)
        out = jnp.zeros(v.shape[:axis] + (size,) + v.shape[axis:], v.dtype)
        out = lax.dynamic_update_index_in_dim(out, v, own, axis)
        for by in range(1, size):
            out = lax.dynamic_update_index_in_dim(
                out, self.shift(v, which, by), (own - by) % size, axis
            )
        return out

    def gather_bit(self, v, bit, axis=0):
        own = (self.head // bit) % 2
        other = self.swap(v, bit)
        first, second = jnp.where(own == 0, v, other), jnp.where(own == 0, other, v)
        return jnp.stack([first, second], axis=axis)

    def gather_all(self, v):
        v = self.gather_digit(v, "outer")
        v = self.gather_digit(v, "inner", 1)
        for bit in self.bits[::-1]:
            v = self.gather_bit(v, bit, 2 + self.bits[::-1].index(bit))
        return v.reshape((self.n, self.heads) + v.shape[2 + len(self.bits) :])

    def reduce_digit(self, v, which, axis=0):
        size, _, own = self.digit(which)
        pick = lambda by: lax.dynamic_index_in_dim(v, (own + by) % size, axis, keepdims=False)
        total = pick(0).astype(F32)
        for by in range(1, size):
            total = total + self.shift(pick(by), which, by).astype(F32)
        return total

    def reduce_bit(self, v, bit, axis):
        own = (self.head // bit) % 2
        pick = lambda at: lax.dynamic_index_in_dim(v, at, axis, keepdims=False)
        return pick(own).astype(F32) + self.swap(pick(1 - own), bit).astype(F32)

    def reduce_all(self, v, dtype):
        rows = v.shape[0] // (self.n * self.heads)
        v = v.reshape((self.outer, self.inner) + (2,) * len(self.bits) + (rows,) + v.shape[1:])
        for bit in self.bits:
            v = self.reduce_bit(v.astype(dtype), bit, 1 + len(self.bits) - self.bits.index(bit))
        v = self.reduce_digit(v.astype(dtype), "inner", 1)
        return self.reduce_digit(v.astype(dtype), "outer", 0)

    def total(self, v):
        for bit in self.bits:
            v = v + self.swap(v, bit)
        for which in ("inner", "outer"):
            size, stride, own = self.digit(which)
            by = 1
            while by < size:
                pairs = []
                for i in range(self.n):
                    at = (i // stride) % size
                    pairs.append((i, i + ((at ^ by) - at) * stride))
                v = v + lax.ppermute(v, "dp", pairs)
                by *= 2
        return v


def gather_attention(place, shards):
    low, high = place.bits[:-1], place.bits[-1:]
    result = []
    for s, shard in enumerate(shards):
        part = place.gather_digit(shard, "outer")
        found = {0: part}

        def exchange(bits, found):
            for bit in bits:
                found = {**found, **{r ^ bit: place.swap(v, bit) for r, v in found.items()}}
            return found

        if s % 2:
            found = exchange(high, found)
        found = {r: place.gather_digit(v, "inner", 1) for r, v in found.items()}
        if s % 2 == 0:
            found = exchange(high, found)
        found = exchange(low[::-1], found)
        result.append({r: v.reshape(-1, v.shape[-1]) for r, v in found.items()})
    return result


def reduce_attention(place, s, grads):
    found = {
        r: v.reshape(place.outer, place.inner, -1, v.shape[-1]) for r, v in grads.items()
    }

    def fold(bits, found):
        for bit in bits:
            found = {
                r: v.astype(F32) + place.swap(found[r ^ bit].astype(BF), bit).astype(F32)
                for r, v in found.items()
                if not r & bit
            }
        return found

    low, high = place.bits[:-1], place.bits[-1:]
    found = fold(low, found)
    if s % 2 == 0:
        found = fold(high, found)
    found = {r: place.reduce_digit(v.astype(BF), "inner", 1) for r, v in found.items()}
    if s % 2:
        found = fold(high, found)
    return place.reduce_digit(found[0].astype(BF), "outer", 0)


def log_total(values, axis):
    top = jnp.max(values, axis=axis, keepdims=True)
    return jnp.squeeze(top, axis) + jnp.log(jnp.sum(jnp.exp(values - top), axis=axis))


def identifiers(table, endpoints):
    graphs = endpoints.shape[0] // LEN
    nodes = table.reshape(graphs, NODE, LAP).astype(BF)
    picks = (
        endpoints.reshape(graphs, LEN, 2)[..., None] == jnp.arange(NODE, dtype=jnp.int32)
    ).astype(BF)
    found = jnp.einsum("glan,gnc->glac", picks, nodes, preferred_element_type=F32)
    return found.reshape(graphs * LEN, 2 * LAP).astype(BF)


def adam_step(weight, gradient, first, second, factor, rate):
    clipped = gradient * factor
    first_new = BETA_ONE * first + (1.0 - BETA_ONE) * clipped
    second_new = BETA_TWO * second + (1.0 - BETA_TWO) * clipped * clipped
    first_hat = first_new / (1.0 - BETA_ONE**STEPS)
    second_hat = second_new / (1.0 - BETA_TWO**STEPS)
    weight_new = weight - rate * (first_hat / (jnp.sqrt(second_hat) + ADAM_EPS) + DECAY * weight)
    return (weight_new, first_new, second_new)


def per_device(
    features,
    laplacian,
    endpoints,
    lengths,
    pairing,
    ident_weight,
    qkv_weight,
    out_weight,
    ffn_weight,
    norm_gains,
    ident_first,
    qkv_first,
    out_first,
    ffn_first,
    gains_first,
    ident_second,
    qkv_second,
    out_second,
    ffn_second,
    gains_second,
):
    place = Place()
    heads, head, dp = place.heads, place.head, place.dp
    tokens = features.shape[0] // heads
    graphs = tokens // LEN
    width = qkv_weight.shape[2]
    subs = width // SW
    own_columns = norm_gains.shape[1]

    small = jnp.concatenate([ident_weight, norm_gains], axis=0)
    small_rows = small.shape[0]
    small = place.gather_all(small.reshape(1, -1)).reshape(-1, small_rows, own_columns)
    small = small.transpose(1, 0, 2).reshape(small_rows, D)
    ident_full, gains = small[: 2 * LAP].astype(BF), small[2 * LAP :]

    packed = [qkv_weight[:, 0], qkv_weight[:, 1], qkv_weight[:, 2], out_weight.T]
    shards = [
        jnp.concatenate([m[:, s * SW : (s + 1) * SW] for m in packed], axis=1).astype(BF)
        for s in range(subs)
    ]
    packs = gather_attention(place, shards)
    ffn = ffn_weight.astype(BF)
    for bit in place.bits[1:][::-1]:
        ffn = place.gather_bit(ffn, bit, 0)
    ffn = place.gather_digit(ffn, "inner", 0)
    ffn = place.gather_digit(ffn, "outer", 0)
    ffn = place.gather_bit(ffn, place.bits[0], 1 + len(place.bits))
    lead = ffn.ndim - 3
    w_up = lax.index_in_dim(ffn, 0, lead, keepdims=False).reshape(D, -1)
    w_down = lax.index_in_dim(ffn, 1, lead, keepdims=False).reshape(D, -1)

    start_row = head * tokens
    lens = lax.dynamic_slice_in_dim(lengths.reshape(-1), head * graphs, graphs, 0)
    table_rows = lax.dynamic_slice_in_dim(laplacian, head * graphs * NODE, graphs * NODE, 0)
    end_rows = lax.dynamic_slice_in_dim(endpoints, start_row, tokens, 0)
    ident_rows = identifiers(table_rows, end_rows)
    embedded = lax.dynamic_slice_in_dim(features, start_row, tokens, 0).astype(F32)
    embedded = embedded + nn(ident_rows, ident_full)
    xhat_one, rstd_one = normalize(embedded)
    normed_one = (xhat_one * gains[0]).astype(BF)

    waves = [[(s, r), (s, r + 1)] for s in range(subs) for r in range(0, heads, 2)]
    stacks = [jnp.stack([packs[s][r] for s, r in wave]) for wave in waves]
    saved = [attend(lens, normed_one, w) for w in stacks]

    middle, slope, hsum, payload = forward_rest(
        lens, embedded, gains, w_up, w_down, [v[2] for v in saved], stacks
    )

    partner_slot = lax.dynamic_slice_in_dim(
        jnp.concatenate([pairing.reshape(-1)] * 2), head * graphs, graphs, 0
    ).astype(F32)
    payload = lax.dynamic_update_slice(payload, partner_slot[:, None], (0, D + 2))
    everyone = place.gather_all(payload).reshape(place.n, 2, GRAPHS_DEV, -1)
    hidden_sums = place.gather_all(hsum).reshape(-1, hsum.shape[-1])
    xhat = everyone[..., :D]
    summaries = xhat * gains[2]
    left, right = summaries[:, 0].reshape(-1, D), summaries[:, 1].reshape(-1, D)
    root_width = D**0.5
    logits = jnp.dot(left, right.T, precision=HIGHEST) / root_width
    row_totals, col_totals = log_total(logits, 1), log_total(logits, 0)
    count = logits.shape[0]
    group = jnp.arange(count, dtype=jnp.int32) // GRAPHS_DEV
    partner = group * GRAPHS_DEV + everyone[:, 0, :, D + 2].reshape(-1).astype(jnp.int32)
    positive = (partner[:, None] == jnp.arange(count, dtype=jnp.int32)[None, :]).astype(F32)
    total_loss = (
        jnp.sum(row_totals) + jnp.sum(col_totals) - 2.0 * jnp.sum(positive * logits)
    )
    d_logits = (
        jnp.exp(logits - row_totals[:, None])
        + jnp.exp(logits - col_totals[None, :])
        - 2.0 * positive
    )
    d_left = jnp.dot(d_logits, right, precision=HIGHEST) / root_width
    d_right = jnp.dot(d_logits.T, left, precision=HIGHEST) / root_width
    d_summary = jnp.stack(
        [d_left.reshape(place.n, GRAPHS_DEV, D), d_right.reshape(place.n, GRAPHS_DEV, D)], axis=1
    ).reshape(-1, D)
    xhat = xhat.reshape(-1, D)
    stats = everyone.reshape(-1, everyone.shape[-1])
    gain_three = jnp.sum(d_summary * xhat, axis=0)
    d_rows = norm_back(d_summary, xhat, stats[:, D : D + 1], gains[2]) * stats[:, D + 1 : D + 2]
    d_rows_low = d_rows.astype(BF)
    own_row = (dp * heads + head) * graphs
    d_out = lax.dynamic_slice_in_dim(d_rows, own_row, graphs, 0)
    d_hidden = nn(d_out.astype(BF), w_down)

    own_column = (dp * heads + head) * own_columns
    d_columns = lax.dynamic_slice_in_dim(d_rows_low, own_column, own_columns, 1)
    grad_down = tn(d_columns, hidden_sums)
    d_middle, d_attn, grad_up, gain_two = ffn_back(
        lens, middle, slope, d_out, d_hidden, gains, w_up
    )
    grad_up = place.reduce_all(grad_up, BF)
    order = sorted(range(len(waves)), key=lambda i: -waves[i][0][1])
    d_normed = 0.0
    by_sub = [dict() for _ in range(subs)]
    half = len(order) // 2
    for chosen in (order[:half], order[half:]):
        cat = lambda k: jnp.concatenate([saved[i][k] for i in chosen], axis=0)
        grads, d_part = attend_back(
            normed_one,
            d_attn,
            jnp.concatenate([stacks[i] for i in chosen], axis=0),
            [cat(k) for k in range(4)],
        )
        d_normed = d_normed + d_part
        for at, (s, r) in enumerate([pair for i in chosen for pair in waves[i]]):
            by_sub[s][r] = grads[at]
    grad_packs = [reduce_attention(place, s, by_sub[s]) for s in range(subs)]
    d_embedded = d_middle + norm_back(d_normed, xhat_one, rstd_one, gains[0])
    gain_one = jnp.sum(d_normed * xhat_one, axis=0)
    grad_ident = tn(ident_rows, d_embedded.astype(BF))
    rows = jnp.concatenate([grad_ident, gain_one[None], jnp.sum(gain_two, axis=0)[None]], axis=0)
    row_count = rows.shape[0]
    rows = rows.T.reshape(-1, own_columns * row_count)
    rows = place.reduce_all(rows, F32).reshape(own_columns, row_count).T
    grad_ident = rows[: 2 * LAP]
    grad_gains = jnp.concatenate(
        [rows[2 * LAP :], lax.dynamic_slice_in_dim(gain_three, own_column, own_columns, 0)[None]],
        axis=0,
    )
    columns = lambda j: jnp.concatenate([v[:, j * SW : (j + 1) * SW] for v in grad_packs], axis=1)
    grad_qkv = jnp.stack([columns(0), columns(1), columns(2)], axis=1)
    grad_out = columns(3).T
    grad_ffn = jnp.stack([grad_up.reshape(own_columns, -1), grad_down])

    grads = (grad_ident, grad_qkv, grad_out, grad_ffn, grad_gains)
    squares = sum((jnp.sum(gradient * gradient) for gradient in grads))
    grad_norm = jnp.sqrt(place.total(squares))
    factor = CLIP_AT / jnp.maximum(grad_norm, CLIP_AT)
    results = [
        adam_step(weight, gradient, first, second, factor, rate)
        for weight, gradient, first, second, rate in zip(
            (ident_weight, qkv_weight, out_weight, ffn_weight, norm_gains),
            grads,
            (ident_first, qkv_first, out_first, ffn_first, gains_first),
            (ident_second, qkv_second, out_second, ffn_second, gains_second),
            STEP_RATES,
        )
    ]
    return (grad_norm, total_loss) + tuple(r[k] for k in range(3) for r in results)


def solution(mesh):
    both = P(None, ("dp", "head"))
    weights = (both, P("dp", None, "head"), P("head", "dp"), P(None, ("dp", "head"), None), both)
    in_specs = (P("dp", None),) * 5 + weights * 3
    out_specs = (P(), P()) + weights * 3
    return jax.shard_map(
        per_device, mesh=mesh, in_specs=in_specs, out_specs=out_specs, check_vma=False
    )
```

```python
import functools

import jax
import jax.numpy as jnp
from jax import lax
from jax.experimental import pallas as pl
from jax.experimental.pallas import tpu as pltpu
from jax.sharding import PartitionSpec as P

D = 768
HEAD_DIM = 24
LAP = 16
LEN = 128
NODE = 32
STEPS = 3
GRAPHS_DEV = 16

HIGHEST = lax.Precision.HIGHEST
NORM_EPS = 1e-05
CLIP_AT = 5.0
STEP_RATES = (0.08, 0.02, 0.15, 0.02, 0.5)
BETA_ONE = 0.5
BETA_TWO = 0.5
DECAY = 0.01
ADAM_EPS = 1e-08
MASKED = -1e30

BF = jnp.bfloat16
F32 = jnp.float32
SUB = 4
SW = SUB * HEAD_DIM
PACK = 4 * SW
V_AT = 128 - SW
SCALE = HEAD_DIM ** (-0.5)
VMEM_LIMIT = 44 * 2**20


def nn(a, b):
    return lax.dot_general(a, b, (((1,), (0,)), ((), ())), preferred_element_type=F32)


def nt(a, b):
    return lax.dot_general(a, b, (((1,), (1,)), ((), ())), preferred_element_type=F32)


def tn(a, b):
    return lax.dot_general(a, b, (((0,), (0,)), ((), ())), preferred_element_type=F32)


def lanes():
    return lax.broadcasted_iota(jnp.int32, (1, 128), 1)


def head_lanes(h, at):
    lane = lanes()
    return (lane >= at + h * HEAD_DIM) & (lane < at + (h + 1) * HEAD_DIM)


def by_head(v, at):
    zero = jnp.zeros_like(v)
    return jnp.concatenate([jnp.where(head_lanes(h, at), v, zero) for h in range(SUB)], axis=0)


def stack_heads(v):
    return jnp.concatenate([v[:, h * LEN : (h + 1) * LEN] for h in range(SUB)], axis=0)


def attend_kernel(lens_ref, x_ref, w_ref, qkv_ref, p_ref, o_ref, rinv_ref, *, graphs):
    y = nn(x_ref[...], w_ref[0])
    qkv_ref[0, 0] = y[:, :128].astype(BF)
    qkv_ref[0, 1] = pltpu.roll(y, PACK - SW, 1)[:, :128].astype(BF)
    qkv_ref[0, 2] = pltpu.roll(y, SW, 1)[:, 256:].astype(BF)
    col = lanes()
    ones = by_head(jnp.ones((LEN, 128), BF), V_AT)
    for g in range(graphs):
        rows = slice(g * LEN, (g + 1) * LEN)
        query, keys, values = qkv_ref[0, 0, rows, :], qkv_ref[0, 1, rows, :], qkv_ref[0, 2, rows, :]
        live = col < lens_ref[g]
        scores = nt(query, by_head(keys, 0))
        parts = []
        for h in range(SUB):
            own = jnp.where(live, scores[:, h * LEN : (h + 1) * LEN] * SCALE, MASKED)
            parts.append(jnp.exp(own - jnp.max(own, axis=1, keepdims=True)).astype(BF))
        expo = jnp.concatenate(parts, axis=1)
        both = nn(expo, jnp.concatenate([by_head(values, V_AT), ones], axis=1))
        rinv = jnp.where(col >= V_AT, 1.0 / both[:, 128:], 0.0)
        p_ref[0, rows, :] = expo
        rinv_ref[0, rows, :] = rinv
        o_ref[0, rows, :] = jnp.where(col >= V_AT, both[:, :128] * rinv, 0.0).astype(BF)


def attend(lens, x, w):
    tokens, groups = x.shape[0], w.shape[0]
    block = lambda *tail: pl.BlockSpec((1,) + tail, lambda i: (i,) + (0,) * len(tail))
    return pl.pallas_call(
        functools.partial(attend_kernel, graphs=tokens // LEN),
        grid=(groups,),
        in_specs=[
            pl.BlockSpec(memory_space=pltpu.SMEM),
            pl.BlockSpec((tokens, D), lambda i: (0, 0)),
            block(D, PACK),
        ],
        out_specs=[block(3, tokens, 128), block(tokens, 512), block(tokens, 128), block(tokens, 128)],
        out_shape=[
            jax.ShapeDtypeStruct((groups, 3, tokens, 128), BF),
            jax.ShapeDtypeStruct((groups, tokens, 512), BF),
            jax.ShapeDtypeStruct((groups, tokens, 128), BF),
            jax.ShapeDtypeStruct((groups, tokens, 128), F32),
        ],
        compiler_params=pltpu.CompilerParams(vmem_limit_bytes=VMEM_LIMIT),
        cost_estimate=pl.CostEstimate(
            flops=groups * 2_500_000_000, bytes_accessed=groups * 3_000_000, transcendentals=0
        ),
        name="attend",
    )(lens, x, w)


def attend_back_kernel(
    xt_ref, dt_ref, da_ref, w_ref, qkv_ref, p_ref, o_ref, rinv_ref, g_ref, d_ref, aug, *, graphs
):
    w = w_ref[0]
    lane = lanes()
    d_out = jnp.where(lane >= V_AT, nn(da_ref[...], w[:, 256:]) * rinv_ref[0], 0.0)
    heads_out = o_ref[0]
    terms = d_out * heads_out.astype(F32)
    high, low = two_parts(terms)
    row = lax.broadcasted_iota(jnp.int32, (128, 128), 0)
    column = lax.broadcasted_iota(jnp.int32, (128, 128), 1)
    pick = jnp.zeros((128, 128), BF)
    for h in range(SUB):
        inside = (row >= V_AT + h * HEAD_DIM) & (row < V_AT + (h + 1) * HEAD_DIM)
        pick = jnp.where(inside & ((column == h) | (column == SUB + h)), jnp.ones_like(pick), pick)
    delta = nn(high, pick) + nn(low, pick)
    rounded = delta.astype(BF).astype(F32)
    aug[...] = jnp.where(
        lane >= V_AT, d_out, jnp.where(lane < SUB, -rounded, rounded - delta)
    ).astype(BF)
    for g in range(graphs):
        rows = slice(g * LEN, (g + 1) * LEN)
        query, keys, values = qkv_ref[0, 0, rows, :], qkv_ref[0, 1, rows, :], qkv_ref[0, 2, rows, :]
        d_rows, expo = aug[rows, :], p_ref[0, rows, :]
        one, zero = jnp.ones_like(values), jnp.zeros_like(values)
        spread = jnp.concatenate(
            [
                jnp.where(
                    head_lanes(h, V_AT), values, jnp.where((lane == h) | (lane == SUB + h), one, zero)
                )
                for h in range(SUB)
            ],
            axis=0,
        )
        d_scores = (expo.astype(F32) * nt(d_rows, spread)).astype(BF)
        d_query = nn(d_scores, by_head(keys, 0)) * SCALE
        d_keys = tn(stack_heads(d_scores), by_head(query, 0)) * SCALE
        d_values = tn(stack_heads(expo), by_head(d_rows, V_AT))
        rolled_keys, rolled_values = pltpu.roll(d_keys, SW, 1), pltpu.roll(d_values, V_AT, 1)
        d_ref[0, rows, 0:128] = jnp.where(lane < SW, d_query, rolled_keys).astype(BF)
        d_ref[0, rows, 128:256] = jnp.where(lane < 64, rolled_keys, rolled_values).astype(BF)
        d_ref[0, rows, 256:384] = jnp.where(lane < V_AT, rolled_values, 0.0).astype(BF)
    grad = nn(xt_ref[...], d_ref[0])
    grad_out = nn(dt_ref[...], heads_out)
    g_ref[0, :, 0:256] = grad[:, 0:256].astype(BF)
    g_ref[0, :, 256:384] = (grad[:, 256:384] + grad_out).astype(BF)


def attend_back(xt, dt, d_attn, w, saved, first, stride, groups):
    qkv, expo, heads_out, rinv = saved
    tokens = d_attn.shape[0]
    block = lambda *tail: pl.BlockSpec(
        (1,) + tail, lambda i: (first + i * stride,) + (0,) * len(tail)
    )
    out = lambda *tail: pl.BlockSpec((1,) + tail, lambda i: (i,) + (0,) * len(tail))
    full = lambda a: pl.BlockSpec(a.shape, lambda i: (0,) * a.ndim)
    return pl.pallas_call(
        functools.partial(attend_back_kernel, graphs=tokens // LEN),
        grid=(groups,),
        in_specs=[
            full(xt),
            full(dt),
            full(d_attn),
            block(D, PACK),
            block(3, tokens, 128),
            block(tokens, 512),
            block(tokens, 128),
            block(tokens, 128),
        ],
        out_specs=[out(D, PACK), out(tokens, PACK)],
        out_shape=[
            jax.ShapeDtypeStruct((groups, D, PACK), BF),
            jax.ShapeDtypeStruct((groups, tokens, PACK), BF),
        ],
        scratch_shapes=[pltpu.VMEM((tokens, 128), BF)],
        compiler_params=pltpu.CompilerParams(vmem_limit_bytes=VMEM_LIMIT),
        cost_estimate=pl.CostEstimate(
            flops=groups * 6_000_000_000, bytes_accessed=groups * 3_000_000, transcendentals=0
        ),
        name="attend_back",
    )(xt, dt, d_attn, w, qkv, expo, heads_out, rinv)


def first_back_kernel(e_ref, dmid_ref, ident_ref, gain_ref, *refs, parts):
    d_refs, w_refs = refs[: len(parts)], refs[len(parts) : -2]
    out_ref, acc = refs[-2:]
    step, steps = pl.program_id(0), pl.num_programs(0)
    d_normed = jnp.zeros(e_ref.shape, F32)
    for d_ref, (which, picks) in zip(d_refs, parts):
        for j, at in enumerate(picks):
            d_normed = d_normed + nt(d_ref[j], w_refs[which][at])
    xhat, rstd = normalize(e_ref[...])
    d_emb = dmid_ref[...] + norm_back(d_normed, xhat, rstd, gain_ref[0:1, :])
    part = tn(ident_ref[...], d_emb.astype(BF))
    part_gain = jnp.sum((d_normed * xhat).reshape(-1, 8, D), axis=0)

    @pl.when(step == 0)
    def _():
        acc[0 : 2 * LAP, :] = part
        acc[2 * LAP :, :] = part_gain

    @pl.when(step > 0)
    def _():
        acc[0 : 2 * LAP, :] += part
        acc[2 * LAP :, :] += part_gain

    @pl.when(step == steps - 1)
    def _():
        out_ref[...] = acc[...]


def first_back(embedded, d_middle, ident_rows, gains, ds, parts, weights):
    tokens = embedded.shape[0]
    rows = LEN * min(2, tokens // LEN)
    full = lambda a: pl.BlockSpec(a.shape, lambda i: (0,) * a.ndim)
    tile = pl.BlockSpec((rows, D), lambda i: (i, 0))
    return pl.pallas_call(
        functools.partial(first_back_kernel, parts=parts),
        grid=(tokens // rows,),
        in_specs=[tile, tile, pl.BlockSpec((rows, 2 * LAP), lambda i: (i, 0)), full(gains)]
        + [pl.BlockSpec((d.shape[0], rows, PACK), lambda i: (0, i, 0)) for d in ds]
        + [full(w) for w in weights],
        out_specs=pl.BlockSpec((2 * LAP + 8, D), lambda i: (0, 0)),
        out_shape=jax.ShapeDtypeStruct((2 * LAP + 8, D), F32),
        scratch_shapes=[pltpu.VMEM((2 * LAP + 8, D), F32)],
        compiler_params=pltpu.CompilerParams(vmem_limit_bytes=VMEM_LIMIT),
        cost_estimate=pl.CostEstimate(
            flops=8_000_000_000, bytes_accessed=15_000_000, transcendentals=0
        ),
        name="first_back",
    )(embedded, d_middle, ident_rows, gains, *ds, *weights)


def erf(x):
    x = jnp.clip(x, -3.832506856900711, 3.832506856900711)
    x2 = x * x
    top = 0.00022905065861350646
    for c in (
        0.0034082910107109506,
        0.050955695062380861,
        0.18520832239976145,
        1.128379143519084,
    ):
        top = top * x2 + c
    bottom = -1.1791602954361697e-7
    for c in (
        0.000023547966471313185,
        0.0010179625278914885,
        0.014070470171167667,
        0.11098505178285362,
        0.49746925110067538,
        1.0,
    ):
        bottom = bottom * x2 + c
    return x * top / bottom


def normalize(values):
    centred = values - jnp.mean(values, axis=-1, keepdims=True)
    spread = jnp.mean(centred * centred, axis=-1, keepdims=True)
    rstd = lax.rsqrt(spread + NORM_EPS)
    return centred * rstd, rstd


def two_parts(v):
    high = v.astype(BF)
    return high, (v - high.astype(F32)).astype(BF)


def forward_kernel(
    lens_ref, partner_ref, e_ref, gain_ref, up_ref, down_ref, *refs, tile_graphs, waves, groups
):
    o_refs, w_refs = refs[:waves], refs[waves : 2 * waves]
    mid_ref, slope_ref, pay_ref, hsum, msum = refs[2 * waves :]
    step, steps = pl.program_id(0), pl.num_programs(0)
    middle = e_ref[...]
    for wave in range(waves):
        left = jnp.concatenate([o_refs[wave][j] for j in range(groups)], axis=1)
        right = jnp.concatenate([w_refs[wave][j][:, 256:] for j in range(groups)], axis=1)
        middle = middle + nt(left, right)
    mid_ref[...] = middle
    xhat, _ = normalize(middle)
    up = nn((xhat * gain_ref[1:2, :]).astype(BF), up_ref[...])
    cdf = 0.5 + 0.5 * erf(up * (0.5**0.5))
    hidden = (up * cdf).astype(BF).astype(F32)
    slope_ref[...] = (cdf + up * (0.3989422804014327 * jnp.exp(-0.5 * up * up))).astype(BF)
    place = lax.broadcasted_iota(jnp.int32, (LEN, 1), 0)
    for j in range(tile_graphs):
        g = step * tile_graphs + j
        live = place < lens_ref[g]
        rows = slice(j * LEN, (j + 1) * LEN)
        hsum[pl.ds(g, 1), :] = jnp.sum(jnp.where(live, hidden[rows], 0.0), axis=0, keepdims=True)
        msum[pl.ds(g, 1), :] = jnp.sum(jnp.where(live, middle[rows], 0.0), axis=0, keepdims=True)

    @pl.when(step == steps - 1)
    def _():
        graphs = hsum.shape[0]
        high, low = two_parts(hsum[...])
        which = lax.broadcasted_iota(jnp.int32, (graphs, 1), 0)
        length, partner = jnp.ones((graphs, 1), F32), jnp.zeros((graphs, 1), F32)
        for g in range(graphs):
            length = jnp.where(which == g, lens_ref[g].astype(F32), length)
            partner = jnp.where(which == g, partner_ref[g].astype(F32), partner)
        pooled = (msum[...] + (nt(high, down_ref[...]) + nt(low, down_ref[...]))) / length
        xhat_pool, rstd = normalize(pooled)
        high, low = two_parts(xhat_pool)
        pay_ref[:, 0:D] = high
        pay_ref[:, D : 2 * D] = low
        pay_ref[:, 2 * D : 3 * D] = hsum[...].astype(BF)
        lane = lanes()
        stats = jnp.zeros((graphs, 128), F32)
        for at, value in enumerate(two_parts(rstd) + two_parts(1.0 / length) + (partner,)):
            stats = jnp.where(lane == at, value.astype(F32), stats)
        pay_ref[:, 3 * D :] = stats.astype(BF)


def forward_rest(lens, partner, embedded, gains, w_up, w_down, outs, weights):
    tokens = embedded.shape[0]
    graphs = tokens // LEN
    tile_graphs = min(2, graphs)
    rows = tile_graphs * LEN
    waves, groups = len(outs), outs[0].shape[0]
    full = lambda a: pl.BlockSpec(a.shape, lambda i: (0,) * a.ndim)
    tile = pl.BlockSpec((rows, D), lambda i: (i, 0))
    return pl.pallas_call(
        functools.partial(forward_kernel, tile_graphs=tile_graphs, waves=waves, groups=groups),
        grid=(tokens // rows,),
        in_specs=[pl.BlockSpec(memory_space=pltpu.SMEM)] * 2
        + [tile, full(gains), full(w_up), full(w_down)]
        + [pl.BlockSpec((groups, rows, 128), lambda i: (0, i, 0)) for _ in outs]
        + [full(w) for w in weights],
        out_specs=[
            tile,
            tile,
            pl.BlockSpec((graphs, 3 * D + 128), lambda i: (0, 0)),
        ],
        out_shape=[
            jax.ShapeDtypeStruct((tokens, D), F32),
            jax.ShapeDtypeStruct((tokens, D), BF),
            jax.ShapeDtypeStruct((graphs, 3 * D + 128), BF),
        ],
        scratch_shapes=[pltpu.VMEM((graphs, D), F32), pltpu.VMEM((graphs, D), F32)],
        compiler_params=pltpu.CompilerParams(vmem_limit_bytes=VMEM_LIMIT),
        cost_estimate=pl.CostEstimate(
            flops=10_000_000_000, bytes_accessed=20_000_000, transcendentals=0
        ),
        name="forward_rest",
    )(lens, partner, embedded, gains, w_up, w_down, *outs, *weights)


def norm_back(d_normed, xhat, rstd, gain):
    d_hat = d_normed * gain
    return rstd * (
        d_hat
        - jnp.mean(d_hat, axis=-1, keepdims=True)
        - xhat * jnp.mean(d_hat * xhat, axis=-1, keepdims=True)
    )


def ffn_back_kernel(
    lens_ref, mid_ref, slope_ref, dout_ref, dhid_ref, gain_ref, up_ref,
    dmid_ref, dattn_ref, dt_ref, grad_ref, dgain_ref, grad, dgain, *, tile_graphs
):
    step, steps = pl.program_id(0), pl.num_programs(0)
    xhat, rstd = normalize(mid_ref[...])
    gain = gain_ref[1:2, :]
    place = lax.broadcasted_iota(jnp.int32, (LEN, 1), 0)
    d_up, d_out = [], []
    for j in range(tile_graphs):
        g = step * tile_graphs + j
        live = place < lens_ref[g]
        rows = slice(j * LEN, (j + 1) * LEN)
        d_hidden = jnp.where(live, dhid_ref[pl.ds(g, 1), :], 0.0)
        d_up.append((slope_ref[rows, :].astype(F32) * d_hidden).astype(BF))
        d_out.append(jnp.where(live, dout_ref[pl.ds(g, 1), :], 0.0))
    d_up, d_out = jnp.concatenate(d_up, axis=0), jnp.concatenate(d_out, axis=0)
    d_normed = nt(d_up, up_ref[...])
    d_mid = d_out + norm_back(d_normed, xhat, rstd, gain)
    dmid_ref[...] = d_mid
    d_attn = d_mid.astype(BF)
    dattn_ref[...] = d_attn
    dt_ref[...] = d_attn.T
    part = tn((xhat * gain).astype(BF), d_up)
    part_gain = jnp.sum((d_normed * xhat).reshape(-1, 8, D), axis=0)

    @pl.when(step == 0)
    def _():
        grad[...] = part
        dgain[...] = part_gain

    @pl.when(step > 0)
    def _():
        grad[...] += part
        dgain[...] += part_gain

    @pl.when(step == steps - 1)
    def _():
        for half in range(2):
            grad_ref[half] = grad[:, half * PACK : (half + 1) * PACK].astype(BF)
        dgain_ref[...] = dgain[...]


def ffn_back(lens, middle, slope, d_out, d_hidden, gains, w_up):
    tokens = middle.shape[0]
    tile_graphs = min(2, tokens // LEN)
    rows = tile_graphs * LEN
    full = lambda a: pl.BlockSpec(a.shape, lambda i: (0,) * a.ndim)
    tile = pl.BlockSpec((rows, D), lambda i: (i, 0))
    return pl.pallas_call(
        functools.partial(ffn_back_kernel, tile_graphs=tile_graphs),
        grid=(tokens // rows,),
        in_specs=[pl.BlockSpec(memory_space=pltpu.SMEM), tile, tile]
        + [full(a) for a in (d_out, d_hidden, gains, w_up)],
        out_specs=[
            tile,
            tile,
            pl.BlockSpec((D, rows), lambda i: (0, i)),
            pl.BlockSpec((2, D, PACK), lambda i: (0, 0, 0)),
            pl.BlockSpec((8, D), lambda i: (0, 0)),
        ],
        out_shape=[
            jax.ShapeDtypeStruct((tokens, D), F32),
            jax.ShapeDtypeStruct((tokens, D), BF),
            jax.ShapeDtypeStruct((D, tokens), BF),
            jax.ShapeDtypeStruct((2, D, PACK), BF),
            jax.ShapeDtypeStruct((8, D), F32),
        ],
        scratch_shapes=[pltpu.VMEM((D, D), F32), pltpu.VMEM((8, D), F32)],
        compiler_params=pltpu.CompilerParams(vmem_limit_bytes=VMEM_LIMIT),
        cost_estimate=pl.CostEstimate(
            flops=10_000_000_000, bytes_accessed=15_000_000, transcendentals=0
        ),
        name="ffn_back",
    )(lens, middle, slope, d_out, d_hidden, gains, w_up)


class Place:
    def __init__(self):
        self.n, self.heads = lax.axis_size("dp"), lax.axis_size("head")
        self.outs = self.n // 2
        dp, head = lax.axis_index("dp"), lax.axis_index("head")
        self.dp, self.head = dp, head
        self.outer, self.inner, self.far, self.core = dp // 2, dp % 2, head // 2, head % 2

    def move(self, v, to):
        pairs = []
        for i in range(self.n * self.heads):
            outer, inner, far, core = i // 8, (i // 4) % 2, (i // 2) % 2, i % 2
            outer, inner, far, core = to(outer, inner, far, core)
            pairs.append((i, ((outer % self.outs * 2 + inner) * 2 + far) * 2 + core))
        return lax.ppermute(v, ("dp", "head"), pairs)

    def to_core(self, v):
        return self.move(v, lambda o, i, f, c: (o, i, f, 1 - c))

    def to_outer(self, v, by):
        return self.move(v, lambda o, i, f, c: (o + by, i, f, c))

    def mixed(self, v, turn):
        return self.move(
            v, lambda o, i, f, c: (o, 1 - i, f, c) if c == turn else (o, i, 1 - f, c)
        )

    def by_core(self, a, b):
        return jnp.where(self.core == 0, a, b)

    def gather_outer(self, v):
        out = jnp.zeros((self.outs,) + v.shape, v.dtype)
        out = lax.dynamic_update_index_in_dim(out, v, self.outer, 0)
        for by in range(1, self.outs):
            out = lax.dynamic_update_index_in_dim(
                out, self.to_outer(v, by), (self.outer - by) % self.outs, 0
            )
        return out

    def gather_pieces(self, v):
        return self.gather_near(self.gather_outer(v))

    def gather_near(self, own):
        second = self.mixed(own, 0)
        third = self.mixed(jnp.stack([own, second]), 1)
        return [
            [own, self.by_core(second, third[0])],
            [self.by_core(third[0], second), third[1]],
        ]

    def whole(self, pieces):
        rows = [
            [jnp.where(self.far == 0, pieces[f][i], pieces[1 - f][i]) for f in range(2)]
            for i in range(2)
        ]
        ordered = [
            [jnp.where(self.inner == 0, rows[i][f], rows[1 - i][f]) for f in range(2)]
            for i in range(2)
        ]
        return jnp.stack([jnp.stack(pair, axis=1) for pair in ordered], axis=1)

    def both_cores(self, v, axis):
        other = self.to_core(v)
        return jnp.stack([self.by_core(v, other), self.by_core(other, v)], axis=axis)

    def both_cores_of(self, own, sent):
        other = self.to_core(sent)
        return jnp.stack([self.by_core(own, other), self.by_core(other, own)])

    def gather_all(self, v):
        v = self.both_cores(self.whole(self.gather_pieces(v)), 3)
        return v.reshape((self.n, self.heads) + v.shape[4:])

    def fold_far(self, pieces):
        sent = jnp.stack([self.by_core(pieces[1][0], pieces[0][1]), pieces[1][1]])
        kept = jnp.stack([pieces[0][0], self.by_core(pieces[0][1], pieces[1][0])])
        return kept, sent

    def fold_near(self, kept, came, dtype):
        total = kept.astype(F32) + came.astype(F32)
        return total[0], total[1].astype(dtype)

    def fold_outer(self, kept, came, dtype):
        total = (kept.astype(F32) + came.astype(F32)).astype(dtype)
        pick = lambda by: lax.dynamic_index_in_dim(
            total, (self.outer + by) % self.outs, 0, keepdims=False
        )
        result = pick(0).astype(F32)
        for by in range(1, self.outs):
            result = result + self.to_outer(pick(by), by).astype(F32)
        return result

    def total(self, v):
        v = v + self.to_core(v)
        v = v + self.move(v, lambda o, i, f, c: (o, i, 1 - f, c))
        v = v + self.move(v, lambda o, i, f, c: (o, 1 - i, f, c))
        by = 1
        while by < self.outs:
            v = v + self.move(v, lambda o, i, f, c, by=by: (o ^ by, i, f, c))
            by *= 2
        return v

    def split_rows(self, v):
        v = v.reshape((self.outs, 2, -1) + v.shape[1:])
        return [
            lax.dynamic_index_in_dim(v, (self.inner + i) % 2, 1, keepdims=False) for i in range(2)
        ]


def tie(*values):
    return lax.optimization_barrier(values)


def log_total(values, axis):
    top = jnp.max(values, axis=axis, keepdims=True)
    return jnp.squeeze(top, axis) + jnp.log(jnp.sum(jnp.exp(values - top), axis=axis))


def identifiers(table, endpoints):
    graphs = endpoints.shape[0] // LEN
    nodes = table.reshape(graphs, NODE, LAP).astype(BF)
    picks = (
        endpoints.reshape(graphs, LEN, 2)[..., None] == jnp.arange(NODE, dtype=jnp.int32)
    ).astype(BF)
    found = jnp.einsum("glan,gnc->glac", picks, nodes, preferred_element_type=F32)
    return found.reshape(graphs * LEN, 2 * LAP).astype(BF)


def split_core(place, grad_up):
    v = grad_up.reshape((2, place.outs, 2, 2, 2, -1, PACK))
    pick = lambda at: lax.dynamic_index_in_dim(v, at, 4, keepdims=False)
    return pick(1 - place.core), pick(place.core)


def fold_pieces(place, own, came, up):
    pieces = []
    for f in range(2):
        total = own[f].astype(F32) + came[f].astype(F32)
        pieces.append([v.astype(BF) for v in place.split_rows(total)])
    if up is None:
        return pieces
    total = (up[0].astype(F32) + up[1].astype(F32)).astype(BF)
    for f in range(2):
        part = lax.dynamic_index_in_dim(total, (place.far + f) % 2, 3, keepdims=False)
        for i in range(2):
            rows = lax.dynamic_index_in_dim(part, (place.inner + i) % 2, 2, keepdims=False)
            pieces[f][i] = jnp.concatenate([pieces[f][i], rows[0], rows[1]], axis=1)
    return pieces


def adam_step(weight, gradient, first, second, factor, rate):
    clipped = gradient * factor
    first_new = BETA_ONE * first + (1.0 - BETA_ONE) * clipped
    second_new = BETA_TWO * second + (1.0 - BETA_TWO) * clipped * clipped
    first_hat = first_new / (1.0 - BETA_ONE**STEPS)
    second_hat = second_new / (1.0 - BETA_TWO**STEPS)
    weight_new = weight - rate * (first_hat / (jnp.sqrt(second_hat) + ADAM_EPS) + DECAY * weight)
    return (weight_new, first_new, second_new)


def per_device(
    features,
    laplacian,
    endpoints,
    lengths,
    pairing,
    ident_weight,
    qkv_weight,
    out_weight,
    ffn_weight,
    norm_gains,
    ident_first,
    qkv_first,
    out_first,
    ffn_first,
    gains_first,
    ident_second,
    qkv_second,
    out_second,
    ffn_second,
    gains_second,
):
    place = Place()
    heads, head, dp, core = place.heads, place.head, place.dp, place.core
    tokens = features.shape[0] // heads
    graphs = tokens // LEN
    own_columns = norm_gains.shape[1]

    small = jnp.concatenate([ident_weight, norm_gains], axis=0)
    small_rows = small.shape[0]

    packed = [qkv_weight[:, 0], qkv_weight[:, 1], qkv_weight[:, 2], out_weight.T]
    shards = jnp.stack(
        [
            jnp.concatenate([m[:, s * SW : (s + 1) * SW] for m in packed], axis=1).astype(BF)
            for s in range(2)
        ]
    )
    pick = lambda v, at: lax.dynamic_index_in_dim(v, at, 0, keepdims=False)
    near = jnp.stack([pick(shards, core), place.to_core(pick(shards, 1 - core))])
    near, small = tie(near, small.reshape(1, -1))
    near, small = tie(place.gather_outer(near), place.gather_outer(small))
    pieces = place.gather_near(near)
    small = place.both_cores(place.whole(place.gather_near(small)), 3)
    small = small.reshape(-1, small_rows, own_columns).transpose(1, 0, 2).reshape(small_rows, D)
    ident_full, gains = small[: 2 * LAP].astype(BF), small[2 * LAP :]
    mine = jnp.stack(
        [
            jnp.stack(
                [
                    jnp.where(place.inner == i, pieces[f][0][:, c], pieces[f][1][:, c])
                    for i in range(2)
                ],
                axis=1,
            ).reshape(D, PACK)
            for f in range(2)
            for c in range(2)
        ]
    )
    others = place.to_core(mine)
    ffn, near = tie(ffn_weight.astype(BF), near)
    ffn_near = place.both_cores_of(pick(ffn, core), pick(ffn, 1 - core))
    ffn_mine = place.whole(place.gather_pieces(ffn_near)).reshape(D, -1)
    ffn_other = place.to_core(ffn_mine)
    w_up, w_down = place.by_core(ffn_mine, ffn_other), place.by_core(ffn_other, ffn_mine)

    start_row = head * tokens
    lens = lax.dynamic_slice_in_dim(lengths.reshape(-1), head * graphs, graphs, 0)
    partner = lax.dynamic_slice_in_dim(
        jnp.concatenate([pairing.reshape(-1)] * 2), head * graphs, graphs, 0
    )
    table_rows = lax.dynamic_slice_in_dim(laplacian, head * graphs * NODE, graphs * NODE, 0)
    end_rows = lax.dynamic_slice_in_dim(endpoints, start_row, tokens, 0)
    ident_rows = identifiers(table_rows, end_rows)
    embedded = lax.dynamic_slice_in_dim(features, start_row, tokens, 0).astype(F32)
    embedded = embedded + nn(ident_rows, ident_full)
    normed_one = (normalize(embedded)[0] * gains[0]).astype(BF)

    saved_mine = attend(lens, normed_one, mine)
    saved_others = attend(lens, normed_one, others)
    normed_turned = normed_one.T
    middle, slope, payload = forward_rest(
        lens, partner, embedded, gains, w_up, w_down, [saved_mine[2], saved_others[2]], [mine, others]
    )

    everyone = place.gather_all(payload).reshape(place.n, 2, GRAPHS_DEV, -1)
    stats = everyone[..., 3 * D :].astype(F32)
    xhat = everyone[..., :D].astype(F32) + everyone[..., D : 2 * D].astype(F32)
    hidden_sums = everyone[..., 2 * D : 3 * D].reshape(-1, D)
    rstd_pool = (stats[..., 0:1] + stats[..., 1:2]).reshape(-1, 1)
    share = (stats[..., 2:3] + stats[..., 3:4]).reshape(-1, 1)
    summaries = xhat * gains[2]
    left, right = summaries[:, 0].reshape(-1, D), summaries[:, 1].reshape(-1, D)
    root_width = D**0.5
    logits = jnp.dot(left, right.T, precision=HIGHEST) / root_width
    row_totals, col_totals = log_total(logits, 1), log_total(logits, 0)
    count = logits.shape[0]
    group = jnp.arange(count, dtype=jnp.int32) // GRAPHS_DEV
    partners = group * GRAPHS_DEV + stats[:, 0, :, 4].reshape(-1).astype(jnp.int32)
    positive = (partners[:, None] == jnp.arange(count, dtype=jnp.int32)[None, :]).astype(F32)
    total_loss = jnp.sum(row_totals) + jnp.sum(col_totals) - 2.0 * jnp.sum(positive * logits)
    d_logits = (
        jnp.exp(logits - row_totals[:, None])
        + jnp.exp(logits - col_totals[None, :])
        - 2.0 * positive
    )
    d_left = jnp.dot(d_logits, right, precision=HIGHEST) / root_width
    d_right = jnp.dot(d_logits.T, left, precision=HIGHEST) / root_width
    d_summary = jnp.stack(
        [d_left.reshape(place.n, GRAPHS_DEV, D), d_right.reshape(place.n, GRAPHS_DEV, D)], axis=1
    ).reshape(-1, D)
    xhat = xhat.reshape(-1, D)
    gain_three = jnp.sum(d_summary * xhat, axis=0)
    d_rows = norm_back(d_summary, xhat, rstd_pool, gains[2]) * share
    d_rows_low = d_rows.astype(BF)
    own_row = (dp * heads + head) * graphs
    d_out = lax.dynamic_slice_in_dim(d_rows, own_row, graphs, 0)
    d_hidden = nn(d_out.astype(BF), w_down)

    own_column = (dp * heads + head) * own_columns
    d_columns = lax.dynamic_slice_in_dim(d_rows_low, own_column, own_columns, 1)
    grad_down = tn(d_columns, hidden_sums)
    d_middle, d_attn, d_turned, grad_up, gain_two = ffn_back(
        lens, middle, slope, d_out, d_hidden, gains, w_up
    )
    back = functools.partial(attend_back, normed_turned)
    up_sent, up_kept = split_core(place, grad_up)
    up_came = place.to_core(up_sent)
    grad_others, d_others = back(d_turned, d_attn, others, saved_others, 0, 1, heads)
    came = place.to_core(grad_others)
    d_attn, grad_others = tie(d_attn, grad_others)
    grad_even, d_even = back(d_turned, d_attn, mine, saved_mine, 0, 2, heads // 2)
    even = fold_pieces(place, [grad_even[0], grad_even[1]], [came[0], came[2]], (up_kept, up_came))
    even_kept, even_sent = place.fold_far(even)
    even_sent, d_attn = tie(even_sent, d_attn)
    even_came = place.mixed(even_sent, 1)
    grad_odd, d_odd = back(d_turned, d_attn, mine, saved_mine, 1, 2, 1)
    d_attn, even_came, grad_odd = tie(d_attn, even_came, grad_odd)
    even_kept, even_sent = place.fold_near(even_kept, even_came, BF)
    even_came = place.mixed(even_sent, 0)
    grad_last, d_last = back(d_turned, d_attn, mine, saved_mine, 3, 2, 1)
    grad_last, even_came = tie(grad_last, even_came)
    odd = fold_pieces(place, [grad_odd[0], grad_last[0]], [came[1], came[3]], None)
    odd_kept, odd_sent = place.fold_far(odd)
    odd_sent, d_last = tie(odd_sent, d_last)
    odd_came = place.mixed(odd_sent, 1)
    even = place.fold_outer(even_kept, even_came, BF)
    rows = first_back(
        embedded,
        d_middle,
        ident_rows,
        gains,
        [d_others, d_even, d_odd, d_last],
        ((1, (0, 1, 2, 3)), (0, (0, 2)), (0, (1,)), (0, (3,))),
        [mine, others],
    )
    odd_came, rows, even = tie(odd_came, rows, even)
    odd_kept, odd_sent = place.fold_near(odd_kept, odd_came, BF)
    odd_came = place.mixed(odd_sent, 0)
    odd = place.fold_outer(odd_kept, odd_came, BF)
    gain_rows = jnp.stack([jnp.sum(rows[2 * LAP :], axis=0), jnp.sum(gain_two, axis=0)])
    rows = jnp.concatenate([rows[: 2 * LAP], gain_rows], axis=0)
    row_count = rows.shape[0]
    rows = rows.T.reshape(place.outs, 2, 2, 2, own_columns * row_count)
    rows_kept = lax.dynamic_index_in_dim(rows, core, 3, keepdims=False)
    rows = rows_kept + place.to_core(lax.dynamic_index_in_dim(rows, 1 - core, 3, keepdims=False))
    turn = lambda v, axis, own, at: lax.dynamic_index_in_dim(v, (own + at) % 2, axis, keepdims=False)
    rows = [[turn(turn(rows, 2, place.far, f), 1, place.inner, i) for i in range(2)] for f in range(2)]
    rows_kept, rows_sent = place.fold_far(rows)
    rows_kept, rows_sent = place.fold_near(rows_kept, place.mixed(rows_sent, 1), F32)
    rows = place.fold_outer(rows_kept, place.mixed(rows_sent, 0), F32).reshape(own_columns, row_count).T
    grad_ident = rows[: 2 * LAP]
    grad_gains = jnp.concatenate(
        [rows[2 * LAP :], lax.dynamic_slice_in_dim(gain_three, own_column, own_columns, 0)[None]],
        axis=0,
    )
    shard_rows = D // place.n
    own_half, other_half = even[:shard_rows], place.to_core(odd)
    halves = [place.by_core(own_half, other_half), place.by_core(other_half, own_half)]
    columns = lambda j: jnp.concatenate([v[:, j * SW : (j + 1) * SW] for v in halves], axis=1)
    grad_qkv = jnp.stack([columns(0), columns(1), columns(2)], axis=1)
    grad_out = columns(3).T
    grad_up = even[shard_rows:].reshape(2, own_columns, PACK)
    grad_ffn = jnp.stack([jnp.concatenate([grad_up[0], grad_up[1]], axis=1), grad_down])

    grads = (grad_ident, grad_qkv, grad_out, grad_ffn, grad_gains)
    squares = sum((jnp.sum(gradient * gradient) for gradient in grads))
    grad_norm = jnp.sqrt(place.total(squares))
    factor = CLIP_AT / jnp.maximum(grad_norm, CLIP_AT)
    results = [
        adam_step(weight, gradient, first, second, factor, rate)
        for weight, gradient, first, second, rate in zip(
            (ident_weight, qkv_weight, out_weight, ffn_weight, norm_gains),
            grads,
            (ident_first, qkv_first, out_first, ffn_first, gains_first),
            (ident_second, qkv_second, out_second, ffn_second, gains_second),
            STEP_RATES,
        )
    ]
    return (grad_norm, total_loss) + tuple(r[k] for k in range(3) for r in results)


def solution(mesh):
    both = P(None, ("dp", "head"))
    weights = (both, P("dp", None, "head"), P("head", "dp"), P(None, ("dp", "head"), None), both)
    in_specs = (P("dp", None),) * 5 + weights * 3
    out_specs = (P(), P()) + weights * 3
    return jax.shard_map(
        per_device, mesh=mesh, in_specs=in_specs, out_specs=out_specs, check_vma=False
    )
```

```python
import functools

import jax
import jax.numpy as jnp
from jax import lax
from jax.experimental import pallas as pl
from jax.experimental.pallas import tpu as pltpu
from jax.sharding import PartitionSpec as P

D = 768
HEAD_DIM = 24
LAP = 16
LEN = 128
NODE = 32
STEPS = 3
GRAPHS_DEV = 16

HIGHEST = lax.Precision.HIGHEST
NORM_EPS = 1e-05
CLIP_AT = 5.0
STEP_RATES = (0.08, 0.02, 0.15, 0.02, 0.5)
BETA_ONE = 0.5
BETA_TWO = 0.5
DECAY = 0.01
ADAM_EPS = 1e-08
MASKED = -1e30

BF = jnp.bfloat16
F32 = jnp.float32
SUB = 4
SW = SUB * HEAD_DIM
PACK = 4 * SW
V_AT = 128 - SW
SCALE = HEAD_DIM ** (-0.5)
VMEM_LIMIT = 44 * 2**20


def nn(a, b):
    return lax.dot_general(a, b, (((1,), (0,)), ((), ())), preferred_element_type=F32)


def nt(a, b):
    return lax.dot_general(a, b, (((1,), (1,)), ((), ())), preferred_element_type=F32)


def tn(a, b):
    return lax.dot_general(a, b, (((0,), (0,)), ((), ())), preferred_element_type=F32)


def lanes():
    return lax.broadcasted_iota(jnp.int32, (1, 128), 1)


def head_lanes(h, at):
    lane = lanes()
    return (lane >= at + h * HEAD_DIM) & (lane < at + (h + 1) * HEAD_DIM)


def by_head(v, at):
    zero = jnp.zeros_like(v)
    return jnp.concatenate([jnp.where(head_lanes(h, at), v, zero) for h in range(SUB)], axis=0)


def stack_heads(v):
    return jnp.concatenate([v[:, h * LEN : (h + 1) * LEN] for h in range(SUB)], axis=0)


def attend_kernel(lens_ref, where_ref, x_ref, *refs, graphs, whole):
    if whole:
        w_ref, qkv_ref, p_ref, o_ref, rinv_ref = refs
    else:
        first_ref, third_ref, w_ref, qkv_ref, p_ref, o_ref, rinv_ref = refs
        outs, rows = first_ref.shape[1], first_ref.shape[3]
        far, head = pl.program_id(0) // 2, pl.program_id(0) % 2
        outer, inner, gatherer = where_ref[0], where_ref[1], where_ref[2]
        for i in range(2):
            in_first = (far == 0) if i == 0 else (far == 0) & (gatherer == 0)
            in_first = in_first | ((far == 1) & (gatherer == 1) & (i == 0))
            at = jnp.where(in_first, jnp.where(far + i == 0, 0, 1), jnp.where(far + i == 2, 1, 0))

            def place(source, at=at, i=i):
                for o in range(outs):
                    row = (lax.rem(outer + outs - o, outs) * 2 + (inner + i) % 2) * rows
                    w_ref[0, pl.ds(pl.multiple_of(row, rows), rows), :] = source[at, o, head]

            @pl.when(in_first)
            def _(place=place):
                place(first_ref)

            @pl.when(jnp.logical_not(in_first))
            def _(place=place):
                place(third_ref)

    y = nn(x_ref[...], w_ref[0])
    qkv_ref[0, 0] = y[:, :128].astype(BF)
    qkv_ref[0, 1] = pltpu.roll(y, PACK - SW, 1)[:, :128].astype(BF)
    qkv_ref[0, 2] = pltpu.roll(y, SW, 1)[:, 256:].astype(BF)
    col = lanes()
    ones = by_head(jnp.ones((LEN, 128), BF), V_AT)
    for g in range(graphs):
        rows = slice(g * LEN, (g + 1) * LEN)
        query, keys, values = qkv_ref[0, 0, rows, :], qkv_ref[0, 1, rows, :], qkv_ref[0, 2, rows, :]
        live = col < lens_ref[g]
        scores = nt(query, by_head(keys, 0))
        parts = []
        for h in range(SUB):
            own = jnp.where(live, scores[:, h * LEN : (h + 1) * LEN] * SCALE, MASKED)
            parts.append(jnp.exp(own - jnp.max(own, axis=1, keepdims=True)).astype(BF))
        expo = jnp.concatenate(parts, axis=1)
        both = nn(expo, jnp.concatenate([by_head(values, V_AT), ones], axis=1))
        rinv = jnp.where(col >= V_AT, 1.0 / both[:, 128:], 0.0)
        p_ref[0, rows, :] = expo
        rinv_ref[0, rows, :] = rinv
        o_ref[0, rows, :] = jnp.where(col >= V_AT, both[:, :128] * rinv, 0.0).astype(BF)


def attend(lens, where, x, pieces):
    tokens = x.shape[0]
    groups = 4
    whole = len(pieces) == 1
    block = lambda *tail: pl.BlockSpec((1,) + tail, lambda i: (i,) + (0,) * len(tail))
    full = lambda a: pl.BlockSpec(a.shape, lambda i: (0,) * a.ndim)
    out_specs = [block(3, tokens, 128), block(tokens, 512), block(tokens, 128), block(tokens, 128)]
    out_shape = [
        jax.ShapeDtypeStruct((groups, 3, tokens, 128), BF),
        jax.ShapeDtypeStruct((groups, tokens, 512), BF),
        jax.ShapeDtypeStruct((groups, tokens, 128), BF),
        jax.ShapeDtypeStruct((groups, tokens, 128), F32),
    ]
    if not whole:
        out_specs = [block(D, PACK)] + out_specs
        out_shape = [jax.ShapeDtypeStruct((groups, D, PACK), BF)] + out_shape
    result = pl.pallas_call(
        functools.partial(attend_kernel, graphs=tokens // LEN, whole=whole),
        grid=(groups,),
        in_specs=[pl.BlockSpec(memory_space=pltpu.SMEM)] * 2
        + [full(x)]
        + ([block(D, PACK)] if whole else [full(a) for a in pieces]),
        out_specs=out_specs,
        out_shape=out_shape,
        compiler_params=pltpu.CompilerParams(vmem_limit_bytes=VMEM_LIMIT),
        cost_estimate=pl.CostEstimate(
            flops=groups * 2_500_000_000, bytes_accessed=groups * 3_000_000, transcendentals=0
        ),
        name="attend",
    )(lens, where, x, *pieces)
    return (pieces[0], result) if whole else (result[0], result[1:])


def attend_back_kernel(
    xt_ref, dt_ref, da_ref, w_ref, qkv_ref, p_ref, o_ref, rinv_ref, g_ref, d_ref, aug, *, graphs
):
    w = w_ref[0]
    lane = lanes()
    d_out = jnp.where(lane >= V_AT, nn(da_ref[...], w[:, 256:]) * rinv_ref[0], 0.0)
    heads_out = o_ref[0]
    terms = d_out * heads_out.astype(F32)
    high, low = two_parts(terms)
    row = lax.broadcasted_iota(jnp.int32, (128, 128), 0)
    column = lax.broadcasted_iota(jnp.int32, (128, 128), 1)
    pick = jnp.zeros((128, 128), BF)
    for h in range(SUB):
        inside = (row >= V_AT + h * HEAD_DIM) & (row < V_AT + (h + 1) * HEAD_DIM)
        pick = jnp.where(inside & ((column == h) | (column == SUB + h)), jnp.ones_like(pick), pick)
    delta = nn(high, pick) + nn(low, pick)
    rounded = delta.astype(BF).astype(F32)
    aug[...] = jnp.where(
        lane >= V_AT, d_out, jnp.where(lane < SUB, -rounded, rounded - delta)
    ).astype(BF)
    for g in range(graphs):
        rows = slice(g * LEN, (g + 1) * LEN)
        query, keys, values = qkv_ref[0, 0, rows, :], qkv_ref[0, 1, rows, :], qkv_ref[0, 2, rows, :]
        d_rows, expo = aug[rows, :], p_ref[0, rows, :]
        one, zero = jnp.ones_like(values), jnp.zeros_like(values)
        spread = jnp.concatenate(
            [
                jnp.where(
                    head_lanes(h, V_AT), values, jnp.where((lane == h) | (lane == SUB + h), one, zero)
                )
                for h in range(SUB)
            ],
            axis=0,
        )
        d_scores = (expo.astype(F32) * nt(d_rows, spread)).astype(BF)
        d_query = nn(d_scores, by_head(keys, 0)) * SCALE
        d_keys = tn(stack_heads(d_scores), by_head(query, 0)) * SCALE
        d_values = tn(stack_heads(expo), by_head(d_rows, V_AT))
        rolled_keys, rolled_values = pltpu.roll(d_keys, SW, 1), pltpu.roll(d_values, V_AT, 1)
        d_ref[0, rows, 0:128] = jnp.where(lane < SW, d_query, rolled_keys).astype(BF)
        d_ref[0, rows, 128:256] = jnp.where(lane < 64, rolled_keys, rolled_values).astype(BF)
        d_ref[0, rows, 256:384] = jnp.where(lane < V_AT, rolled_values, 0.0).astype(BF)
    grad = nn(xt_ref[...], d_ref[0])
    grad_out = nn(dt_ref[...], heads_out)
    g_ref[0, :, 0:256] = grad[:, 0:256].astype(BF)
    g_ref[0, :, 256:384] = (grad[:, 256:384] + grad_out).astype(BF)


def attend_back(xt, dt, d_attn, w, saved, first, stride, groups):
    qkv, expo, heads_out, rinv = saved
    tokens = d_attn.shape[0]
    block = lambda *tail: pl.BlockSpec(
        (1,) + tail, lambda i: (first + i * stride,) + (0,) * len(tail)
    )
    out = lambda *tail: pl.BlockSpec((1,) + tail, lambda i: (i,) + (0,) * len(tail))
    full = lambda a: pl.BlockSpec(a.shape, lambda i: (0,) * a.ndim)
    return pl.pallas_call(
        functools.partial(attend_back_kernel, graphs=tokens // LEN),
        grid=(groups,),
        in_specs=[
            full(xt),
            full(dt),
            full(d_attn),
            block(D, PACK),
            block(3, tokens, 128),
            block(tokens, 512),
            block(tokens, 128),
            block(tokens, 128),
        ],
        out_specs=[out(D, PACK), out(tokens, PACK)],
        out_shape=[
            jax.ShapeDtypeStruct((groups, D, PACK), BF),
            jax.ShapeDtypeStruct((groups, tokens, PACK), BF),
        ],
        scratch_shapes=[pltpu.VMEM((tokens, 128), BF)],
        compiler_params=pltpu.CompilerParams(vmem_limit_bytes=VMEM_LIMIT),
        cost_estimate=pl.CostEstimate(
            flops=groups * 6_000_000_000, bytes_accessed=groups * 3_000_000, transcendentals=0
        ),
        name="attend_back",
    )(xt, dt, d_attn, w, qkv, expo, heads_out, rinv)


def first_back_kernel(e_ref, dmid_ref, ident_ref, gain_ref, *refs, parts):
    d_refs, w_refs = refs[: len(parts)], refs[len(parts) : -2]
    out_ref, acc = refs[-2:]
    step, steps = pl.program_id(0), pl.num_programs(0)
    d_normed = jnp.zeros(e_ref.shape, F32)
    for d_ref, (which, picks) in zip(d_refs, parts):
        for j, at in enumerate(picks):
            d_normed = d_normed + nt(d_ref[j], w_refs[which][at])
    xhat, rstd = normalize(e_ref[...])
    d_emb = dmid_ref[...] + norm_back(d_normed, xhat, rstd, gain_ref[0:1, :])
    part = tn(ident_ref[...], d_emb.astype(BF))
    part_gain = jnp.sum((d_normed * xhat).reshape(-1, 8, D), axis=0)

    @pl.when(step == 0)
    def _():
        acc[0 : 2 * LAP, :] = part
        acc[2 * LAP :, :] = part_gain

    @pl.when(step > 0)
    def _():
        acc[0 : 2 * LAP, :] += part
        acc[2 * LAP :, :] += part_gain

    @pl.when(step == steps - 1)
    def _():
        out_ref[...] = acc[...]


def first_back(embedded, d_middle, ident_rows, gains, ds, parts, weights):
    tokens = embedded.shape[0]
    rows = LEN * min(2, tokens // LEN)
    full = lambda a: pl.BlockSpec(a.shape, lambda i: (0,) * a.ndim)
    tile = pl.BlockSpec((rows, D), lambda i: (i, 0))
    return pl.pallas_call(
        functools.partial(first_back_kernel, parts=parts),
        grid=(tokens // rows,),
        in_specs=[tile, tile, pl.BlockSpec((rows, 2 * LAP), lambda i: (i, 0)), full(gains)]
        + [pl.BlockSpec((d.shape[0], rows, PACK), lambda i: (0, i, 0)) for d in ds]
        + [full(w) for w in weights],
        out_specs=pl.BlockSpec((2 * LAP + 8, D), lambda i: (0, 0)),
        out_shape=jax.ShapeDtypeStruct((2 * LAP + 8, D), F32),
        scratch_shapes=[pltpu.VMEM((2 * LAP + 8, D), F32)],
        compiler_params=pltpu.CompilerParams(vmem_limit_bytes=VMEM_LIMIT),
        cost_estimate=pl.CostEstimate(
            flops=8_000_000_000, bytes_accessed=15_000_000, transcendentals=0
        ),
        name="first_back",
    )(embedded, d_middle, ident_rows, gains, *ds, *weights)


def erf(x):
    x = jnp.clip(x, -3.832506856900711, 3.832506856900711)
    x2 = x * x
    top = 0.00022905065861350646
    for c in (
        0.0034082910107109506,
        0.050955695062380861,
        0.18520832239976145,
        1.128379143519084,
    ):
        top = top * x2 + c
    bottom = -1.1791602954361697e-7
    for c in (
        0.000023547966471313185,
        0.0010179625278914885,
        0.014070470171167667,
        0.11098505178285362,
        0.49746925110067538,
        1.0,
    ):
        bottom = bottom * x2 + c
    return x * top / bottom


def normalize(values):
    centred = values - jnp.mean(values, axis=-1, keepdims=True)
    spread = jnp.mean(centred * centred, axis=-1, keepdims=True)
    rstd = lax.rsqrt(spread + NORM_EPS)
    return centred * rstd, rstd


def two_parts(v):
    high = v.astype(BF)
    return high, (v - high.astype(F32)).astype(BF)


def forward_kernel(
    lens_ref, partner_ref, e_ref, gain_ref, up_ref, down_ref, *refs, tile_graphs, waves, groups
):
    o_refs, w_refs = refs[:waves], refs[waves : 2 * waves]
    mid_ref, slope_ref, pay_ref, hsum, msum = refs[2 * waves :]
    step, steps = pl.program_id(0), pl.num_programs(0)
    middle = e_ref[...]
    for wave in range(waves):
        left = jnp.concatenate([o_refs[wave][j] for j in range(groups)], axis=1)
        right = jnp.concatenate([w_refs[wave][j][:, 256:] for j in range(groups)], axis=1)
        middle = middle + nt(left, right)
    mid_ref[...] = middle
    xhat, _ = normalize(middle)
    up = nn((xhat * gain_ref[1:2, :]).astype(BF), up_ref[...])
    cdf = 0.5 + 0.5 * erf(up * (0.5**0.5))
    hidden = (up * cdf).astype(BF).astype(F32)
    slope_ref[...] = (cdf + up * (0.3989422804014327 * jnp.exp(-0.5 * up * up))).astype(BF)
    place = lax.broadcasted_iota(jnp.int32, (LEN, 1), 0)
    for j in range(tile_graphs):
        g = step * tile_graphs + j
        live = place < lens_ref[g]
        rows = slice(j * LEN, (j + 1) * LEN)
        hsum[pl.ds(g, 1), :] = jnp.sum(jnp.where(live, hidden[rows], 0.0), axis=0, keepdims=True)
        msum[pl.ds(g, 1), :] = jnp.sum(jnp.where(live, middle[rows], 0.0), axis=0, keepdims=True)

    @pl.when(step == steps - 1)
    def _():
        graphs = hsum.shape[0]
        high, low = two_parts(hsum[...])
        which = lax.broadcasted_iota(jnp.int32, (graphs, 1), 0)
        length, partner = jnp.ones((graphs, 1), F32), jnp.zeros((graphs, 1), F32)
        for g in range(graphs):
            length = jnp.where(which == g, lens_ref[g].astype(F32), length)
            partner = jnp.where(which == g, partner_ref[g].astype(F32), partner)
        pooled = (msum[...] + (nt(high, down_ref[...]) + nt(low, down_ref[...]))) / length
        xhat_pool, rstd = normalize(pooled)
        high, low = two_parts(xhat_pool)
        pay_ref[:, 0:D] = high
        pay_ref[:, D : 2 * D] = low
        pay_ref[:, 2 * D : 3 * D] = hsum[...].astype(BF)
        lane = lanes()
        stats = jnp.zeros((graphs, 128), F32)
        for at, value in enumerate(two_parts(rstd) + two_parts(1.0 / length) + (partner,)):
            stats = jnp.where(lane == at, value.astype(F32), stats)
        pay_ref[:, 3 * D :] = stats.astype(BF)


def forward_rest(lens, partner, embedded, gains, w_up, w_down, outs, weights):
    tokens = embedded.shape[0]
    graphs = tokens // LEN
    tile_graphs = min(2, graphs)
    rows = tile_graphs * LEN
    waves, groups = len(outs), outs[0].shape[0]
    full = lambda a: pl.BlockSpec(a.shape, lambda i: (0,) * a.ndim)
    tile = pl.BlockSpec((rows, D), lambda i: (i, 0))
    return pl.pallas_call(
        functools.partial(forward_kernel, tile_graphs=tile_graphs, waves=waves, groups=groups),
        grid=(tokens // rows,),
        in_specs=[pl.BlockSpec(memory_space=pltpu.SMEM)] * 2
        + [tile, full(gains), full(w_up), full(w_down)]
        + [pl.BlockSpec((groups, rows, 128), lambda i: (0, i, 0)) for _ in outs]
        + [full(w) for w in weights],
        out_specs=[
            tile,
            tile,
            pl.BlockSpec((graphs, 3 * D + 128), lambda i: (0, 0)),
        ],
        out_shape=[
            jax.ShapeDtypeStruct((tokens, D), F32),
            jax.ShapeDtypeStruct((tokens, D), BF),
            jax.ShapeDtypeStruct((graphs, 3 * D + 128), BF),
        ],
        scratch_shapes=[pltpu.VMEM((graphs, D), F32), pltpu.VMEM((graphs, D), F32)],
        compiler_params=pltpu.CompilerParams(vmem_limit_bytes=VMEM_LIMIT),
        cost_estimate=pl.CostEstimate(
            flops=10_000_000_000, bytes_accessed=20_000_000, transcendentals=0
        ),
        name="forward_rest",
    )(lens, partner, embedded, gains, w_up, w_down, *outs, *weights)


def norm_back(d_normed, xhat, rstd, gain):
    d_hat = d_normed * gain
    return rstd * (
        d_hat
        - jnp.mean(d_hat, axis=-1, keepdims=True)
        - xhat * jnp.mean(d_hat * xhat, axis=-1, keepdims=True)
    )


def ffn_back_kernel(
    lens_ref, mid_ref, slope_ref, dout_ref, dhid_ref, gain_ref, up_ref,
    dmid_ref, dattn_ref, dt_ref, grad_ref, dgain_ref, grad, dgain, *, tile_graphs
):
    step, steps = pl.program_id(0), pl.num_programs(0)
    xhat, rstd = normalize(mid_ref[...])
    gain = gain_ref[1:2, :]
    place = lax.broadcasted_iota(jnp.int32, (LEN, 1), 0)
    d_up, d_out = [], []
    for j in range(tile_graphs):
        g = step * tile_graphs + j
        live = place < lens_ref[g]
        rows = slice(j * LEN, (j + 1) * LEN)
        d_hidden = jnp.where(live, dhid_ref[pl.ds(g, 1), :], 0.0)
        d_up.append((slope_ref[rows, :].astype(F32) * d_hidden).astype(BF))
        d_out.append(jnp.where(live, dout_ref[pl.ds(g, 1), :], 0.0))
    d_up, d_out = jnp.concatenate(d_up, axis=0), jnp.concatenate(d_out, axis=0)
    d_normed = nt(d_up, up_ref[...])
    d_mid = d_out + norm_back(d_normed, xhat, rstd, gain)
    dmid_ref[...] = d_mid
    d_attn = d_mid.astype(BF)
    dattn_ref[...] = d_attn
    dt_ref[...] = d_attn.T
    part = tn((xhat * gain).astype(BF), d_up)
    part_gain = jnp.sum((d_normed * xhat).reshape(-1, 8, D), axis=0)

    @pl.when(step == 0)
    def _():
        grad[...] = part
        dgain[...] = part_gain

    @pl.when(step > 0)
    def _():
        grad[...] += part
        dgain[...] += part_gain

    @pl.when(step == steps - 1)
    def _():
        for half in range(2):
            grad_ref[half] = grad[:, half * PACK : (half + 1) * PACK].astype(BF)
        dgain_ref[...] = dgain[...]


def ffn_back(lens, middle, slope, d_out, d_hidden, gains, w_up):
    tokens = middle.shape[0]
    tile_graphs = min(2, tokens // LEN)
    rows = tile_graphs * LEN
    full = lambda a: pl.BlockSpec(a.shape, lambda i: (0,) * a.ndim)
    tile = pl.BlockSpec((rows, D), lambda i: (i, 0))
    return pl.pallas_call(
        functools.partial(ffn_back_kernel, tile_graphs=tile_graphs),
        grid=(tokens // rows,),
        in_specs=[pl.BlockSpec(memory_space=pltpu.SMEM), tile, tile]
        + [full(a) for a in (d_out, d_hidden, gains, w_up)],
        out_specs=[
            tile,
            tile,
            pl.BlockSpec((D, rows), lambda i: (0, i)),
            pl.BlockSpec((2, D, PACK), lambda i: (0, 0, 0)),
            pl.BlockSpec((8, D), lambda i: (0, 0)),
        ],
        out_shape=[
            jax.ShapeDtypeStruct((tokens, D), F32),
            jax.ShapeDtypeStruct((tokens, D), BF),
            jax.ShapeDtypeStruct((D, tokens), BF),
            jax.ShapeDtypeStruct((2, D, PACK), BF),
            jax.ShapeDtypeStruct((8, D), F32),
        ],
        scratch_shapes=[pltpu.VMEM((D, D), F32), pltpu.VMEM((8, D), F32)],
        compiler_params=pltpu.CompilerParams(vmem_limit_bytes=VMEM_LIMIT),
        cost_estimate=pl.CostEstimate(
            flops=10_000_000_000, bytes_accessed=15_000_000, transcendentals=0
        ),
        name="ffn_back",
    )(lens, middle, slope, d_out, d_hidden, gains, w_up)


def loss_kernel(
    where_ref, a1_ref, a3_ref, b1_ref, b3_ref, gain_ref, down_ref,
    loss_ref, dout_ref, dhid_ref, dlow_ref, hid_ref, dgain_ref, xhat, stats, rows_ref
):
    outs, graphs = a1_ref.shape[1], a1_ref.shape[2]
    outer, inner, far, core = (where_ref[i] for i in range(4))
    count = outs * 2 * GRAPHS_DEV
    place = lambda f, o, i, c: pl.multiple_of(
        f * count + (o * 2 + i) * GRAPHS_DEV + c * graphs, graphs
    )
    for owner, refs in ((core, (a1_ref, a3_ref)), (1 - core, (b1_ref, b3_ref))):
        for part, ref in enumerate(refs):
            for at in range(2):
                if part == at:
                    f, i = part, part
                else:
                    f, i = (owner, 1 - owner) if part == 0 else (1 - owner, owner)
                for o in range(outs):
                    values = ref[at, o].astype(F32)
                    row = place(
                        lax.rem(far + f, 2), lax.rem(outer + outs - o, outs), lax.rem(inner + i, 2), owner
                    )
                    rows = pl.ds(row, graphs)
                    xhat[rows, :] = values[:, 0:D] + values[:, D : 2 * D]
                    rows_ref[rows, :] = values[:, 2 * D : 3 * D]
                    stats[rows, :] = values[:, 3 * D :]
    hid_ref[...] = rows_ref[...].astype(BF)
    root = D**-0.5
    left, right = xhat[0:count, :] * gain_ref[2:3, :], xhat[count:, :] * gain_ref[2:3, :]
    exact = lambda a, b, dims: lax.dot_general(
        a, b, (dims, ((), ())), precision=HIGHEST, preferred_element_type=F32
    )
    logits = exact(left, right, ((1,), (1,))) * root
    row_top, col_top = jnp.max(logits, axis=1, keepdims=True), jnp.max(logits, axis=0, keepdims=True)
    row_expo, col_expo = jnp.exp(logits - row_top), jnp.exp(logits - col_top)
    row_sum, col_sum = jnp.sum(row_expo, axis=1, keepdims=True), jnp.sum(col_expo, axis=0, keepdims=True)
    row_id = lax.broadcasted_iota(jnp.int32, (count, count), 0)
    col_id = lax.broadcasted_iota(jnp.int32, (count, count), 1)
    slot = stats[0:count, 4:5].astype(jnp.int32)
    positive = jnp.where(col_id == (row_id & -GRAPHS_DEV) + slot, 1.0, 0.0)
    loss = (
        jnp.sum(row_top + jnp.log(row_sum), axis=0, keepdims=True)
        + jnp.sum(col_top + jnp.log(col_sum), axis=1, keepdims=True)
        - 2.0 * jnp.sum(jnp.sum(positive * logits, axis=1, keepdims=True), axis=0, keepdims=True)
    )
    loss_ref[...] = loss
    d_logits = row_expo / row_sum + col_expo / col_sum - 2.0 * positive
    rows_ref[0:count, :] = exact(d_logits, right, ((1,), (0,))) * root
    rows_ref[count:, :] = exact(d_logits, left, ((0,), (0,))) * root
    every = xhat[...]
    d_summary = rows_ref[...]
    dgain_ref[...] = jnp.sum(d_summary * every, axis=0, keepdims=True)
    rstd, share = stats[:, 0:1] + stats[:, 1:2], stats[:, 2:3] + stats[:, 3:4]
    d_rows = norm_back(d_summary, every, rstd, gain_ref[2:3, :]) * share
    rows_ref[...] = d_rows
    dlow_ref[...] = d_rows.astype(BF)
    own = rows_ref[pl.ds(place(far, outer, inner, core), graphs), :]
    dout_ref[...] = own
    dhid_ref[...] = nn(own.astype(BF), down_ref[...])


def contrast(where, pieces, gains, w_down):
    outs, graphs = pieces[0].shape[1], pieces[0].shape[2]
    total = outs * 4 * GRAPHS_DEV
    return pl.pallas_call(
        loss_kernel,
        in_specs=[pl.BlockSpec(memory_space=pltpu.SMEM)]
        + [pl.BlockSpec(memory_space=pltpu.VMEM)] * 6,
        out_specs=[pl.BlockSpec(memory_space=pltpu.VMEM)] * 6,
        out_shape=[
            jax.ShapeDtypeStruct((1, 1), F32),
            jax.ShapeDtypeStruct((graphs, D), F32),
            jax.ShapeDtypeStruct((graphs, D), F32),
            jax.ShapeDtypeStruct((total, D), BF),
            jax.ShapeDtypeStruct((total, D), BF),
            jax.ShapeDtypeStruct((1, D), F32),
        ],
        scratch_shapes=[
            pltpu.VMEM((total, D), F32),
            pltpu.VMEM((total, 128), F32),
            pltpu.VMEM((total, D), F32),
        ],
        compiler_params=pltpu.CompilerParams(vmem_limit_bytes=24 * 2**20),
        cost_estimate=pl.CostEstimate(
            flops=3_000_000_000, bytes_accessed=4_000_000, transcendentals=0
        ),
        name="contrast",
    )(where, *pieces, gains, w_down)


def contrast_plain(everyone, gains, w_down, own_row, graphs):
    n = everyone.shape[0]
    stats = everyone[..., 3 * D :].astype(F32)
    xhat = everyone[..., :D].astype(F32) + everyone[..., D : 2 * D].astype(F32)
    hidden_sums = everyone[..., 2 * D : 3 * D].reshape(-1, D)
    rstd_pool = (stats[..., 0:1] + stats[..., 1:2]).reshape(-1, 1)
    share = (stats[..., 2:3] + stats[..., 3:4]).reshape(-1, 1)
    summaries = xhat * gains[2]
    left, right = summaries[:, 0].reshape(-1, D), summaries[:, 1].reshape(-1, D)
    root_width = D**0.5
    logits = jnp.dot(left, right.T, precision=HIGHEST) / root_width
    row_totals, col_totals = log_total(logits, 1), log_total(logits, 0)
    count = logits.shape[0]
    group = jnp.arange(count, dtype=jnp.int32) // GRAPHS_DEV
    partners = group * GRAPHS_DEV + stats[:, 0, :, 4].reshape(-1).astype(jnp.int32)
    positive = (partners[:, None] == jnp.arange(count, dtype=jnp.int32)[None, :]).astype(F32)
    total_loss = jnp.sum(row_totals) + jnp.sum(col_totals) - 2.0 * jnp.sum(positive * logits)
    d_logits = (
        jnp.exp(logits - row_totals[:, None])
        + jnp.exp(logits - col_totals[None, :])
        - 2.0 * positive
    )
    d_left = jnp.dot(d_logits, right, precision=HIGHEST) / root_width
    d_right = jnp.dot(d_logits.T, left, precision=HIGHEST) / root_width
    d_summary = jnp.stack(
        [d_left.reshape(n, GRAPHS_DEV, D), d_right.reshape(n, GRAPHS_DEV, D)], axis=1
    ).reshape(-1, D)
    xhat = xhat.reshape(-1, D)
    gain_three = jnp.sum(d_summary * xhat, axis=0, keepdims=True)
    d_rows = norm_back(d_summary, xhat, rstd_pool, gains[2]) * share
    d_out = lax.dynamic_slice_in_dim(d_rows, own_row, graphs, 0)
    d_hidden = nn(d_out.astype(BF), w_down)
    return total_loss, d_out, d_hidden, d_rows.astype(BF), hidden_sums, gain_three


class Place:
    def __init__(self):
        self.n, self.heads = lax.axis_size("dp"), lax.axis_size("head")
        self.outs = self.n // 2
        dp, head = lax.axis_index("dp"), lax.axis_index("head")
        self.dp, self.head = dp, head
        self.outer, self.inner, self.far, self.core = dp // 2, dp % 2, head // 2, head % 2

    def move(self, v, to):
        pairs = []
        for i in range(self.n * self.heads):
            outer, inner, far, core = i // 8, (i // 4) % 2, (i // 2) % 2, i % 2
            outer, inner, far, core = to(outer, inner, far, core)
            pairs.append((i, ((outer % self.outs * 2 + inner) * 2 + far) * 2 + core))
        return lax.ppermute(v, ("dp", "head"), pairs)

    def to_core(self, v):
        return self.move(v, lambda o, i, f, c: (o, i, f, 1 - c))

    def to_outer(self, v, by):
        return self.move(v, lambda o, i, f, c: (o + by, i, f, c))

    def mixed(self, v, turn):
        return self.move(
            v, lambda o, i, f, c: (o, 1 - i, f, c) if c == turn else (o, i, 1 - f, c)
        )

    def by_core(self, a, b):
        return jnp.where(self.core == 0, a, b)

    def gather_outer(self, v):
        out = jnp.zeros((self.outs,) + v.shape, v.dtype)
        out = lax.dynamic_update_index_in_dim(out, v, self.outer, 0)
        for by in range(1, self.outs):
            out = lax.dynamic_update_index_in_dim(
                out, self.to_outer(v, by), (self.outer - by) % self.outs, 0
            )
        return out

    def outer_list(self, v):
        return jnp.stack([v] + [self.to_outer(v, by) for by in range(1, self.outs)])

    def gather_pieces(self, v):
        return self.gather_near(self.gather_outer(v))

    def gather_near(self, own):
        return self.gather_last(own, self.mixed(own, 0))

    def gather_last(self, own, second):
        return self.pieces_of(own, second, self.mixed(jnp.stack([own, second]), 1))

    def pieces_of(self, own, second, third):
        return [
            [own, self.by_core(second, third[0])],
            [self.by_core(third[0], second), third[1]],
        ]

    def whole(self, pieces):
        rows = [
            [jnp.where(self.far == 0, pieces[f][i], pieces[1 - f][i]) for f in range(2)]
            for i in range(2)
        ]
        ordered = [
            [jnp.where(self.inner == 0, rows[i][f], rows[1 - i][f]) for f in range(2)]
            for i in range(2)
        ]
        return jnp.stack([jnp.stack(pair, axis=1) for pair in ordered], axis=1)

    def both_cores(self, v, axis):
        other = self.to_core(v)
        return jnp.stack([self.by_core(v, other), self.by_core(other, v)], axis=axis)

    def both_cores_of(self, own, sent):
        other = self.to_core(sent)
        return jnp.stack([self.by_core(own, other), self.by_core(other, own)])

    def gather_all(self, v):
        v = self.both_cores(self.whole(self.gather_pieces(v)), 3)
        return v.reshape((self.n, self.heads) + v.shape[4:])

    def fold_far(self, pieces):
        sent = jnp.stack([self.by_core(pieces[1][0], pieces[0][1]), pieces[1][1]])
        kept = jnp.stack([pieces[0][0], self.by_core(pieces[0][1], pieces[1][0])])
        return kept, sent

    def fold_near(self, kept, came, dtype):
        total = kept.astype(F32) + came.astype(F32)
        return total[0], total[1].astype(dtype)

    def fold_outer(self, kept, came, dtype):
        total = (kept.astype(F32) + came.astype(F32)).astype(dtype)
        pick = lambda by: lax.dynamic_index_in_dim(
            total, (self.outer + by) % self.outs, 0, keepdims=False
        )
        result = pick(0).astype(F32)
        for by in range(1, self.outs):
            result = result + self.to_outer(pick(by), by).astype(F32)
        return result

    def total(self, v):
        v = v + self.to_core(v)
        v = v + self.move(v, lambda o, i, f, c: (o, i, 1 - f, c))
        v = v + self.move(v, lambda o, i, f, c: (o, 1 - i, f, c))
        by = 1
        while by < self.outs:
            v = v + self.move(v, lambda o, i, f, c, by=by: (o ^ by, i, f, c))
            by *= 2
        return v

    def split_rows(self, v):
        v = v.reshape((self.outs, 2, -1) + v.shape[1:])
        return [
            lax.dynamic_index_in_dim(v, (self.inner + i) % 2, 1, keepdims=False) for i in range(2)
        ]


def tie(*values):
    return lax.optimization_barrier(values)


def log_total(values, axis):
    top = jnp.max(values, axis=axis, keepdims=True)
    return jnp.squeeze(top, axis) + jnp.log(jnp.sum(jnp.exp(values - top), axis=axis))


def identifiers(table, endpoints):
    graphs = endpoints.shape[0] // LEN
    nodes = table.reshape(graphs, NODE, LAP).astype(BF)
    picks = (
        endpoints.reshape(graphs, LEN, 2)[..., None] == jnp.arange(NODE, dtype=jnp.int32)
    ).astype(BF)
    found = jnp.einsum("glan,gnc->glac", picks, nodes, preferred_element_type=F32)
    return found.reshape(graphs * LEN, 2 * LAP).astype(BF)


def stack_pieces(place, near, last):
    pieces = place.pieces_of(near[0], near[1], last)
    packs = []
    for f in range(2):
        for c in range(2):
            rows = [
                jnp.where(place.inner == i, pieces[f][0][:, c], pieces[f][1][:, c]) for i in range(2)
            ]
            packs.append(jnp.stack(rows, axis=1).reshape(D, PACK))
    return jnp.stack(packs)


def split_core(place, grad_up):
    v = grad_up.reshape((2, place.outs, 2, 2, 2, -1, PACK))
    pick = lambda at: lax.dynamic_index_in_dim(v, at, 4, keepdims=False)
    return pick(1 - place.core), pick(place.core)


def fold_pieces(place, own, came, up):
    pieces = []
    for f in range(2):
        total = own[f].astype(F32) + came[f].astype(F32)
        pieces.append([v.astype(BF) for v in place.split_rows(total)])
    if up is None:
        return pieces
    total = (up[0].astype(F32) + up[1].astype(F32)).astype(BF)
    for f in range(2):
        part = lax.dynamic_index_in_dim(total, (place.far + f) % 2, 3, keepdims=False)
        for i in range(2):
            rows = lax.dynamic_index_in_dim(part, (place.inner + i) % 2, 2, keepdims=False)
            pieces[f][i] = jnp.concatenate([pieces[f][i], rows[0], rows[1]], axis=1)
    return pieces


def adam_step(weight, gradient, first, second, factor, rate):
    clipped = gradient * factor
    first_new = BETA_ONE * first + (1.0 - BETA_ONE) * clipped
    second_new = BETA_TWO * second + (1.0 - BETA_TWO) * clipped * clipped
    first_hat = first_new / (1.0 - BETA_ONE**STEPS)
    second_hat = second_new / (1.0 - BETA_TWO**STEPS)
    weight_new = weight - rate * (first_hat / (jnp.sqrt(second_hat) + ADAM_EPS) + DECAY * weight)
    return (weight_new, first_new, second_new)


def per_device(
    features,
    laplacian,
    endpoints,
    lengths,
    pairing,
    ident_weight,
    qkv_weight,
    out_weight,
    ffn_weight,
    norm_gains,
    ident_first,
    qkv_first,
    out_first,
    ffn_first,
    gains_first,
    ident_second,
    qkv_second,
    out_second,
    ffn_second,
    gains_second,
):
    place = Place()
    heads, head, dp, core = place.heads, place.head, place.dp, place.core
    tokens = features.shape[0] // heads
    graphs = tokens // LEN
    own_columns = norm_gains.shape[1]

    small = jnp.concatenate([ident_weight, norm_gains], axis=0)
    small_rows = small.shape[0]

    packed = [qkv_weight[:, 0], qkv_weight[:, 1], qkv_weight[:, 2], out_weight.T]
    shards = jnp.stack(
        [
            jnp.concatenate([m[:, s * SW : (s + 1) * SW] for m in packed], axis=1).astype(BF)
            for s in range(2)
        ]
    )
    pick = lambda v, at: lax.dynamic_index_in_dim(v, at, 0, keepdims=False)
    near = jnp.stack([pick(shards, core), place.to_core(pick(shards, 1 - core))])
    shard_rows = D // place.n
    aligned = shard_rows % 16 == 0
    near, small = tie(near, small.reshape(1, -1))
    near, small = tie((place.outer_list if aligned else place.gather_outer)(near), place.gather_outer(small))
    near, small_near = jnp.stack([near, place.mixed(near, 0)]), place.mixed(small, 0)
    near, small_near, ffn = tie(near, small_near, ffn_weight.astype(BF))
    last = place.mixed(near, 1)
    near_others = place.to_core(near)
    small = place.both_cores(place.whole(place.gather_last(small, small_near)), 3)
    small = small.reshape(-1, small_rows, own_columns).transpose(1, 0, 2).reshape(small_rows, D)
    ident_full, gains = small[: 2 * LAP].astype(BF), small[2 * LAP :]
    ffn_near = place.both_cores_of(pick(ffn, core), pick(ffn, 1 - core))
    ffn_pieces = place.gather_pieces(ffn_near)

    start_row = head * tokens
    lens = lax.dynamic_slice_in_dim(lengths.reshape(-1), head * graphs, graphs, 0)
    partner = lax.dynamic_slice_in_dim(
        jnp.concatenate([pairing.reshape(-1)] * 2), head * graphs, graphs, 0
    )
    table_rows = lax.dynamic_slice_in_dim(laplacian, head * graphs * NODE, graphs * NODE, 0)
    end_rows = lax.dynamic_slice_in_dim(endpoints, start_row, tokens, 0)
    ident_rows = identifiers(table_rows, end_rows)
    embedded = lax.dynamic_slice_in_dim(features, start_row, tokens, 0).astype(F32)
    embedded = embedded + nn(ident_rows, ident_full)
    normed_one = (normalize(embedded)[0] * gains[0]).astype(BF)

    normed_turned = normed_one.T
    last, normed_turned = tie(last, normed_turned)
    last_others = place.to_core(last)
    where = jnp.stack([place.outer, place.inner, core]).astype(jnp.int32)
    where_others = jnp.stack([place.outer, place.inner, 1 - core]).astype(jnp.int32)
    if aligned:
        mine, saved_mine = attend(lens, where, normed_one, [near, last])
    else:
        packs = stack_pieces(place, near, last)
        mine, saved_mine = attend(lens, where, normed_one, [packs])
    ffn_pieces, heads_mine = tie(ffn_pieces, saved_mine[2])
    if aligned:
        others, saved_others = attend(lens, where_others, normed_one, [near_others, last_others])
    else:
        others, saved_others = attend(lens, where_others, normed_one, [place.to_core(packs)])
    ffn_mine = place.whole(ffn_pieces).reshape(D, -1)
    ffn_other = place.to_core(ffn_mine)
    w_up, w_down = place.by_core(ffn_mine, ffn_other), place.by_core(ffn_other, ffn_mine)
    middle, slope, payload = forward_rest(
        lens, partner, embedded, gains, w_up, w_down, [heads_mine, saved_others[2]], [mine, others]
    )

    own_row = (dp * heads + head) * graphs
    if place.n * GRAPHS_DEV <= 128:
        first = place.outer_list(payload)
        first = jnp.stack([first, place.mixed(first, 0)])
        third = place.mixed(first, 1)
        four = jnp.stack([place.outer, place.inner, place.far, core]).astype(jnp.int32)
        total_loss, d_out, d_hidden, d_rows_low, hidden_sums, gain_three = contrast(
            four, [first, third, place.to_core(first), place.to_core(third)], gains, w_down
        )
        total_loss = total_loss[0, 0]
    else:
        everyone = place.gather_all(payload).reshape(place.n, 2, GRAPHS_DEV, -1)
        total_loss, d_out, d_hidden, d_rows_low, hidden_sums, gain_three = contrast_plain(
            everyone, gains, w_down, own_row, graphs
        )

    own_column = (dp * heads + head) * own_columns
    d_columns = lax.dynamic_slice_in_dim(d_rows_low, own_column, own_columns, 1)
    grad_down = tn(d_columns, hidden_sums)
    d_middle, d_attn, d_turned, grad_up, gain_two = ffn_back(
        lens, middle, slope, d_out, d_hidden, gains, w_up
    )
    back = functools.partial(attend_back, normed_turned)
    up_sent, up_kept = split_core(place, grad_up)
    up_came = place.to_core(up_sent)
    grad_others, d_others = back(d_turned, d_attn, others, saved_others, 0, 1, heads)
    came = place.to_core(grad_others)
    d_attn, grad_others = tie(d_attn, grad_others)
    grad_even, d_even = back(d_turned, d_attn, mine, saved_mine, 0, 2, heads // 2)
    even = fold_pieces(place, [grad_even[0], grad_even[1]], [came[0], came[2]], (up_kept, up_came))
    even_kept, even_sent = place.fold_far(even)
    even_sent, d_attn = tie(even_sent, d_attn)
    even_came = place.mixed(even_sent, 1)
    grad_odd, d_odd = back(d_turned, d_attn, mine, saved_mine, 1, 2, 1)
    d_attn, even_came, grad_odd = tie(d_attn, even_came, grad_odd)
    even_kept, even_sent = place.fold_near(even_kept, even_came, BF)
    even_came = place.mixed(even_sent, 0)
    grad_last, d_last = back(d_turned, d_attn, mine, saved_mine, 3, 2, 1)
    grad_last, even_came = tie(grad_last, even_came)
    odd = fold_pieces(place, [grad_odd[0], grad_last[0]], [came[1], came[3]], None)
    odd_kept, odd_sent = place.fold_far(odd)
    odd_sent, d_last = tie(odd_sent, d_last)
    odd_came = place.mixed(odd_sent, 1)
    even = place.fold_outer(even_kept, even_came, BF)
    rows = first_back(
        embedded,
        d_middle,
        ident_rows,
        gains,
        [d_others, d_even, d_odd, d_last],
        ((1, (0, 1, 2, 3)), (0, (0, 2)), (0, (1,)), (0, (3,))),
        [mine, others],
    )
    odd_came, rows, even = tie(odd_came, rows, even)
    odd_kept, odd_sent = place.fold_near(odd_kept, odd_came, BF)
    odd_came = place.mixed(odd_sent, 0)
    odd = place.fold_outer(odd_kept, odd_came, BF)
    gain_rows = jnp.stack([jnp.sum(rows[2 * LAP :], axis=0), jnp.sum(gain_two, axis=0)])
    rows = jnp.concatenate([rows[: 2 * LAP], gain_rows], axis=0)
    row_count = rows.shape[0]
    rows = rows.T.reshape(place.outs, 2, 2, 2, own_columns * row_count)
    rows_kept = lax.dynamic_index_in_dim(rows, core, 3, keepdims=False)
    rows = rows_kept + place.to_core(lax.dynamic_index_in_dim(rows, 1 - core, 3, keepdims=False))
    turn = lambda v, axis, own, at: lax.dynamic_index_in_dim(v, (own + at) % 2, axis, keepdims=False)
    rows = [[turn(turn(rows, 2, place.far, f), 1, place.inner, i) for i in range(2)] for f in range(2)]
    rows_kept, rows_sent = place.fold_far(rows)
    rows_kept, rows_sent = place.fold_near(rows_kept, place.mixed(rows_sent, 1), F32)
    rows = place.fold_outer(rows_kept, place.mixed(rows_sent, 0), F32).reshape(own_columns, row_count).T
    grad_ident = rows[: 2 * LAP]
    grad_gains = jnp.concatenate(
        [rows[2 * LAP :], lax.dynamic_slice_in_dim(gain_three, own_column, own_columns, 1)],
        axis=0,
    )
    own_half, other_half = even[:shard_rows], place.to_core(odd)
    halves = [place.by_core(own_half, other_half), place.by_core(other_half, own_half)]
    columns = lambda j: jnp.concatenate([v[:, j * SW : (j + 1) * SW] for v in halves], axis=1)
    grad_qkv = jnp.stack([columns(0), columns(1), columns(2)], axis=1)
    grad_out = columns(3).T
    grad_up = even[shard_rows:].reshape(2, own_columns, PACK)
    grad_ffn = jnp.stack([jnp.concatenate([grad_up[0], grad_up[1]], axis=1), grad_down])

    grads = (grad_ident, grad_qkv, grad_out, grad_ffn, grad_gains)
    squares = sum((jnp.sum(gradient * gradient) for gradient in grads))
    grad_norm = jnp.sqrt(place.total(squares))
    factor = CLIP_AT / jnp.maximum(grad_norm, CLIP_AT)
    results = [
        adam_step(weight, gradient, first, second, factor, rate)
        for weight, gradient, first, second, rate in zip(
            (ident_weight, qkv_weight, out_weight, ffn_weight, norm_gains),
            grads,
            (ident_first, qkv_first, out_first, ffn_first, gains_first),
            (ident_second, qkv_second, out_second, ffn_second, gains_second),
            STEP_RATES,
        )
    ]
    return (grad_norm, total_loss) + tuple(r[k] for k in range(3) for r in results)


def solution(mesh):
    both = P(None, ("dp", "head"))
    weights = (both, P("dp", None, "head"), P("head", "dp"), P(None, ("dp", "head"), None), both)
    in_specs = (P("dp", None),) * 5 + weights * 3
    out_specs = (P(), P()) + weights * 3
    return jax.shard_map(
        per_device, mesh=mesh, in_specs=in_specs, out_specs=out_specs, check_vma=False
    )
```

```python
import functools

import jax
import jax.numpy as jnp
from jax import lax
from jax.experimental import pallas as pl
from jax.experimental.pallas import tpu as pltpu
from jax.sharding import PartitionSpec as P

D = 768
HEAD_DIM = 24
LAP = 16
LEN = 128
NODE = 32
STEPS = 3
GRAPHS_DEV = 16

HIGHEST = lax.Precision.HIGHEST
NORM_EPS = 1e-05
CLIP_AT = 5.0
STEP_RATES = (0.08, 0.02, 0.15, 0.02, 0.5)
BETA_ONE = 0.5
BETA_TWO = 0.5
DECAY = 0.01
ADAM_EPS = 1e-08
MASKED = -1e30

BF = jnp.bfloat16
F32 = jnp.float32
SUB = 4
SW = SUB * HEAD_DIM
PACK = 4 * SW
V_AT = 128 - SW
SCALE = HEAD_DIM ** (-0.5)
VMEM_LIMIT = 44 * 2**20


def nn(a, b):
    return lax.dot_general(a, b, (((1,), (0,)), ((), ())), preferred_element_type=F32)


def nt(a, b):
    return lax.dot_general(a, b, (((1,), (1,)), ((), ())), preferred_element_type=F32)


def tn(a, b):
    return lax.dot_general(a, b, (((0,), (0,)), ((), ())), preferred_element_type=F32)


def lanes():
    return lax.broadcasted_iota(jnp.int32, (1, 128), 1)


def head_lanes(h, at):
    lane = lanes()
    return (lane >= at + h * HEAD_DIM) & (lane < at + (h + 1) * HEAD_DIM)


def by_head(v, at):
    zero = jnp.zeros_like(v)
    return jnp.concatenate([jnp.where(head_lanes(h, at), v, zero) for h in range(SUB)], axis=0)


def stack_heads(v):
    return jnp.concatenate([v[:, h * LEN : (h + 1) * LEN] for h in range(SUB)], axis=0)


def attend_kernel(lens_ref, where_ref, x_ref, *refs, graphs, whole, turn):
    refs, turned = (refs[:-1], refs[-1:]) if turn else (refs, ())
    if whole:
        w_ref, qkv_ref, p_ref, o_ref, rinv_ref = refs
    else:
        first_ref, third_ref, w_ref, qkv_ref, p_ref, o_ref, rinv_ref = refs
        outs, rows = first_ref.shape[1], first_ref.shape[3]
        far, head = pl.program_id(0) // 2, pl.program_id(0) % 2
        outer, inner, gatherer = where_ref[0], where_ref[1], where_ref[2]
        for i in range(2):
            in_first = (far == 0) if i == 0 else (far == 0) & (gatherer == 0)
            in_first = in_first | ((far == 1) & (gatherer == 1) & (i == 0))
            at = jnp.where(in_first, jnp.where(far + i == 0, 0, 1), jnp.where(far + i == 2, 1, 0))

            def place(source, at=at, i=i):
                for o in range(outs):
                    row = (lax.rem(outer + outs - o, outs) * 2 + (inner + i) % 2) * rows
                    w_ref[0, pl.ds(pl.multiple_of(row, rows), rows), :] = source[at, o, head]

            @pl.when(in_first)
            def _(place=place):
                place(first_ref)

            @pl.when(jnp.logical_not(in_first))
            def _(place=place):
                place(third_ref)

    if turned:

        @pl.when(pl.program_id(0) == 0)
        def _():
            turned[0][...] = x_ref[...].T

    y = nn(x_ref[...], w_ref[0])
    qkv_ref[0, 0] = y[:, :128].astype(BF)
    qkv_ref[0, 1] = pltpu.roll(y, PACK - SW, 1)[:, :128].astype(BF)
    qkv_ref[0, 2] = pltpu.roll(y, SW, 1)[:, 256:].astype(BF)
    col = lanes()
    ones = by_head(jnp.ones((LEN, 128), BF), V_AT)
    for g in range(graphs):
        rows = slice(g * LEN, (g + 1) * LEN)
        query, keys, values = qkv_ref[0, 0, rows, :], qkv_ref[0, 1, rows, :], qkv_ref[0, 2, rows, :]
        live = col < lens_ref[g]
        scores = nt(query, by_head(keys, 0))
        parts = []
        for h in range(SUB):
            own = jnp.where(live, scores[:, h * LEN : (h + 1) * LEN] * SCALE, MASKED)
            parts.append(jnp.exp(own - jnp.max(own, axis=1, keepdims=True)).astype(BF))
        expo = jnp.concatenate(parts, axis=1)
        both = nn(expo, jnp.concatenate([by_head(values, V_AT), ones], axis=1))
        rinv = jnp.where(col >= V_AT, 1.0 / both[:, 128:], 0.0)
        p_ref[0, rows, :] = expo
        rinv_ref[0, rows, :] = rinv
        o_ref[0, rows, :] = jnp.where(col >= V_AT, both[:, :128] * rinv, 0.0).astype(BF)


def attend(lens, where, x, pieces, turn):
    tokens = x.shape[0]
    groups = 4
    whole = len(pieces) == 1
    block = lambda *tail: pl.BlockSpec((1,) + tail, lambda i: (i,) + (0,) * len(tail))
    full = lambda a: pl.BlockSpec(a.shape, lambda i: (0,) * a.ndim)
    out_specs = [block(3, tokens, 128), block(tokens, 512), block(tokens, 128), block(tokens, 128)]
    out_shape = [
        jax.ShapeDtypeStruct((groups, 3, tokens, 128), BF),
        jax.ShapeDtypeStruct((groups, tokens, 512), BF),
        jax.ShapeDtypeStruct((groups, tokens, 128), BF),
        jax.ShapeDtypeStruct((groups, tokens, 128), F32),
    ]
    if not whole:
        out_specs = [block(D, PACK)] + out_specs
        out_shape = [jax.ShapeDtypeStruct((groups, D, PACK), BF)] + out_shape
    if turn:
        out_specs = out_specs + [pl.BlockSpec((D, tokens), lambda i: (0, 0))]
        out_shape = out_shape + [jax.ShapeDtypeStruct((D, tokens), BF)]
    result = pl.pallas_call(
        functools.partial(attend_kernel, graphs=tokens // LEN, whole=whole, turn=turn),
        grid=(groups,),
        in_specs=[pl.BlockSpec(memory_space=pltpu.SMEM)] * 2
        + [full(x)]
        + ([block(D, PACK)] if whole else [full(a) for a in pieces]),
        out_specs=out_specs,
        out_shape=out_shape,
        compiler_params=pltpu.CompilerParams(vmem_limit_bytes=VMEM_LIMIT),
        cost_estimate=pl.CostEstimate(
            flops=groups * 2_500_000_000, bytes_accessed=groups * 3_000_000, transcendentals=0
        ),
        name="attend",
    )(lens, where, x, *pieces)
    return (pieces[0], result) if whole else (result[0], result[1:])


def attend_back_kernel(xt_ref, qkv_ref, p_ref, aug_ref, go_ref, *refs, graphs):
    *more, g_ref, d_ref = refs
    lane = lanes()
    for g in range(graphs):
        rows = slice(g * LEN, (g + 1) * LEN)
        query, keys, values = qkv_ref[0, 0, rows, :], qkv_ref[0, 1, rows, :], qkv_ref[0, 2, rows, :]
        d_rows, expo = aug_ref[0, rows, :], p_ref[0, rows, :]
        one, zero = jnp.ones_like(values), jnp.zeros_like(values)
        spread = jnp.concatenate(
            [
                jnp.where(
                    head_lanes(h, V_AT), values, jnp.where((lane == h) | (lane == SUB + h), one, zero)
                )
                for h in range(SUB)
            ],
            axis=0,
        )
        d_scores = (expo.astype(F32) * nt(d_rows, spread)).astype(BF)
        d_query = nn(d_scores, by_head(keys, 0)) * SCALE
        d_keys = tn(stack_heads(d_scores), by_head(query, 0)) * SCALE
        d_values = tn(stack_heads(expo), by_head(d_rows, V_AT))
        rolled_keys, rolled_values = pltpu.roll(d_keys, SW, 1), pltpu.roll(d_values, V_AT, 1)
        d_ref[0, rows, 0:128] = jnp.where(lane < SW, d_query, rolled_keys).astype(BF)
        d_ref[0, rows, 128:256] = jnp.where(lane < 64, rolled_keys, rolled_values).astype(BF)
        d_ref[0, rows, 256:384] = jnp.where(lane < V_AT, rolled_values, 0.0).astype(BF)
    grad = nn(xt_ref[...], d_ref[0])
    end = jnp.where(lane < V_AT, grad[:, 256:384], go_ref[0].astype(F32))
    if not more:
        g_ref[0, :, 0:256] = grad[:, 0:256].astype(BF)
        g_ref[0, :, 256:384] = end.astype(BF)
        return
    inner_ref, came_ref = more
    outs, size = g_ref.shape[2], g_ref.shape[3]
    for o in range(outs):
        for i in range(2):
            rows = slice((o * 2 + i) * size, (o * 2 + i + 1) * size)
            at = lax.rem(i + inner_ref[0], 2)
            came = came_ref[0, rows, :].astype(F32)
            g_ref[0, at, o, :, 0:256] = (grad[rows, 0:256] + came[:, 0:256]).astype(BF)
            g_ref[0, at, o, :, 256:384] = (end[rows] + came[:, 256:384]).astype(BF)


def attend_back(xt, saved, aug, grad_out, first, stride, groups, more=(), outs=0):
    qkv, expo = saved[:2]
    tokens = xt.shape[1]
    shape = (2, outs, D // (2 * outs), PACK) if more else (D, PACK)
    block = lambda *tail: pl.BlockSpec(
        (1,) + tail, lambda i: (first + i * stride,) + (0,) * len(tail)
    )
    out = lambda *tail: pl.BlockSpec((1,) + tail, lambda i: (i,) + (0,) * len(tail))
    return pl.pallas_call(
        functools.partial(attend_back_kernel, graphs=tokens // LEN),
        grid=(groups,),
        in_specs=[
            pl.BlockSpec(xt.shape, lambda i: (0, 0)),
            block(3, tokens, 128),
            block(tokens, 512),
            block(tokens, 128),
            block(D, 128),
        ]
        + ([pl.BlockSpec(memory_space=pltpu.SMEM), block(D, PACK)] if more else []),
        out_specs=[out(*shape), out(tokens, PACK)],
        out_shape=[
            jax.ShapeDtypeStruct((groups,) + shape, BF),
            jax.ShapeDtypeStruct((groups, tokens, PACK), BF),
        ],
        compiler_params=pltpu.CompilerParams(vmem_limit_bytes=VMEM_LIMIT),
        cost_estimate=pl.CostEstimate(
            flops=groups * 4_000_000_000, bytes_accessed=groups * 3_000_000, transcendentals=0
        ),
        name="attend_back",
    )(xt, qkv, expo, aug, grad_out, *more)


def first_sum_kernel(*refs, parts):
    d_refs, w_refs, out_ref = refs[: len(parts)], refs[len(parts) : -1], refs[-1]
    total = jnp.zeros(out_ref.shape, F32)
    for d_ref, (which, picks) in zip(d_refs, parts):
        for j in range(0, len(picks), 2):
            pair = range(j, min(j + 2, len(picks)))
            left = jnp.concatenate([d_ref[k] for k in pair], axis=1)
            right = jnp.concatenate([w_refs[which][picks[k]] for k in pair], axis=1)
            total = total + nt(left, right)
    out_ref[...] = total


def first_sum(ds, parts, weights):
    tokens = ds[0].shape[1]
    rows = LEN * min(2, tokens // LEN)
    full = lambda a: pl.BlockSpec(a.shape, lambda i: (0,) * a.ndim)
    return pl.pallas_call(
        functools.partial(first_sum_kernel, parts=parts),
        grid=(tokens // rows,),
        in_specs=[pl.BlockSpec((d.shape[0], rows, PACK), lambda i: (0, i, 0)) for d in ds]
        + [full(w) for w in weights],
        out_specs=pl.BlockSpec((rows, D), lambda i: (i, 0)),
        out_shape=jax.ShapeDtypeStruct((tokens, D), F32),
        compiler_params=pltpu.CompilerParams(vmem_limit_bytes=VMEM_LIMIT),
        cost_estimate=pl.CostEstimate(
            flops=7_000_000_000, bytes_accessed=12_000_000, transcendentals=0
        ),
        name="first_sum",
    )(*ds, *weights)


def first_back_kernel(e_ref, dmid_ref, ident_ref, gain_ref, sum_ref, d_ref, w_ref, out_ref, acc):
    step, steps = pl.program_id(0), pl.num_programs(0)
    d_normed = sum_ref[...] + nt(d_ref[0], w_ref[0])
    xhat, rstd = normalize(e_ref[...])
    d_emb = dmid_ref[...] + norm_back(d_normed, xhat, rstd, gain_ref[0:1, :])
    part = tn(ident_ref[...], d_emb.astype(BF))
    part_gain = jnp.sum((d_normed * xhat).reshape(-1, 8, D), axis=0)

    @pl.when(step == 0)
    def _():
        acc[0 : 2 * LAP, :] = part
        acc[2 * LAP :, :] = part_gain

    @pl.when(step > 0)
    def _():
        acc[0 : 2 * LAP, :] += part
        acc[2 * LAP :, :] += part_gain

    @pl.when(step == steps - 1)
    def _():
        out_ref[...] = acc[...]


def first_back(embedded, d_middle, ident_rows, gains, total, d_last, weights):
    tokens = embedded.shape[0]
    rows = LEN * min(2, tokens // LEN)
    last = weights.shape[0] - 1
    full = lambda a: pl.BlockSpec(a.shape, lambda i: (0,) * a.ndim)
    tile = pl.BlockSpec((rows, D), lambda i: (i, 0))
    return pl.pallas_call(
        first_back_kernel,
        grid=(tokens // rows,),
        in_specs=[tile, tile, pl.BlockSpec((rows, 2 * LAP), lambda i: (i, 0)), full(gains), tile]
        + [pl.BlockSpec((1, rows, PACK), lambda i: (0, i, 0))]
        + [pl.BlockSpec((1, D, PACK), lambda i: (last, 0, 0))],
        out_specs=pl.BlockSpec((2 * LAP + 8, D), lambda i: (0, 0)),
        out_shape=jax.ShapeDtypeStruct((2 * LAP + 8, D), F32),
        scratch_shapes=[pltpu.VMEM((2 * LAP + 8, D), F32)],
        compiler_params=pltpu.CompilerParams(vmem_limit_bytes=VMEM_LIMIT),
        cost_estimate=pl.CostEstimate(
            flops=4_000_000_000, bytes_accessed=10_000_000, transcendentals=0
        ),
        name="first_back",
    )(embedded, d_middle, ident_rows, gains, total, d_last, weights)


def normal_parts(x):
    falling = jnp.exp(-0.5 * x * x)
    t = 1.0 / (1.0 + (0.3275911 * 0.5**0.5) * jnp.abs(x))
    tail = 0.5 * 1.061405429
    for c in (-1.453152027, 1.421413741, -0.284496736, 0.254829592):
        tail = tail * t + 0.5 * c
    tail = tail * t * falling
    return jnp.where(x < 0.0, tail, 1.0 - tail), 0.3989422804014327 * falling


def normalize(values):
    centred = values - jnp.mean(values, axis=-1, keepdims=True)
    spread = jnp.mean(centred * centred, axis=-1, keepdims=True)
    rstd = lax.rsqrt(spread + NORM_EPS)
    return centred * rstd, rstd


def two_parts(v):
    high = v.astype(BF)
    return high, (v - high.astype(F32)).astype(BF)


def forward_kernel(
    lens_ref, partner_ref, e_ref, gain_ref, ffn_ref, other_ref, *refs, tile_graphs, waves, groups
):
    o_refs, w_refs = refs[:waves], refs[waves : 2 * waves]
    mid_ref, slope_ref, pay_ref, up_ref, down_ref, hsum, msum = refs[2 * waves :]
    step, steps = pl.program_id(0), pl.num_programs(0)
    core = partner_ref[hsum.shape[0]]

    @pl.when((step == 0) & (core == 0))
    def _():
        up_ref[...] = ffn_ref[...]
        down_ref[...] = other_ref[...]

    @pl.when((step == 0) & (core != 0))
    def _():
        up_ref[...] = other_ref[...]
        down_ref[...] = ffn_ref[...]

    middle = e_ref[...]
    for wave in range(waves):
        left = jnp.concatenate([o_refs[wave][j] for j in range(groups)], axis=1)
        right = jnp.concatenate([w_refs[wave][j][:, 256:] for j in range(groups)], axis=1)
        middle = middle + nt(left, right)
    mid_ref[...] = middle
    xhat, _ = normalize(middle)
    up = nn((xhat * gain_ref[1:2, :]).astype(BF), up_ref[...])
    cdf, density = normal_parts(up)
    hidden = (up * cdf).astype(BF).astype(F32)
    slope_ref[...] = (cdf + up * density).astype(BF)
    place = lax.broadcasted_iota(jnp.int32, (LEN, 1), 0)
    for j in range(tile_graphs):
        g = step * tile_graphs + j
        live = place < lens_ref[g]
        rows = slice(j * LEN, (j + 1) * LEN)
        hsum[pl.ds(g, 1), :] = jnp.sum(jnp.where(live, hidden[rows], 0.0), axis=0, keepdims=True)
        msum[pl.ds(g, 1), :] = jnp.sum(jnp.where(live, middle[rows], 0.0), axis=0, keepdims=True)

    @pl.when(step == steps - 1)
    def _():
        graphs = hsum.shape[0]
        high, low = two_parts(hsum[...])
        which = lax.broadcasted_iota(jnp.int32, (graphs, 1), 0)
        length, partner = jnp.ones((graphs, 1), F32), jnp.zeros((graphs, 1), F32)
        for g in range(graphs):
            length = jnp.where(which == g, lens_ref[g].astype(F32), length)
            partner = jnp.where(which == g, partner_ref[g].astype(F32), partner)
        pooled = (msum[...] + (nt(high, down_ref[...]) + nt(low, down_ref[...]))) / length
        xhat_pool, rstd = normalize(pooled)
        high, low = two_parts(xhat_pool)
        pay_ref[:, 0:D] = high
        pay_ref[:, D : 2 * D] = low
        pay_ref[:, 2 * D : 3 * D] = hsum[...].astype(BF)
        lane = lanes()
        stats = jnp.zeros((graphs, 128), F32)
        for at, value in enumerate(two_parts(rstd) + two_parts(1.0 / length) + (partner,)):
            stats = jnp.where(lane == at, value.astype(F32), stats)
        pay_ref[:, 3 * D :] = stats.astype(BF)


def forward_rest(lens, partner, embedded, gains, w_up, w_down, outs, weights):
    tokens = embedded.shape[0]
    graphs = tokens // LEN
    tile_graphs = min(2, graphs)
    rows = tile_graphs * LEN
    waves, groups = len(outs), outs[0].shape[0]
    full = lambda a: pl.BlockSpec(a.shape, lambda i: (0,) * a.ndim)
    tile = pl.BlockSpec((rows, D), lambda i: (i, 0))
    return pl.pallas_call(
        functools.partial(forward_kernel, tile_graphs=tile_graphs, waves=waves, groups=groups),
        grid=(tokens // rows,),
        in_specs=[pl.BlockSpec(memory_space=pltpu.SMEM)] * 2
        + [tile, full(gains), full(w_up), full(w_down)]
        + [pl.BlockSpec((groups, rows, 128), lambda i: (0, i, 0)) for _ in outs]
        + [full(w) for w in weights],
        out_specs=[
            tile,
            tile,
            pl.BlockSpec((graphs, 3 * D + 128), lambda i: (0, 0)),
            full(w_up),
            full(w_down),
        ],
        out_shape=[
            jax.ShapeDtypeStruct((tokens, D), F32),
            jax.ShapeDtypeStruct((tokens, D), BF),
            jax.ShapeDtypeStruct((graphs, 3 * D + 128), BF),
            jax.ShapeDtypeStruct(w_up.shape, BF),
            jax.ShapeDtypeStruct(w_down.shape, BF),
        ],
        scratch_shapes=[pltpu.VMEM((graphs, D), F32), pltpu.VMEM((graphs, D), F32)],
        compiler_params=pltpu.CompilerParams(vmem_limit_bytes=VMEM_LIMIT),
        cost_estimate=pl.CostEstimate(
            flops=10_000_000_000, bytes_accessed=20_000_000, transcendentals=0
        ),
        name="forward_rest",
    )(lens, partner, embedded, gains, w_up, w_down, *outs, *weights)


def norm_back(d_normed, xhat, rstd, gain):
    d_hat = d_normed * gain
    return rstd * (
        d_hat
        - jnp.mean(d_hat, axis=-1, keepdims=True)
        - xhat * jnp.mean(d_hat * xhat, axis=-1, keepdims=True)
    )


def ffn_back_kernel(
    lens_ref, mid_ref, slope_ref, dout_ref, dhid_ref, gain_ref, up_ref, *refs, tile_graphs, groups
):
    o_refs, rinv_refs, w_refs = refs[0:2], refs[2:4], refs[4:6]
    dmid_ref, grad_ref, dgain_ref = refs[6:9]
    aug_refs, go_refs = refs[9:11], refs[11:13]
    grad, dgain, grad_out = refs[13:]
    step, steps = pl.program_id(0), pl.num_programs(0)
    xhat, rstd = normalize(mid_ref[...])
    gain = gain_ref[1:2, :]
    place = lax.broadcasted_iota(jnp.int32, (LEN, 1), 0)
    d_up, d_out = [], []
    for j in range(tile_graphs):
        g = step * tile_graphs + j
        live = place < lens_ref[g]
        rows = slice(j * LEN, (j + 1) * LEN)
        d_hidden = jnp.where(live, dhid_ref[pl.ds(g, 1), :], 0.0)
        d_up.append((slope_ref[rows, :].astype(F32) * d_hidden).astype(BF))
        d_out.append(jnp.where(live, dout_ref[pl.ds(g, 1), :], 0.0))
    d_up, d_out = jnp.concatenate(d_up, axis=0), jnp.concatenate(d_out, axis=0)
    d_normed = nt(d_up, up_ref[...])
    d_mid = d_out + norm_back(d_normed, xhat, rstd, gain)
    dmid_ref[...] = d_mid
    d_attn = d_mid.astype(BF)
    d_turned = d_attn.T
    part = tn((xhat * gain).astype(BF), d_up)
    part_gain = jnp.sum((d_normed * xhat).reshape(-1, 8, D), axis=0)

    lane = lanes()
    row = lax.broadcasted_iota(jnp.int32, (256, 128), 0) & 127
    column = lax.broadcasted_iota(jnp.int32, (256, 128), 1)
    pick = jnp.zeros((256, 128), BF)
    for h in range(SUB):
        inside = (row >= V_AT + h * HEAD_DIM) & (row < V_AT + (h + 1) * HEAD_DIM)
        pick = jnp.where(inside & ((column == h) | (column == SUB + h)), jnp.ones_like(pick), pick)
    parts_out = []
    for half in range(2):
        d_heads = nn(d_attn, jnp.concatenate([w_refs[half][j] for j in range(groups)], axis=1))
        for j in range(groups):
            d_over = d_heads[:, j * 128 : (j + 1) * 128] * rinv_refs[half][j]
            d_over = jnp.where(lane >= V_AT, d_over, 0.0)
            terms = d_over * o_refs[half][j].astype(F32)
            delta = nn(jnp.concatenate(two_parts(terms), axis=1), pick)
            rounded = delta.astype(BF).astype(F32)
            aug_refs[half][j] = jnp.where(
                lane >= V_AT, d_over, jnp.where(lane < SUB, -rounded, rounded - delta)
            ).astype(BF)
        parts_out.append(
            nn(d_turned, jnp.concatenate([o_refs[half][j] for j in range(groups)], axis=1))
        )

    @pl.when(step == 0)
    def _():
        grad[...] = part
        dgain[...] = part_gain
        for half in range(2):
            grad_out[half] = parts_out[half]

    @pl.when(step > 0)
    def _():
        grad[...] += part
        dgain[...] += part_gain
        for half in range(2):
            grad_out[half] += parts_out[half]

    @pl.when(step == steps - 1)
    def _():
        for half in range(2):
            grad_ref[half] = grad[:, half * PACK : (half + 1) * PACK].astype(BF)
            for j in range(groups):
                go_refs[half][j] = grad_out[half, :, j * 128 : (j + 1) * 128].astype(BF)
        dgain_ref[...] = dgain[...]


def ffn_back(lens, middle, slope, d_out, d_hidden, gains, w_up, outs, rinvs, weights):
    tokens = middle.shape[0]
    tile_graphs = min(2, tokens // LEN)
    rows = tile_graphs * LEN
    groups = outs[0].shape[0]
    full = lambda a: pl.BlockSpec(a.shape, lambda i: (0,) * a.ndim)
    tile = pl.BlockSpec((rows, D), lambda i: (i, 0))
    sub_tile = pl.BlockSpec((groups, rows, 128), lambda i: (0, i, 0))
    result = pl.pallas_call(
        functools.partial(ffn_back_kernel, tile_graphs=tile_graphs, groups=groups),
        grid=(tokens // rows,),
        in_specs=[pl.BlockSpec(memory_space=pltpu.SMEM), tile, tile]
        + [full(a) for a in (d_out, d_hidden, gains, w_up)]
        + [sub_tile] * 4
        + [pl.BlockSpec((groups, D, 128), lambda i: (0, 0, 2))] * 2,
        out_specs=[
            tile,
            pl.BlockSpec((2, D, PACK), lambda i: (0, 0, 0)),
            pl.BlockSpec((8, D), lambda i: (0, 0)),
        ]
        + [sub_tile] * 2
        + [pl.BlockSpec((groups, D, 128), lambda i: (0, 0, 0))] * 2,
        out_shape=[
            jax.ShapeDtypeStruct((tokens, D), F32),
            jax.ShapeDtypeStruct((2, D, PACK), BF),
            jax.ShapeDtypeStruct((8, D), F32),
        ]
        + [jax.ShapeDtypeStruct((groups, tokens, 128), BF)] * 2
        + [jax.ShapeDtypeStruct((groups, D, 128), BF)] * 2,
        scratch_shapes=[
            pltpu.VMEM((D, D), F32),
            pltpu.VMEM((8, D), F32),
            pltpu.VMEM((2, D, groups * 128), F32),
        ],
        compiler_params=pltpu.CompilerParams(vmem_limit_bytes=VMEM_LIMIT),
        cost_estimate=pl.CostEstimate(
            flops=14_000_000_000, bytes_accessed=20_000_000, transcendentals=0
        ),
        name="ffn_back",
    )(lens, middle, slope, d_out, d_hidden, gains, w_up, *outs, *rinvs, *weights)
    return result[:3], result[3:5], result[5:7]


def loss_kernel(
    where_ref, a1_ref, a3_ref, b1_ref, b3_ref, gain_ref, down_ref,
    loss_ref, dout_ref, dhid_ref, dlow_ref, hid_ref, dgain_ref, xhat, stats, rows_ref
):
    outs, graphs = a1_ref.shape[1], a1_ref.shape[2]
    outer, inner, far, core = (where_ref[i] for i in range(4))
    count = outs * 2 * GRAPHS_DEV
    place = lambda f, o, i, c: pl.multiple_of(
        f * count + (o * 2 + i) * GRAPHS_DEV + c * graphs, graphs
    )
    for owner, refs in ((core, (a1_ref, a3_ref)), (1 - core, (b1_ref, b3_ref))):
        for part, ref in enumerate(refs):
            for at in range(2):
                if part == at:
                    f, i = part, part
                else:
                    f, i = (owner, 1 - owner) if part == 0 else (1 - owner, owner)
                for o in range(outs):
                    values = ref[at, o].astype(F32)
                    row = place(
                        lax.rem(far + f, 2), lax.rem(outer + outs - o, outs), lax.rem(inner + i, 2), owner
                    )
                    rows = pl.ds(row, graphs)
                    xhat[rows, :] = values[:, 0:D] + values[:, D : 2 * D]
                    rows_ref[rows, :] = values[:, 2 * D : 3 * D]
                    stats[rows, :] = values[:, 3 * D :]
    hid_ref[...] = rows_ref[...].astype(BF)
    root = D**-0.5
    left, right = xhat[0:count, :] * gain_ref[2:3, :], xhat[count:, :] * gain_ref[2:3, :]
    exact = lambda a, b, dims: lax.dot_general(
        a, b, (dims, ((), ())), precision=HIGHEST, preferred_element_type=F32
    )
    logits = exact(left, right, ((1,), (1,))) * root
    row_top, col_top = jnp.max(logits, axis=1, keepdims=True), jnp.max(logits, axis=0, keepdims=True)
    row_expo, col_expo = jnp.exp(logits - row_top), jnp.exp(logits - col_top)
    row_sum, col_sum = jnp.sum(row_expo, axis=1, keepdims=True), jnp.sum(col_expo, axis=0, keepdims=True)
    row_id = lax.broadcasted_iota(jnp.int32, (count, count), 0)
    col_id = lax.broadcasted_iota(jnp.int32, (count, count), 1)
    slot = stats[0:count, 4:5].astype(jnp.int32)
    positive = jnp.where(col_id == (row_id & -GRAPHS_DEV) + slot, 1.0, 0.0)
    loss = (
        jnp.sum(row_top + jnp.log(row_sum), axis=0, keepdims=True)
        + jnp.sum(col_top + jnp.log(col_sum), axis=1, keepdims=True)
        - 2.0 * jnp.sum(jnp.sum(positive * logits, axis=1, keepdims=True), axis=0, keepdims=True)
    )
    loss_ref[...] = loss
    d_logits = row_expo / row_sum + col_expo / col_sum - 2.0 * positive
    rows_ref[0:count, :] = exact(d_logits, right, ((1,), (0,))) * root
    rows_ref[count:, :] = exact(d_logits, left, ((0,), (0,))) * root
    every = xhat[...]
    d_summary = rows_ref[...]
    dgain_ref[...] = jnp.sum(d_summary * every, axis=0, keepdims=True)
    rstd, share = stats[:, 0:1] + stats[:, 1:2], stats[:, 2:3] + stats[:, 3:4]
    d_rows = norm_back(d_summary, every, rstd, gain_ref[2:3, :]) * share
    rows_ref[...] = d_rows
    dlow_ref[...] = d_rows.astype(BF)
    own = rows_ref[pl.ds(place(far, outer, inner, core), graphs), :]
    dout_ref[...] = own
    dhid_ref[...] = nn(own.astype(BF), down_ref[...])


def contrast(where, pieces, gains, w_down):
    outs, graphs = pieces[0].shape[1], pieces[0].shape[2]
    total = outs * 4 * GRAPHS_DEV
    return pl.pallas_call(
        loss_kernel,
        in_specs=[pl.BlockSpec(memory_space=pltpu.SMEM)]
        + [pl.BlockSpec(memory_space=pltpu.VMEM)] * 6,
        out_specs=[pl.BlockSpec(memory_space=pltpu.VMEM)] * 6,
        out_shape=[
            jax.ShapeDtypeStruct((1, 1), F32),
            jax.ShapeDtypeStruct((graphs, D), F32),
            jax.ShapeDtypeStruct((graphs, D), F32),
            jax.ShapeDtypeStruct((total, D), BF),
            jax.ShapeDtypeStruct((total, D), BF),
            jax.ShapeDtypeStruct((1, D), F32),
        ],
        scratch_shapes=[
            pltpu.VMEM((total, D), F32),
            pltpu.VMEM((total, 128), F32),
            pltpu.VMEM((total, D), F32),
        ],
        compiler_params=pltpu.CompilerParams(vmem_limit_bytes=24 * 2**20),
        cost_estimate=pl.CostEstimate(
            flops=3_000_000_000, bytes_accessed=4_000_000, transcendentals=0
        ),
        name="contrast",
    )(where, *pieces, gains, w_down)


def contrast_plain(everyone, gains, w_down, own_row, graphs):
    n = everyone.shape[0]
    stats = everyone[..., 3 * D :].astype(F32)
    xhat = everyone[..., :D].astype(F32) + everyone[..., D : 2 * D].astype(F32)
    hidden_sums = everyone[..., 2 * D : 3 * D].reshape(-1, D)
    rstd_pool = (stats[..., 0:1] + stats[..., 1:2]).reshape(-1, 1)
    share = (stats[..., 2:3] + stats[..., 3:4]).reshape(-1, 1)
    summaries = xhat * gains[2]
    left, right = summaries[:, 0].reshape(-1, D), summaries[:, 1].reshape(-1, D)
    root_width = D**0.5
    logits = jnp.dot(left, right.T, precision=HIGHEST) / root_width
    row_totals, col_totals = log_total(logits, 1), log_total(logits, 0)
    count = logits.shape[0]
    group = jnp.arange(count, dtype=jnp.int32) // GRAPHS_DEV
    partners = group * GRAPHS_DEV + stats[:, 0, :, 4].reshape(-1).astype(jnp.int32)
    positive = (partners[:, None] == jnp.arange(count, dtype=jnp.int32)[None, :]).astype(F32)
    total_loss = jnp.sum(row_totals) + jnp.sum(col_totals) - 2.0 * jnp.sum(positive * logits)
    d_logits = (
        jnp.exp(logits - row_totals[:, None])
        + jnp.exp(logits - col_totals[None, :])
        - 2.0 * positive
    )
    d_left = jnp.dot(d_logits, right, precision=HIGHEST) / root_width
    d_right = jnp.dot(d_logits.T, left, precision=HIGHEST) / root_width
    d_summary = jnp.stack(
        [d_left.reshape(n, GRAPHS_DEV, D), d_right.reshape(n, GRAPHS_DEV, D)], axis=1
    ).reshape(-1, D)
    xhat = xhat.reshape(-1, D)
    gain_three = jnp.sum(d_summary * xhat, axis=0, keepdims=True)
    d_rows = norm_back(d_summary, xhat, rstd_pool, gains[2]) * share
    d_out = lax.dynamic_slice_in_dim(d_rows, own_row, graphs, 0)
    d_hidden = nn(d_out.astype(BF), w_down)
    return total_loss, d_out, d_hidden, d_rows.astype(BF), hidden_sums, gain_three


class Place:
    def __init__(self):
        self.n, self.heads = lax.axis_size("dp"), lax.axis_size("head")
        self.outs = self.n // 2
        dp, head = lax.axis_index("dp"), lax.axis_index("head")
        self.dp, self.head = dp, head
        self.outer, self.inner, self.far, self.core = dp // 2, dp % 2, head // 2, head % 2

    def move(self, v, to):
        pairs = []
        for i in range(self.n * self.heads):
            outer, inner, far, core = i // 8, (i // 4) % 2, (i // 2) % 2, i % 2
            outer, inner, far, core = to(outer, inner, far, core)
            pairs.append((i, ((outer % self.outs * 2 + inner) * 2 + far) * 2 + core))
        return lax.ppermute(v, ("dp", "head"), pairs)

    def to_core(self, v):
        return self.move(v, lambda o, i, f, c: (o, i, f, 1 - c))

    def to_outer(self, v, by):
        return self.move(v, lambda o, i, f, c: (o + by, i, f, c))

    def mixed(self, v, turn):
        return self.move(
            v, lambda o, i, f, c: (o, 1 - i, f, c) if c == turn else (o, i, 1 - f, c)
        )

    def by_core(self, a, b):
        return jnp.where(self.core == 0, a, b)

    def gather_outer(self, v):
        out = jnp.zeros((self.outs,) + v.shape, v.dtype)
        out = lax.dynamic_update_index_in_dim(out, v, self.outer, 0)
        for by in range(1, self.outs):
            out = lax.dynamic_update_index_in_dim(
                out, self.to_outer(v, by), (self.outer - by) % self.outs, 0
            )
        return out

    def outer_list(self, v):
        return jnp.stack([v] + [self.to_outer(v, by) for by in range(1, self.outs)])

    def gather_pieces(self, v):
        return self.gather_near(self.gather_outer(v))

    def gather_near(self, own):
        return self.gather_last(own, self.mixed(own, 0))

    def gather_last(self, own, second):
        return self.pieces_of(own, second, self.mixed(jnp.stack([own, second]), 1))

    def pieces_of(self, own, second, third):
        return [
            [own, self.by_core(second, third[0])],
            [self.by_core(third[0], second), third[1]],
        ]

    def whole(self, pieces):
        rows = [
            [jnp.where(self.far == 0, pieces[f][i], pieces[1 - f][i]) for f in range(2)]
            for i in range(2)
        ]
        ordered = [
            [jnp.where(self.inner == 0, rows[i][f], rows[1 - i][f]) for f in range(2)]
            for i in range(2)
        ]
        return jnp.stack([jnp.stack(pair, axis=1) for pair in ordered], axis=1)

    def both_cores(self, v, axis):
        other = self.to_core(v)
        return jnp.stack([self.by_core(v, other), self.by_core(other, v)], axis=axis)

    def both_cores_of(self, own, sent):
        other = self.to_core(sent)
        return jnp.stack([self.by_core(own, other), self.by_core(other, own)])

    def gather_all(self, v):
        v = self.both_cores(self.whole(self.gather_pieces(v)), 3)
        return v.reshape((self.n, self.heads) + v.shape[4:])

    def fold_far(self, pieces):
        sent = jnp.stack([self.by_core(pieces[1][0], pieces[0][1]), pieces[1][1]])
        kept = jnp.stack([pieces[0][0], self.by_core(pieces[0][1], pieces[1][0])])
        return kept, sent

    def fold_near(self, kept, came, dtype):
        total = kept.astype(F32) + came.astype(F32)
        return total[0], total[1].astype(dtype)

    def fold_outer(self, kept, came, dtype):
        total = (kept.astype(F32) + came.astype(F32)).astype(dtype)
        pick = lambda by: lax.dynamic_index_in_dim(
            total, (self.outer + by) % self.outs, 0, keepdims=False
        )
        result = pick(0).astype(F32)
        for by in range(1, self.outs):
            result = result + self.to_outer(pick(by), by).astype(F32)
        return result

    def total(self, v):
        v = jnp.broadcast_to(v, (self.n * self.heads, 128))
        return jnp.sum(lax.all_to_all(v, ("dp", "head"), 0, 0, tiled=True)[:, 0])

    def split_rows(self, v):
        v = v.reshape((self.outs, 2, -1) + v.shape[1:])
        return [
            lax.dynamic_index_in_dim(v, (self.inner + i) % 2, 1, keepdims=False) for i in range(2)
        ]


def tie(*values):
    return lax.optimization_barrier(values)


def after(value, *others):
    return lax.optimization_barrier((value,) + others)[0]


def log_total(values, axis):
    top = jnp.max(values, axis=axis, keepdims=True)
    return jnp.squeeze(top, axis) + jnp.log(jnp.sum(jnp.exp(values - top), axis=axis))


def identifiers(table, endpoints):
    graphs = endpoints.shape[0] // LEN
    nodes = table.reshape(graphs, NODE, LAP).astype(BF)
    picks = (
        endpoints.reshape(graphs, LEN, 2)[..., None] == jnp.arange(NODE, dtype=jnp.int32)
    ).astype(BF)
    found = jnp.einsum("glan,gnc->glac", picks, nodes, preferred_element_type=F32)
    return found.reshape(graphs * LEN, 2 * LAP).astype(BF)


def stack_pieces(place, near, last):
    pieces = place.pieces_of(near[0], near[1], last)
    packs = []
    for f in range(2):
        for c in range(2):
            rows = [
                jnp.where(place.inner == i, pieces[f][0][:, c], pieces[f][1][:, c]) for i in range(2)
            ]
            packs.append(jnp.stack(rows, axis=1).reshape(D, PACK))
    return jnp.stack(packs)


def split_core(place, grad_up):
    v = grad_up.reshape((2, place.outs, 2, 2, 2, -1, PACK))
    pick = lambda at: lax.dynamic_index_in_dim(v, at, 4, keepdims=False)
    return pick(1 - place.core), pick(place.core)


def fold_pieces(place, own, came, up):
    pieces = []
    for f in range(2):
        total = own[f].astype(F32) + came[f].astype(F32)
        pieces.append([v.astype(BF) for v in place.split_rows(total)])
    if up is None:
        return pieces
    total = (up[0].astype(F32) + up[1].astype(F32)).astype(BF)
    for f in range(2):
        part = lax.dynamic_index_in_dim(total, (place.far + f) % 2, 3, keepdims=False)
        for i in range(2):
            rows = lax.dynamic_index_in_dim(part, (place.inner + i) % 2, 2, keepdims=False)
            pieces[f][i] = jnp.concatenate([pieces[f][i], rows[0], rows[1]], axis=1)
    return pieces


def squares_kernel(*refs):
    *grad_refs, out_ref = refs
    total = jnp.zeros((1, 1), F32)
    for ref in grad_refs:
        v = ref[...]
        total = total + jnp.sum(jnp.sum(v * v, axis=0, keepdims=True), axis=1, keepdims=True)
    out_ref[...] = jnp.broadcast_to(total, out_ref.shape)


def squares(grads, devices):
    return pl.pallas_call(
        squares_kernel,
        out_shape=jax.ShapeDtypeStruct((devices, 128), F32),
        cost_estimate=pl.CostEstimate(flops=1_000_000, bytes_accessed=500_000, transcendentals=0),
        name="squares",
    )(*grads)


def update_kernel(parts_ref, *refs):
    count = len(STEP_RATES)
    grads, weights, firsts, seconds = (refs[k * count : (k + 1) * count] for k in range(4))
    norm_ref, refs = refs[4 * count], refs[4 * count + 1 :]
    new_weights, new_firsts, new_seconds = (refs[k * count : (k + 1) * count] for k in range(3))
    norm = jnp.sqrt(jnp.sum(parts_ref[...], axis=0, keepdims=True)[:, 0:1])
    norm_ref[...] = norm
    factor = CLIP_AT / jnp.maximum(norm, CLIP_AT)
    for k, rate in enumerate(STEP_RATES):
        for at in range(grads[k].shape[0]) if len(grads[k].shape) == 3 else (...,):
            weight = weights[k][at]
            clipped = grads[k][at] * factor
            first = BETA_ONE * firsts[k][at] + (1.0 - BETA_ONE) * clipped
            second = BETA_TWO * seconds[k][at] + (1.0 - BETA_TWO) * clipped * clipped
            first_hat = first / (1.0 - BETA_ONE**STEPS)
            second_hat = second / (1.0 - BETA_TWO**STEPS)
            new_weights[k][at] = weight - rate * (
                first_hat / (jnp.sqrt(second_hat) + ADAM_EPS) + DECAY * weight
            )
            new_firsts[k][at] = first
            new_seconds[k][at] = second


def update(norm_parts, grads, state):
    result = pl.pallas_call(
        update_kernel,
        out_shape=[jax.ShapeDtypeStruct((1, 1), F32)]
        + [jax.ShapeDtypeStruct(v.shape, F32) for kind in state for v in kind],
        cost_estimate=pl.CostEstimate(
            flops=5_000_000, bytes_accessed=6_000_000, transcendentals=0
        ),
        name="update",
    )(norm_parts, *grads, *(v for kind in state for v in kind))
    count = len(grads)
    return result[0], [result[1 + k * count : 1 + (k + 1) * count] for k in range(3)]


def per_device(
    features,
    laplacian,
    endpoints,
    lengths,
    pairing,
    ident_weight,
    qkv_weight,
    out_weight,
    ffn_weight,
    norm_gains,
    ident_first,
    qkv_first,
    out_first,
    ffn_first,
    gains_first,
    ident_second,
    qkv_second,
    out_second,
    ffn_second,
    gains_second,
):
    place = Place()
    heads, head, dp, core = place.heads, place.head, place.dp, place.core
    tokens = features.shape[0] // heads
    graphs = tokens // LEN
    own_columns = norm_gains.shape[1]

    small = jnp.concatenate([ident_weight, norm_gains], axis=0)
    small_rows = small.shape[0]

    packed = [qkv_weight[:, 0], qkv_weight[:, 1], qkv_weight[:, 2], out_weight.T]
    shards = jnp.stack(
        [
            jnp.concatenate([m[:, s * SW : (s + 1) * SW] for m in packed], axis=1).astype(BF)
            for s in range(2)
        ]
    )
    pick = lambda v, at: lax.dynamic_index_in_dim(v, at, 0, keepdims=False)
    near = jnp.stack([pick(shards, core), place.to_core(pick(shards, 1 - core))])
    shard_rows = D // place.n
    aligned = shard_rows % 16 == 0
    devices = place.n * heads
    small = jnp.broadcast_to(after(small.reshape(1, -1), near), (devices, small.size))
    small = lax.all_to_all(small, ("dp", "head"), 0, 0, tiled=True)
    near_own = (place.outer_list if aligned else place.gather_outer)(near)
    ffn = after(ffn_weight.astype(BF), near_own)
    ffn_near = place.both_cores_of(pick(ffn, core), pick(ffn, 1 - core))
    ffn_own = place.gather_outer(ffn_near)
    near = jnp.stack([near_own, place.mixed(near_own, 0)])
    last = place.mixed(near, 1)
    near_others = place.to_core(near)
    ffn_own = after(ffn_own, near)
    ffn_near = jnp.stack([ffn_own, place.mixed(ffn_own, 0)])
    ffn_last = place.mixed(ffn_near, 1)
    small = small.reshape(-1, small_rows, own_columns).transpose(1, 0, 2).reshape(small_rows, D)
    ident_full, gains = small[: 2 * LAP].astype(BF), small[2 * LAP :]
    start_row = head * tokens
    lens = lax.dynamic_slice_in_dim(lengths.reshape(-1), head * graphs, graphs, 0)
    partner = lax.dynamic_slice_in_dim(
        jnp.concatenate([pairing.reshape(-1)] * 2), head * graphs, graphs, 0
    )
    table_rows = lax.dynamic_slice_in_dim(laplacian, head * graphs * NODE, graphs * NODE, 0)
    end_rows = lax.dynamic_slice_in_dim(endpoints, start_row, tokens, 0)
    ident_rows = identifiers(table_rows, end_rows)
    embedded = lax.dynamic_slice_in_dim(features, start_row, tokens, 0).astype(F32)
    embedded = embedded + nn(ident_rows, ident_full)
    normed_one = (normalize(embedded)[0] * gains[0]).astype(BF)

    last_others = place.to_core(last)
    where = jnp.stack([place.outer, place.inner, core]).astype(jnp.int32)
    where_others = jnp.stack([place.outer, place.inner, 1 - core]).astype(jnp.int32)
    if aligned:
        mine, saved_mine = attend(lens, where, normed_one, [near, last], True)
    else:
        packs = stack_pieces(place, near, last)
        mine, saved_mine = attend(lens, where, normed_one, [packs], True)
    normed_turned = saved_mine[4]
    heads_mine = saved_mine[2]
    ffn_pieces = place.pieces_of(ffn_near[0], ffn_near[1], after(ffn_last, heads_mine))
    if aligned:
        others, saved_others = attend(lens, where_others, normed_one, [near_others, last_others], False)
    else:
        others, saved_others = attend(lens, where_others, normed_one, [place.to_core(packs)], False)
    ffn_mine = place.whole(ffn_pieces).reshape(D, -1)
    ffn_other = place.to_core(ffn_mine)
    middle, slope, payload, w_up, w_down = forward_rest(
        lens,
        jnp.concatenate([partner, core[None].astype(jnp.int32)]),
        embedded,
        gains,
        ffn_mine,
        ffn_other,
        [heads_mine, saved_others[2]],
        [mine, others],
    )

    own_row = (dp * heads + head) * graphs
    if place.n * GRAPHS_DEV <= 128:
        first = place.outer_list(payload)
        first = jnp.stack([first, place.mixed(first, 0)])
        third = place.mixed(first, 1)
        four = jnp.stack([place.outer, place.inner, place.far, core]).astype(jnp.int32)
        total_loss, d_out, d_hidden, d_rows_low, hidden_sums, gain_three = contrast(
            four, [first, third, place.to_core(first), place.to_core(third)], gains, w_down
        )
        total_loss = total_loss[0, 0]
    else:
        everyone = place.gather_all(payload).reshape(place.n, 2, GRAPHS_DEV, -1)
        total_loss, d_out, d_hidden, d_rows_low, hidden_sums, gain_three = contrast_plain(
            everyone, gains, w_down, own_row, graphs
        )

    own_column = (dp * heads + head) * own_columns
    d_columns = lax.dynamic_slice_in_dim(d_rows_low, own_column, own_columns, 1)
    grad_down = tn(d_columns, hidden_sums)
    (d_middle, grad_up, gain_two), augs, grad_outs = ffn_back(
        lens,
        middle,
        slope,
        d_out,
        d_hidden,
        gains,
        w_up,
        [saved_mine[2], saved_others[2]],
        [saved_mine[3], saved_others[3]],
        [mine, others],
    )
    up_sent, up_kept = split_core(place, grad_up)
    up_came = place.to_core(up_sent)
    grad_others, d_others = attend_back(
        normed_turned, saved_others, augs[1], grad_outs[1], 0, 1, heads
    )
    came = place.to_core(grad_others)
    back = functools.partial(attend_back, normed_turned, saved_mine)
    aug = after(augs[0], grad_others)
    grad_even, d_even = back(aug, grad_outs[0], 0, 2, heads // 2)
    even = fold_pieces(place, [grad_even[0], grad_even[1]], [came[0], came[2]], (up_kept, up_came))
    even_kept, even_sent = place.fold_far(even)
    even_came = place.mixed(even_sent, 1)
    more = ([place.inner[None].astype(jnp.int32), came], place.outs) if aligned else ()
    grad_odd, d_odd = back(after(aug, even_sent), grad_outs[0], 1, 2, 1, *more)
    even_kept, even_sent = place.fold_near(even_kept, after(even_came, grad_odd), BF)
    even_came = place.mixed(even_sent, 0)
    grad_last, d_last = back(after(aug, even_sent), grad_outs[0], 3, 2, 1, *more)
    if aligned:
        odd = [[v[0, 0], v[0, 1]] for v in (grad_odd, grad_last)]
    else:
        odd = fold_pieces(place, [grad_odd[0], grad_last[0]], [came[1], came[3]], None)
    odd_kept, odd_sent = place.fold_far(odd)
    odd_came = place.mixed(odd_sent, 1)
    d_normed = first_sum(
        [after(d_others, odd_sent), d_even, d_odd],
        ((1, (0, 1, 2, 3)), (0, (0, 2)), (0, (1,))),
        [mine, others],
    )
    rows = first_back(
        embedded, d_middle, ident_rows, gains, d_normed, after(d_last, odd_came, even_came), mine
    )
    odd_kept, odd_sent = place.fold_near(odd_kept, odd_came, BF)
    odd_came = place.mixed(odd_sent, 0)
    rows = after(rows, odd_came)
    even = place.fold_outer(even_kept, after(even_came, odd_sent), BF)
    odd = place.fold_outer(odd_kept, after(odd_came, even), BF)
    gain_rows = jnp.stack([jnp.sum(rows[2 * LAP :], axis=0), jnp.sum(gain_two, axis=0)])
    rows = jnp.concatenate([rows[: 2 * LAP], gain_rows], axis=0)
    row_count = rows.shape[0]
    rows = rows.T.reshape(devices, own_columns * row_count)
    rows = jnp.sum(lax.all_to_all(rows, ("dp", "head"), 0, 0, tiled=True), axis=0)
    rows = rows.reshape(own_columns, row_count)
    own_gains = lax.dynamic_slice_in_dim(gain_three, own_column, own_columns, 1)
    norm_parts = lax.all_to_all(
        squares([even, odd, grad_down, rows, own_gains], devices),
        ("dp", "head"),
        0,
        0,
        tiled=True,
    )
    own_half, other_half = even[:shard_rows], place.to_core(odd)
    halves = [place.by_core(own_half, other_half), place.by_core(other_half, own_half)]
    columns = lambda j: jnp.concatenate([v[:, j * SW : (j + 1) * SW] for v in halves], axis=1)
    grad_up = even[shard_rows:].reshape(2, own_columns, PACK)
    grads = (
        rows[:, : 2 * LAP],
        jnp.stack([columns(0), columns(1), columns(2)]),
        columns(3).T,
        jnp.stack([jnp.concatenate([grad_up[0], grad_up[1]], axis=1), grad_down]),
        jnp.concatenate([rows[:, 2 * LAP :].T, own_gains], axis=0),
    )
    turns = (lambda v: v.T, lambda v: v.transpose(1, 0, 2)) + (lambda v: v,) * 3
    state = [
        [turn(v) for turn, v in zip(turns, kind)]
        for kind in (
            (ident_weight, qkv_weight, out_weight, ffn_weight, norm_gains),
            (ident_first, qkv_first, out_first, ffn_first, gains_first),
            (ident_second, qkv_second, out_second, ffn_second, gains_second),
        )
    ]
    grad_norm, results = update(norm_parts, grads, state)
    return (grad_norm[0, 0], total_loss) + tuple(
        turn(v) for kind in results for turn, v in zip(turns, kind)
    )


def solution(mesh):
    both = P(None, ("dp", "head"))
    weights = (both, P("dp", None, "head"), P("head", "dp"), P(None, ("dp", "head"), None), both)
    in_specs = (P("dp", None),) * 5 + weights * 3
    out_specs = (P(), P()) + weights * 3
    return jax.shard_map(
        per_device, mesh=mesh, in_specs=in_specs, out_specs=out_specs, check_vma=False
    )
```

```python
import functools

import jax
import jax.numpy as jnp
from jax import lax
from jax.experimental import pallas as pl
from jax.experimental.pallas import tpu as pltpu
from jax.sharding import PartitionSpec as P

D = 768
HEAD_DIM = 24
LAP = 16
LEN = 128
NODE = 32
STEPS = 3
GRAPHS_DEV = 16
GAIN = 2 * LAP

HIGHEST = lax.Precision.HIGHEST
NORM_EPS = 1e-05
CLIP_AT = 5.0
STEP_RATES = (0.08, 0.02, 0.15, 0.02, 0.5)
BETA_ONE = 0.5
BETA_TWO = 0.5
DECAY = 0.01
ADAM_EPS = 1e-08
MASKED = -1e30

BF = jnp.bfloat16
F32 = jnp.float32
SUB = 4
SW = SUB * HEAD_DIM
PACK = 4 * SW
V_AT = 128 - SW
SCALE = HEAD_DIM ** (-0.5)
LENS = 5
VMEM_LIMIT = 52 * 2**20


def nn(a, b):
    return lax.dot_general(a, b, (((1,), (0,)), ((), ())), preferred_element_type=F32)


def nt(a, b):
    return lax.dot_general(a, b, (((1,), (1,)), ((), ())), preferred_element_type=F32)


def tn(a, b):
    return lax.dot_general(a, b, (((0,), (0,)), ((), ())), preferred_element_type=F32)


def lanes():
    return lax.broadcasted_iota(jnp.int32, (1, 128), 1)


def head_lanes(h, at):
    lane = lanes()
    return (lane >= at + h * HEAD_DIM) & (lane < at + (h + 1) * HEAD_DIM)


def by_head(v, at):
    zero = jnp.zeros_like(v)
    return jnp.concatenate([jnp.where(head_lanes(h, at), v, zero) for h in range(SUB)], axis=0)


def stack_heads(v):
    return jnp.concatenate([v[:, h * LEN : (h + 1) * LEN] for h in range(SUB)], axis=0)


def attend_kernel(info_ref, x_ref, *refs, graphs, whole, turn, owner):
    refs, turned = (refs[:-1], refs[-1:]) if turn else (refs, ())
    if whole:
        w_ref, qkv_ref, p_ref, o_ref, rinv_ref = refs
    else:
        first_ref, third_ref, w_ref, qkv_ref, p_ref, o_ref, rinv_ref = refs
        outs, rows = first_ref.shape[1], first_ref.shape[3]
        far, head = pl.program_id(0) // 2, pl.program_id(0) % 2
        outer, inner, gatherer = info_ref[0], info_ref[1], info_ref[owner]
        for i in range(2):
            in_first = (far == 0) if i == 0 else (far == 0) & (gatherer == 0)
            in_first = in_first | ((far == 1) & (gatherer == 1) & (i == 0))
            at = jnp.where(in_first, jnp.where(far + i == 0, 0, 1), jnp.where(far + i == 2, 1, 0))

            def place(source, at=at, i=i):
                for o in range(outs):
                    row = (lax.rem(outer + outs - o, outs) * 2 + (inner + i) % 2) * rows
                    w_ref[0, pl.ds(pl.multiple_of(row, rows), rows), :] = source[at, o, head]

            @pl.when(in_first)
            def _(place=place):
                place(first_ref)

            @pl.when(jnp.logical_not(in_first))
            def _(place=place):
                place(third_ref)

    if turned:

        @pl.when(pl.program_id(0) == 0)
        def _():
            turned[0][...] = x_ref[...].T

    y = nn(x_ref[...], w_ref[0])
    qkv_ref[0, 0] = y[:, :128].astype(BF)
    qkv_ref[0, 1] = pltpu.roll(y, PACK - SW, 1)[:, :128].astype(BF)
    qkv_ref[0, 2] = pltpu.roll(y, SW, 1)[:, 256:].astype(BF)
    col = lanes()
    ones = by_head(jnp.ones((LEN, 128), BF), V_AT)
    for g in range(graphs):
        rows = slice(g * LEN, (g + 1) * LEN)
        query, keys, values = qkv_ref[0, 0, rows, :], qkv_ref[0, 1, rows, :], qkv_ref[0, 2, rows, :]
        live = col < info_ref[LENS + g]
        scores = nt(query, by_head(keys, 0))
        parts = []
        for h in range(SUB):
            own = jnp.where(live, scores[:, h * LEN : (h + 1) * LEN] * SCALE, MASKED)
            parts.append(jnp.exp(own - jnp.max(own, axis=1, keepdims=True)).astype(BF))
        expo = jnp.concatenate(parts, axis=1)
        both = nn(expo, jnp.concatenate([by_head(values, V_AT), ones], axis=1))
        rinv = jnp.where(col >= V_AT, 1.0 / both[:, 128:], 0.0)
        p_ref[0, rows, :] = expo
        rinv_ref[0, rows, :] = rinv
        o_ref[0, rows, :] = jnp.where(col >= V_AT, both[:, :128] * rinv, 0.0).astype(BF)


def attend(info, owner, x, pieces, turn):
    tokens = x.shape[0]
    groups = 4
    whole = len(pieces) == 1
    block = lambda *tail: pl.BlockSpec((1,) + tail, lambda i: (i,) + (0,) * len(tail))
    full = lambda a: pl.BlockSpec(a.shape, lambda i: (0,) * a.ndim)
    out_specs = [block(3, tokens, 128), block(tokens, 512), block(tokens, 128), block(tokens, 128)]
    out_shape = [
        jax.ShapeDtypeStruct((groups, 3, tokens, 128), BF),
        jax.ShapeDtypeStruct((groups, tokens, 512), BF),
        jax.ShapeDtypeStruct((groups, tokens, 128), BF),
        jax.ShapeDtypeStruct((groups, tokens, 128), F32),
    ]
    if not whole:
        out_specs = [block(D, PACK)] + out_specs
        out_shape = [jax.ShapeDtypeStruct((groups, D, PACK), BF)] + out_shape
    if turn:
        out_specs = out_specs + [pl.BlockSpec((D, tokens), lambda i: (0, 0))]
        out_shape = out_shape + [jax.ShapeDtypeStruct((D, tokens), BF)]
    result = pl.pallas_call(
        functools.partial(attend_kernel, graphs=tokens // LEN, whole=whole, turn=turn, owner=owner),
        grid=(groups,),
        in_specs=[pl.BlockSpec(memory_space=pltpu.SMEM)]
        + [full(x)]
        + ([block(D, PACK)] if whole else [full(a) for a in pieces]),
        out_specs=out_specs,
        out_shape=out_shape,
        compiler_params=pltpu.CompilerParams(vmem_limit_bytes=VMEM_LIMIT),
        cost_estimate=pl.CostEstimate(
            flops=groups * 2_500_000_000, bytes_accessed=groups * 3_000_000, transcendentals=0
        ),
        name="attend",
    )(info, x, *pieces)
    return (pieces[0], result) if whole else (result[0], result[1:])


def attend_back_kernel(xt_ref, qkv_ref, p_ref, aug_ref, go_ref, *refs, graphs):
    *more, g_ref, d_ref = refs
    lane = lanes()
    for g in range(graphs):
        rows = slice(g * LEN, (g + 1) * LEN)
        query, keys, values = qkv_ref[0, 0, rows, :], qkv_ref[0, 1, rows, :], qkv_ref[0, 2, rows, :]
        d_rows, expo = aug_ref[0, rows, :], p_ref[0, rows, :]
        one, zero = jnp.ones_like(values), jnp.zeros_like(values)
        spread = jnp.concatenate(
            [
                jnp.where(
                    head_lanes(h, V_AT), values, jnp.where((lane == h) | (lane == SUB + h), one, zero)
                )
                for h in range(SUB)
            ],
            axis=0,
        )
        d_scores = (expo.astype(F32) * nt(d_rows, spread)).astype(BF)
        d_query = nn(d_scores, by_head(keys, 0)) * SCALE
        d_keys = tn(stack_heads(d_scores), by_head(query, 0)) * SCALE
        d_values = tn(stack_heads(expo), by_head(d_rows, V_AT))
        rolled_keys, rolled_values = pltpu.roll(d_keys, SW, 1), pltpu.roll(d_values, V_AT, 1)
        d_ref[0, rows, 0:128] = jnp.where(lane < SW, d_query, rolled_keys).astype(BF)
        d_ref[0, rows, 128:256] = jnp.where(lane < 64, rolled_keys, rolled_values).astype(BF)
        d_ref[0, rows, 256:384] = jnp.where(lane < V_AT, rolled_values, 0.0).astype(BF)
    grad = nn(xt_ref[...], d_ref[0])
    end = jnp.where(lane < V_AT, grad[:, 256:384], go_ref[0].astype(F32))
    if not more:
        g_ref[0, :, 0:256] = grad[:, 0:256].astype(BF)
        g_ref[0, :, 256:384] = end.astype(BF)
        return
    info_ref, came_ref = more
    outs, size = g_ref.shape[2], g_ref.shape[3]
    for o in range(outs):
        for i in range(2):
            rows = slice((o * 2 + i) * size, (o * 2 + i + 1) * size)
            at = lax.rem(i + info_ref[1], 2)
            came = came_ref[0, rows, :].astype(F32)
            g_ref[0, at, o, :, 0:256] = (grad[rows, 0:256] + came[:, 0:256]).astype(BF)
            g_ref[0, at, o, :, 256:384] = (end[rows] + came[:, 256:384]).astype(BF)


def attend_back(xt, saved, aug, grad_out, first, stride, groups, more=(), outs=0):
    qkv, expo = saved[:2]
    tokens = xt.shape[1]
    shape = (2, outs, D // (2 * outs), PACK) if more else (D, PACK)
    block = lambda *tail: pl.BlockSpec(
        (1,) + tail, lambda i: (first + i * stride,) + (0,) * len(tail)
    )
    out = lambda *tail: pl.BlockSpec((1,) + tail, lambda i: (i,) + (0,) * len(tail))
    return pl.pallas_call(
        functools.partial(attend_back_kernel, graphs=tokens // LEN),
        grid=(groups,),
        in_specs=[
            pl.BlockSpec(xt.shape, lambda i: (0, 0)),
            block(3, tokens, 128),
            block(tokens, 512),
            block(tokens, 128),
            block(D, 128),
        ]
        + ([pl.BlockSpec(memory_space=pltpu.SMEM), block(D, PACK)] if more else []),
        out_specs=[out(*shape), out(tokens, PACK)],
        out_shape=[
            jax.ShapeDtypeStruct((groups,) + shape, BF),
            jax.ShapeDtypeStruct((groups, tokens, PACK), BF),
        ],
        compiler_params=pltpu.CompilerParams(vmem_limit_bytes=VMEM_LIMIT),
        cost_estimate=pl.CostEstimate(
            flops=groups * 4_000_000_000, bytes_accessed=groups * 3_000_000, transcendentals=0
        ),
        name="attend_back",
    )(xt, qkv, expo, aug, grad_out, *more)


def first_sum_kernel(*refs, parts):
    d_refs, w_refs, out_ref = refs[: len(parts)], refs[len(parts) : -1], refs[-1]
    total = jnp.zeros(out_ref.shape, F32)
    for d_ref, (which, picks) in zip(d_refs, parts):
        for j in range(0, len(picks), 2):
            pair = range(j, min(j + 2, len(picks)))
            left = jnp.concatenate([d_ref[k] for k in pair], axis=1)
            right = jnp.concatenate([w_refs[which][picks[k]] for k in pair], axis=1)
            total = total + nt(left, right)
    out_ref[...] = total


def first_sum(ds, parts, weights):
    tokens = ds[0].shape[1]
    rows = LEN * min(2, tokens // LEN)
    full = lambda a: pl.BlockSpec(a.shape, lambda i: (0,) * a.ndim)
    return pl.pallas_call(
        functools.partial(first_sum_kernel, parts=parts),
        grid=(tokens // rows,),
        in_specs=[pl.BlockSpec((d.shape[0], rows, PACK), lambda i: (0, i, 0)) for d in ds]
        + [full(w) for w in weights],
        out_specs=pl.BlockSpec((rows, D), lambda i: (i, 0)),
        out_shape=jax.ShapeDtypeStruct((tokens, D), F32),
        compiler_params=pltpu.CompilerParams(vmem_limit_bytes=VMEM_LIMIT),
        cost_estimate=pl.CostEstimate(
            flops=7_000_000_000, bytes_accessed=12_000_000, transcendentals=0
        ),
        name="first_sum",
    )(*ds, *weights)


def first_back_kernel(
    e_ref, dmid_ref, ident_ref, gain_ref, sum_ref, even_ref, odd_ref, w_ref, out_ref, acc
):
    step, steps = pl.program_id(0), pl.num_programs(0)
    d_normed = sum_ref[...]
    for at, d_ref in enumerate((even_ref, odd_ref)):
        left = jnp.concatenate([d_ref[0], d_ref[1]], axis=1)
        d_normed = d_normed + nt(left, jnp.concatenate([w_ref[at], w_ref[at + 2]], axis=1))
    xhat, rstd = normalize(e_ref[...])
    d_emb = dmid_ref[...] + norm_back(d_normed, xhat, rstd, gain_ref[GAIN : GAIN + 1, :])
    part = tn(ident_ref[...], d_emb.astype(BF))
    part_gain = jnp.sum((d_normed * xhat).reshape(-1, 8, D), axis=0)

    @pl.when(step == 0)
    def _():
        acc[0 : 2 * LAP, :] = part
        acc[2 * LAP :, :] = part_gain

    @pl.when(step > 0)
    def _():
        acc[0 : 2 * LAP, :] += part
        acc[2 * LAP :, :] += part_gain

    @pl.when(step == steps - 1)
    def _():
        out_ref[...] = acc[...]


def first_back(embedded, d_middle, ident_rows, gains, total, d_even, d_odd, weights):
    tokens = embedded.shape[0]
    rows = LEN * min(2, tokens // LEN)
    full = lambda a: pl.BlockSpec(a.shape, lambda i: (0,) * a.ndim)
    tile = pl.BlockSpec((rows, D), lambda i: (i, 0))
    return pl.pallas_call(
        first_back_kernel,
        grid=(tokens // rows,),
        in_specs=[tile, tile, pl.BlockSpec((rows, 2 * LAP), lambda i: (i, 0)), full(gains), tile]
        + [pl.BlockSpec((2, rows, PACK), lambda i: (0, i, 0))] * 2
        + [full(weights)],
        out_specs=pl.BlockSpec((2 * LAP + 8, D), lambda i: (0, 0)),
        out_shape=jax.ShapeDtypeStruct((2 * LAP + 8, D), F32),
        scratch_shapes=[pltpu.VMEM((2 * LAP + 8, D), F32)],
        compiler_params=pltpu.CompilerParams(vmem_limit_bytes=VMEM_LIMIT),
        cost_estimate=pl.CostEstimate(
            flops=4_000_000_000, bytes_accessed=10_000_000, transcendentals=0
        ),
        name="first_back",
    )(embedded, d_middle, ident_rows, gains, total, d_even, d_odd, weights)


def normal_parts(x):
    falling = jnp.exp(-0.5 * x * x)
    t = 1.0 / (1.0 + (0.3275911 * 0.5**0.5) * jnp.abs(x))
    tail = 0.5 * 1.061405429
    for c in (-1.453152027, 1.421413741, -0.284496736, 0.254829592):
        tail = tail * t + 0.5 * c
    tail = tail * t * falling
    return jnp.where(x < 0.0, tail, 1.0 - tail), 0.3989422804014327 * falling


def normalize(values):
    centred = values - jnp.mean(values, axis=-1, keepdims=True)
    spread = jnp.mean(centred * centred, axis=-1, keepdims=True)
    rstd = lax.rsqrt(spread + NORM_EPS)
    return centred * rstd, rstd


def two_parts(v):
    high = v.astype(BF)
    return high, (v - high.astype(F32)).astype(BF)


def forward_kernel(
    info_ref, e_ref, gain_ref, ffn_ref, other_ref, *refs, tile_graphs, waves, groups
):
    o_refs, w_refs = refs[:waves], refs[waves : 2 * waves]
    mid_ref, slope_ref, pay_ref, up_ref, down_ref, hsum, msum = refs[2 * waves :]
    step, steps = pl.program_id(0), pl.num_programs(0)
    core = info_ref[3]

    @pl.when((step == 0) & (core == 0))
    def _():
        up_ref[...] = ffn_ref[...]
        down_ref[...] = other_ref[...]

    @pl.when((step == 0) & (core != 0))
    def _():
        up_ref[...] = other_ref[...]
        down_ref[...] = ffn_ref[...]

    middle = e_ref[...]
    for wave in range(waves):
        left = jnp.concatenate([o_refs[wave][j] for j in range(groups)], axis=1)
        right = jnp.concatenate([w_refs[wave][j][:, 256:] for j in range(groups)], axis=1)
        middle = middle + nt(left, right)
    mid_ref[...] = middle
    xhat, _ = normalize(middle)
    up = nn((xhat * gain_ref[GAIN + 1 : GAIN + 2, :]).astype(BF), up_ref[...])
    cdf, density = normal_parts(up)
    hidden = (up * cdf).astype(BF).astype(F32)
    slope_ref[...] = (cdf + up * density).astype(BF)
    place = lax.broadcasted_iota(jnp.int32, (LEN, 1), 0)
    for j in range(tile_graphs):
        g = step * tile_graphs + j
        live = place < info_ref[LENS + g]
        rows = slice(j * LEN, (j + 1) * LEN)
        hsum[pl.ds(g, 1), :] = jnp.sum(jnp.where(live, hidden[rows], 0.0), axis=0, keepdims=True)
        msum[pl.ds(g, 1), :] = jnp.sum(jnp.where(live, middle[rows], 0.0), axis=0, keepdims=True)

    @pl.when(step == steps - 1)
    def _():
        graphs = hsum.shape[0]
        high, low = two_parts(hsum[...])
        which = lax.broadcasted_iota(jnp.int32, (graphs, 1), 0)
        length, partner = jnp.ones((graphs, 1), F32), jnp.zeros((graphs, 1), F32)
        for g in range(graphs):
            length = jnp.where(which == g, info_ref[LENS + g].astype(F32), length)
            partner = jnp.where(which == g, info_ref[LENS + graphs + g].astype(F32), partner)
        pooled = (msum[...] + (nt(high, down_ref[...]) + nt(low, down_ref[...]))) / length
        xhat_pool, rstd = normalize(pooled)
        high, low = two_parts(xhat_pool)
        pay_ref[:, 0:D] = high
        pay_ref[:, D : 2 * D] = low
        pay_ref[:, 2 * D : 3 * D] = hsum[...].astype(BF)
        lane = lanes()
        stats = jnp.zeros((graphs, 128), F32)
        for at, value in enumerate(two_parts(rstd) + two_parts(1.0 / length) + (partner,)):
            stats = jnp.where(lane == at, value.astype(F32), stats)
        pay_ref[:, 3 * D :] = stats.astype(BF)


def forward_rest(info, embedded, gains, w_up, w_down, outs, weights):
    tokens = embedded.shape[0]
    graphs = tokens // LEN
    tile_graphs = min(2, graphs)
    rows = tile_graphs * LEN
    waves, groups = len(outs), outs[0].shape[0]
    full = lambda a: pl.BlockSpec(a.shape, lambda i: (0,) * a.ndim)
    tile = pl.BlockSpec((rows, D), lambda i: (i, 0))
    return pl.pallas_call(
        functools.partial(forward_kernel, tile_graphs=tile_graphs, waves=waves, groups=groups),
        grid=(tokens // rows,),
        in_specs=[pl.BlockSpec(memory_space=pltpu.SMEM)]
        + [tile, full(gains), full(w_up), full(w_down)]
        + [pl.BlockSpec((groups, rows, 128), lambda i: (0, i, 0)) for _ in outs]
        + [full(w) for w in weights],
        out_specs=[
            tile,
            tile,
            pl.BlockSpec((graphs, 3 * D + 128), lambda i: (0, 0)),
            full(w_up),
            full(w_down),
        ],
        out_shape=[
            jax.ShapeDtypeStruct((tokens, D), F32),
            jax.ShapeDtypeStruct((tokens, D), BF),
            jax.ShapeDtypeStruct((graphs, 3 * D + 128), BF),
            jax.ShapeDtypeStruct(w_up.shape, BF),
            jax.ShapeDtypeStruct(w_down.shape, BF),
        ],
        scratch_shapes=[pltpu.VMEM((graphs, D), F32), pltpu.VMEM((graphs, D), F32)],
        compiler_params=pltpu.CompilerParams(vmem_limit_bytes=VMEM_LIMIT),
        cost_estimate=pl.CostEstimate(
            flops=10_000_000_000, bytes_accessed=20_000_000, transcendentals=0
        ),
        name="forward_rest",
    )(info, embedded, gains, w_up, w_down, *outs, *weights)


def norm_back(d_normed, xhat, rstd, gain):
    d_hat = d_normed * gain
    return rstd * (
        d_hat
        - jnp.mean(d_hat, axis=-1, keepdims=True)
        - xhat * jnp.mean(d_hat * xhat, axis=-1, keepdims=True)
    )


def ffn_back_kernel(
    info_ref, mid_ref, slope_ref, dout_ref, dhid_ref, gain_ref, up_ref, *refs, tile_graphs, groups
):
    o_refs, rinv_refs, w_refs = refs[0:2], refs[2:4], refs[4:6]
    dmid_ref, grad_ref, dgain_ref = refs[6:9]
    aug_refs, go_refs = refs[9:11], refs[11:13]
    grad, dgain, grad_out = refs[13:]
    step, steps = pl.program_id(0), pl.num_programs(0)
    xhat, rstd = normalize(mid_ref[...])
    gain = gain_ref[GAIN + 1 : GAIN + 2, :]
    place = lax.broadcasted_iota(jnp.int32, (LEN, 1), 0)
    d_up, d_out = [], []
    for j in range(tile_graphs):
        g = step * tile_graphs + j
        live = place < info_ref[LENS + g]
        rows = slice(j * LEN, (j + 1) * LEN)
        d_hidden = jnp.where(live, dhid_ref[pl.ds(g, 1), :], 0.0)
        d_up.append((slope_ref[rows, :].astype(F32) * d_hidden).astype(BF))
        d_out.append(jnp.where(live, dout_ref[pl.ds(g, 1), :], 0.0))
    d_up, d_out = jnp.concatenate(d_up, axis=0), jnp.concatenate(d_out, axis=0)
    d_normed = nt(d_up, up_ref[...])
    d_mid = d_out + norm_back(d_normed, xhat, rstd, gain)
    dmid_ref[...] = d_mid
    d_attn = d_mid.astype(BF)
    d_turned = d_attn.T
    part = tn((xhat * gain).astype(BF), d_up)
    part_gain = jnp.sum((d_normed * xhat).reshape(-1, 8, D), axis=0)

    lane = lanes()
    row = lax.broadcasted_iota(jnp.int32, (256, 128), 0) & 127
    column = lax.broadcasted_iota(jnp.int32, (256, 128), 1)
    pick = jnp.zeros((256, 128), BF)
    for h in range(SUB):
        inside = (row >= V_AT + h * HEAD_DIM) & (row < V_AT + (h + 1) * HEAD_DIM)
        pick = jnp.where(inside & ((column == h) | (column == SUB + h)), jnp.ones_like(pick), pick)
    parts_out = []
    for half in range(2):
        d_heads = nn(d_attn, jnp.concatenate([w_refs[half][j] for j in range(groups)], axis=1))
        for j in range(groups):
            d_over = d_heads[:, j * 128 : (j + 1) * 128] * rinv_refs[half][j]
            d_over = jnp.where(lane >= V_AT, d_over, 0.0)
            terms = d_over * o_refs[half][j].astype(F32)
            delta = nn(jnp.concatenate(two_parts(terms), axis=1), pick)
            rounded = delta.astype(BF).astype(F32)
            aug_refs[half][j] = jnp.where(
                lane >= V_AT, d_over, jnp.where(lane < SUB, -rounded, rounded - delta)
            ).astype(BF)
        parts_out.append(
            nn(d_turned, jnp.concatenate([o_refs[half][j] for j in range(groups)], axis=1))
        )

    @pl.when(step == 0)
    def _():
        grad[...] = part
        dgain[...] = part_gain
        for half in range(2):
            grad_out[half] = parts_out[half]

    @pl.when(step > 0)
    def _():
        grad[...] += part
        dgain[...] += part_gain
        for half in range(2):
            grad_out[half] += parts_out[half]

    @pl.when(step == steps - 1)
    def _():
        for half in range(2):
            grad_ref[half] = grad[:, half * PACK : (half + 1) * PACK].astype(BF)
            for j in range(groups):
                go_refs[half][j] = grad_out[half, :, j * 128 : (j + 1) * 128].astype(BF)
        dgain_ref[...] = dgain[...]


def ffn_back(info, middle, slope, d_out, d_hidden, gains, w_up, outs, rinvs, weights):
    tokens = middle.shape[0]
    tile_graphs = min(2, tokens // LEN)
    rows = tile_graphs * LEN
    groups = outs[0].shape[0]
    full = lambda a: pl.BlockSpec(a.shape, lambda i: (0,) * a.ndim)
    tile = pl.BlockSpec((rows, D), lambda i: (i, 0))
    sub_tile = pl.BlockSpec((groups, rows, 128), lambda i: (0, i, 0))
    result = pl.pallas_call(
        functools.partial(ffn_back_kernel, tile_graphs=tile_graphs, groups=groups),
        grid=(tokens // rows,),
        in_specs=[pl.BlockSpec(memory_space=pltpu.SMEM), tile, tile]
        + [full(a) for a in (d_out, d_hidden, gains, w_up)]
        + [sub_tile] * 4
        + [pl.BlockSpec((groups, D, 128), lambda i: (0, 0, 2))] * 2,
        out_specs=[
            tile,
            pl.BlockSpec((2, D, PACK), lambda i: (0, 0, 0)),
            pl.BlockSpec((8, D), lambda i: (0, 0)),
        ]
        + [sub_tile] * 2
        + [pl.BlockSpec((groups, D, 128), lambda i: (0, 0, 0))] * 2,
        out_shape=[
            jax.ShapeDtypeStruct((tokens, D), F32),
            jax.ShapeDtypeStruct((2, D, PACK), BF),
            jax.ShapeDtypeStruct((8, D), F32),
        ]
        + [jax.ShapeDtypeStruct((groups, tokens, 128), BF)] * 2
        + [jax.ShapeDtypeStruct((groups, D, 128), BF)] * 2,
        scratch_shapes=[
            pltpu.VMEM((D, D), F32),
            pltpu.VMEM((8, D), F32),
            pltpu.VMEM((2, D, groups * 128), F32),
        ],
        compiler_params=pltpu.CompilerParams(vmem_limit_bytes=VMEM_LIMIT),
        cost_estimate=pl.CostEstimate(
            flops=14_000_000_000, bytes_accessed=20_000_000, transcendentals=0
        ),
        name="ffn_back",
    )(info, middle, slope, d_out, d_hidden, gains, w_up, *outs, *rinvs, *weights)
    return result[:3], result[3:5], result[5:7]


def loss_kernel(
    info_ref, a1_ref, a3_ref, b1_ref, b3_ref, gain_ref, down_ref,
    loss_ref, dout_ref, dhid_ref, dlow_ref, hid_ref, dgain_ref, xhat, stats, rows_ref
):
    outs, graphs = a1_ref.shape[1], a1_ref.shape[2]
    outer, inner, far, core = (info_ref[i] for i in range(4))
    count = outs * 2 * GRAPHS_DEV
    place = lambda f, o, i, c: pl.multiple_of(
        f * count + (o * 2 + i) * GRAPHS_DEV + c * graphs, graphs
    )
    for owner, refs in ((core, (a1_ref, a3_ref)), (1 - core, (b1_ref, b3_ref))):
        for part, ref in enumerate(refs):
            for at in range(2):
                if part == at:
                    f, i = part, part
                else:
                    f, i = (owner, 1 - owner) if part == 0 else (1 - owner, owner)
                for o in range(outs):
                    values = ref[at, o].astype(F32)
                    row = place(
                        lax.rem(far + f, 2), lax.rem(outer + outs - o, outs), lax.rem(inner + i, 2), owner
                    )
                    rows = pl.ds(row, graphs)
                    xhat[rows, :] = values[:, 0:D] + values[:, D : 2 * D]
                    rows_ref[rows, :] = values[:, 2 * D : 3 * D]
                    stats[rows, :] = values[:, 3 * D :]
    hid_ref[...] = rows_ref[...].astype(BF)
    root = D**-0.5
    left, right = xhat[0:count, :] * gain_ref[GAIN + 2 : GAIN + 3, :], xhat[count:, :] * gain_ref[GAIN + 2 : GAIN + 3, :]
    exact = lambda a, b, dims: lax.dot_general(
        a, b, (dims, ((), ())), precision=HIGHEST, preferred_element_type=F32
    )
    logits = exact(left, right, ((1,), (1,))) * root
    row_top, col_top = jnp.max(logits, axis=1, keepdims=True), jnp.max(logits, axis=0, keepdims=True)
    row_expo, col_expo = jnp.exp(logits - row_top), jnp.exp(logits - col_top)
    row_sum, col_sum = jnp.sum(row_expo, axis=1, keepdims=True), jnp.sum(col_expo, axis=0, keepdims=True)
    row_id = lax.broadcasted_iota(jnp.int32, (count, count), 0)
    col_id = lax.broadcasted_iota(jnp.int32, (count, count), 1)
    slot = stats[0:count, 4:5].astype(jnp.int32)
    positive = jnp.where(col_id == (row_id & -GRAPHS_DEV) + slot, 1.0, 0.0)
    loss = (
        jnp.sum(row_top + jnp.log(row_sum), axis=0, keepdims=True)
        + jnp.sum(col_top + jnp.log(col_sum), axis=1, keepdims=True)
        - 2.0 * jnp.sum(jnp.sum(positive * logits, axis=1, keepdims=True), axis=0, keepdims=True)
    )
    loss_ref[...] = loss
    d_logits = row_expo / row_sum + col_expo / col_sum - 2.0 * positive
    rows_ref[0:count, :] = exact(d_logits, right, ((1,), (0,))) * root
    rows_ref[count:, :] = exact(d_logits, left, ((0,), (0,))) * root
    every = xhat[...]
    d_summary = rows_ref[...]
    dgain_ref[...] = jnp.sum(d_summary * every, axis=0, keepdims=True)
    rstd, share = stats[:, 0:1] + stats[:, 1:2], stats[:, 2:3] + stats[:, 3:4]
    d_rows = norm_back(d_summary, every, rstd, gain_ref[GAIN + 2 : GAIN + 3, :]) * share
    rows_ref[...] = d_rows
    dlow_ref[...] = d_rows.astype(BF)
    own = rows_ref[pl.ds(place(far, outer, inner, core), graphs), :]
    dout_ref[...] = own
    dhid_ref[...] = nn(own.astype(BF), down_ref[...])


def contrast(info, pieces, gains, w_down):
    outs, graphs = pieces[0].shape[1], pieces[0].shape[2]
    total = outs * 4 * GRAPHS_DEV
    return pl.pallas_call(
        loss_kernel,
        in_specs=[pl.BlockSpec(memory_space=pltpu.SMEM)]
        + [pl.BlockSpec(memory_space=pltpu.VMEM)] * 6,
        out_specs=[pl.BlockSpec(memory_space=pltpu.VMEM)] * 6,
        out_shape=[
            jax.ShapeDtypeStruct((1, 1), F32),
            jax.ShapeDtypeStruct((graphs, D), F32),
            jax.ShapeDtypeStruct((graphs, D), F32),
            jax.ShapeDtypeStruct((total, D), BF),
            jax.ShapeDtypeStruct((total, D), BF),
            jax.ShapeDtypeStruct((1, D), F32),
        ],
        scratch_shapes=[
            pltpu.VMEM((total, D), F32),
            pltpu.VMEM((total, 128), F32),
            pltpu.VMEM((total, D), F32),
        ],
        compiler_params=pltpu.CompilerParams(vmem_limit_bytes=24 * 2**20),
        cost_estimate=pl.CostEstimate(
            flops=3_000_000_000, bytes_accessed=4_000_000, transcendentals=0
        ),
        name="contrast",
    )(info, *pieces, gains, w_down)


def contrast_plain(everyone, gains, w_down, own_row, graphs):
    n = everyone.shape[0]
    stats = everyone[..., 3 * D :].astype(F32)
    xhat = everyone[..., :D].astype(F32) + everyone[..., D : 2 * D].astype(F32)
    hidden_sums = everyone[..., 2 * D : 3 * D].reshape(-1, D)
    rstd_pool = (stats[..., 0:1] + stats[..., 1:2]).reshape(-1, 1)
    share = (stats[..., 2:3] + stats[..., 3:4]).reshape(-1, 1)
    summaries = xhat * gains[GAIN + 2]
    left, right = summaries[:, 0].reshape(-1, D), summaries[:, 1].reshape(-1, D)
    root_width = D**0.5
    logits = jnp.dot(left, right.T, precision=HIGHEST) / root_width
    row_totals, col_totals = log_total(logits, 1), log_total(logits, 0)
    count = logits.shape[0]
    group = jnp.arange(count, dtype=jnp.int32) // GRAPHS_DEV
    partners = group * GRAPHS_DEV + stats[:, 0, :, 4].reshape(-1).astype(jnp.int32)
    positive = (partners[:, None] == jnp.arange(count, dtype=jnp.int32)[None, :]).astype(F32)
    total_loss = jnp.sum(row_totals) + jnp.sum(col_totals) - 2.0 * jnp.sum(positive * logits)
    d_logits = (
        jnp.exp(logits - row_totals[:, None])
        + jnp.exp(logits - col_totals[None, :])
        - 2.0 * positive
    )
    d_left = jnp.dot(d_logits, right, precision=HIGHEST) / root_width
    d_right = jnp.dot(d_logits.T, left, precision=HIGHEST) / root_width
    d_summary = jnp.stack(
        [d_left.reshape(n, GRAPHS_DEV, D), d_right.reshape(n, GRAPHS_DEV, D)], axis=1
    ).reshape(-1, D)
    xhat = xhat.reshape(-1, D)
    gain_three = jnp.sum(d_summary * xhat, axis=0, keepdims=True)
    d_rows = norm_back(d_summary, xhat, rstd_pool, gains[GAIN + 2]) * share
    d_out = lax.dynamic_slice_in_dim(d_rows, own_row, graphs, 0)
    d_hidden = nn(d_out.astype(BF), w_down)
    return total_loss, d_out, d_hidden, d_rows.astype(BF), hidden_sums, gain_three


class Place:
    def __init__(self):
        self.n, self.heads = lax.axis_size("dp"), lax.axis_size("head")
        self.outs = self.n // 2
        dp, head = lax.axis_index("dp"), lax.axis_index("head")
        self.dp, self.head = dp, head
        self.outer, self.inner, self.far, self.core = dp // 2, dp % 2, head // 2, head % 2

    def move(self, v, to):
        pairs = []
        for i in range(self.n * self.heads):
            outer, inner, far, core = i // 8, (i // 4) % 2, (i // 2) % 2, i % 2
            outer, inner, far, core = to(outer, inner, far, core)
            pairs.append((i, ((outer % self.outs * 2 + inner) * 2 + far) * 2 + core))
        return lax.ppermute(v, ("dp", "head"), pairs)

    def to_core(self, v):
        return self.move(v, lambda o, i, f, c: (o, i, f, 1 - c))

    def to_outer(self, v, by):
        return self.move(v, lambda o, i, f, c: (o + by, i, f, c))

    def mixed(self, v, turn):
        return self.move(
            v, lambda o, i, f, c: (o, 1 - i, f, c) if c == turn else (o, i, 1 - f, c)
        )

    def by_core(self, a, b):
        return jnp.where(self.core == 0, a, b)

    def gather_outer(self, v):
        out = jnp.zeros((self.outs,) + v.shape, v.dtype)
        out = lax.dynamic_update_index_in_dim(out, v, self.outer, 0)
        for by in range(1, self.outs):
            out = lax.dynamic_update_index_in_dim(
                out, self.to_outer(v, by), (self.outer - by) % self.outs, 0
            )
        return out

    def outer_list(self, v):
        return jnp.stack([v] + [self.to_outer(v, by) for by in range(1, self.outs)])

    def gather_pieces(self, v):
        return self.gather_near(self.gather_outer(v))

    def gather_near(self, own):
        return self.gather_last(own, self.mixed(own, 0))

    def gather_last(self, own, second):
        return self.pieces_of(own, second, self.mixed(jnp.stack([own, second]), 1))

    def pieces_of(self, own, second, third):
        return [
            [own, self.by_core(second, third[0])],
            [self.by_core(third[0], second), third[1]],
        ]

    def whole(self, pieces):
        rows = [
            [jnp.where(self.far == 0, pieces[f][i], pieces[1 - f][i]) for f in range(2)]
            for i in range(2)
        ]
        ordered = [
            [jnp.where(self.inner == 0, rows[i][f], rows[1 - i][f]) for f in range(2)]
            for i in range(2)
        ]
        return jnp.stack([jnp.stack(pair, axis=1) for pair in ordered], axis=1)

    def both_cores(self, v, axis):
        other = self.to_core(v)
        return jnp.stack([self.by_core(v, other), self.by_core(other, v)], axis=axis)

    def both_cores_of(self, own, sent):
        other = self.to_core(sent)
        return jnp.stack([self.by_core(own, other), self.by_core(other, own)])

    def gather_all(self, v):
        v = self.both_cores(self.whole(self.gather_pieces(v)), 3)
        return v.reshape((self.n, self.heads) + v.shape[4:])

    def fold_far(self, pieces):
        sent = jnp.stack([self.by_core(pieces[1][0], pieces[0][1]), pieces[1][1]])
        kept = jnp.stack([pieces[0][0], self.by_core(pieces[0][1], pieces[1][0])])
        return kept, sent

    def fold_near(self, kept, came, dtype):
        total = kept.astype(F32) + came.astype(F32)
        return total[0], total[1].astype(dtype)

    def fold_outer(self, kept, came, dtype):
        total = (kept.astype(F32) + came.astype(F32)).astype(dtype)
        pick = lambda by: lax.dynamic_index_in_dim(
            total, (self.outer + by) % self.outs, 0, keepdims=False
        )
        result = pick(0).astype(F32)
        for by in range(1, self.outs):
            result = result + self.to_outer(pick(by), by).astype(F32)
        return result

    def total(self, v):
        v = jnp.broadcast_to(v, (self.n * self.heads, 128))
        return jnp.sum(lax.all_to_all(v, ("dp", "head"), 0, 0, tiled=True)[:, 0])

    def split_rows(self, v):
        v = v.reshape((self.outs, 2, -1) + v.shape[1:])
        return [
            lax.dynamic_index_in_dim(v, (self.inner + i) % 2, 1, keepdims=False) for i in range(2)
        ]


def tie(*values):
    return lax.optimization_barrier(values)


def after(value, *others):
    return lax.optimization_barrier((value,) + others)[0]


def log_total(values, axis):
    top = jnp.max(values, axis=axis, keepdims=True)
    return jnp.squeeze(top, axis) + jnp.log(jnp.sum(jnp.exp(values - top), axis=axis))


def identifiers(table, endpoints):
    graphs = endpoints.shape[0] // LEN
    nodes = table.reshape(graphs, NODE, LAP).astype(BF)
    picks = (
        endpoints.reshape(graphs, LEN, 2)[..., None] == jnp.arange(NODE, dtype=jnp.int32)
    ).astype(BF)
    found = jnp.einsum("glan,gnc->glac", picks, nodes, preferred_element_type=F32)
    return found.reshape(graphs * LEN, 2 * LAP).astype(BF)


def stack_pieces(place, near, last):
    pieces = place.pieces_of(near[0], near[1], last)
    packs = []
    for f in range(2):
        for c in range(2):
            rows = [
                jnp.where(place.inner == i, pieces[f][0][:, c], pieces[f][1][:, c]) for i in range(2)
            ]
            packs.append(jnp.stack(rows, axis=1).reshape(D, PACK))
    return jnp.stack(packs)


def split_core(place, grad_up):
    v = grad_up.reshape((2, place.outs, 2, 2, 2, -1, PACK))
    pick = lambda at: lax.dynamic_index_in_dim(v, at, 4, keepdims=False)
    return pick(1 - place.core), pick(place.core)


def fold_pieces(place, own, came, up):
    pieces = []
    for f in range(2):
        total = own[f].astype(F32) + came[f].astype(F32)
        pieces.append([v.astype(BF) for v in place.split_rows(total)])
    if up is None:
        return pieces
    total = (up[0].astype(F32) + up[1].astype(F32)).astype(BF)
    for f in range(2):
        part = lax.dynamic_index_in_dim(total, (place.far + f) % 2, 3, keepdims=False)
        for i in range(2):
            rows = lax.dynamic_index_in_dim(part, (place.inner + i) % 2, 2, keepdims=False)
            pieces[f][i] = jnp.concatenate([pieces[f][i], rows[0], rows[1]], axis=1)
    return pieces


def squares_kernel(*refs):
    *grad_refs, out_ref = refs
    total = jnp.zeros((1, 1), F32)
    for ref in grad_refs:
        v = ref[...]
        total = total + jnp.sum(jnp.sum(v * v, axis=0, keepdims=True), axis=1, keepdims=True)
    out_ref[...] = jnp.broadcast_to(total, out_ref.shape)


def squares(grads, devices):
    return pl.pallas_call(
        squares_kernel,
        out_shape=jax.ShapeDtypeStruct((devices, 128), F32),
        cost_estimate=pl.CostEstimate(flops=1_000_000, bytes_accessed=500_000, transcendentals=0),
        name="squares",
    )(*grads)


def update_kernel(parts_ref, *refs):
    count = len(STEP_RATES)
    grads, weights, firsts, seconds = (refs[k * count : (k + 1) * count] for k in range(4))
    norm_ref, refs = refs[4 * count], refs[4 * count + 1 :]
    new_weights, new_firsts, new_seconds = (refs[k * count : (k + 1) * count] for k in range(3))
    norm = jnp.sqrt(jnp.sum(parts_ref[...], axis=0, keepdims=True)[:, 0:1])
    norm_ref[...] = norm
    factor = CLIP_AT / jnp.maximum(norm, CLIP_AT)
    for k, rate in enumerate(STEP_RATES):
        for at in range(grads[k].shape[0]) if len(grads[k].shape) == 3 else (...,):
            weight = weights[k][at]
            clipped = grads[k][at] * factor
            first = BETA_ONE * firsts[k][at] + (1.0 - BETA_ONE) * clipped
            second = BETA_TWO * seconds[k][at] + (1.0 - BETA_TWO) * clipped * clipped
            first_hat = first / (1.0 - BETA_ONE**STEPS)
            second_hat = second / (1.0 - BETA_TWO**STEPS)
            new_weights[k][at] = weight - rate * (
                first_hat / (jnp.sqrt(second_hat) + ADAM_EPS) + DECAY * weight
            )
            new_firsts[k][at] = first
            new_seconds[k][at] = second


def update(norm_parts, grads, state):
    result = pl.pallas_call(
        update_kernel,
        out_shape=[jax.ShapeDtypeStruct((1, 1), F32)]
        + [jax.ShapeDtypeStruct(v.shape, F32) for kind in state for v in kind],
        cost_estimate=pl.CostEstimate(
            flops=5_000_000, bytes_accessed=6_000_000, transcendentals=0
        ),
        name="update",
    )(norm_parts, *grads, *(v for kind in state for v in kind))
    count = len(grads)
    return result[0], [result[1 + k * count : 1 + (k + 1) * count] for k in range(3)]


def per_device(
    features,
    laplacian,
    endpoints,
    lengths,
    pairing,
    ident_weight,
    qkv_weight,
    out_weight,
    ffn_weight,
    norm_gains,
    ident_first,
    qkv_first,
    out_first,
    ffn_first,
    gains_first,
    ident_second,
    qkv_second,
    out_second,
    ffn_second,
    gains_second,
):
    place = Place()
    heads, head, dp, core = place.heads, place.head, place.dp, place.core
    tokens = features.shape[0] // heads
    graphs = tokens // LEN
    own_columns = norm_gains.shape[1]

    small = jnp.concatenate([ident_weight, norm_gains], axis=0)
    small_rows = small.shape[0]

    packed = [qkv_weight[:, 0], qkv_weight[:, 1], qkv_weight[:, 2], out_weight.T]
    shards = jnp.stack(
        [
            jnp.concatenate([m[:, s * SW : (s + 1) * SW] for m in packed], axis=1).astype(BF)
            for s in range(2)
        ]
    )
    pick = lambda v, at: lax.dynamic_index_in_dim(v, at, 0, keepdims=False)
    near = jnp.stack([pick(shards, core), place.to_core(pick(shards, 1 - core))])
    shard_rows = D // place.n
    aligned = shard_rows % 16 == 0
    devices = place.n * heads
    small = jnp.broadcast_to(after(small.reshape(1, -1), near), (devices, small.size))
    small = lax.all_to_all(small, ("dp", "head"), 0, 0, tiled=True)
    near_own = (place.outer_list if aligned else place.gather_outer)(near)
    ffn = after(ffn_weight.astype(BF), near_own)
    ffn_near = place.both_cores_of(pick(ffn, core), pick(ffn, 1 - core))
    ffn_own = place.gather_outer(ffn_near)
    near_own = after(near_own, small)
    near = jnp.stack([near_own, place.mixed(near_own, 0)])
    last = place.mixed(near, 1)
    near_others = place.to_core(near)
    ffn_own = after(ffn_own, near)
    ffn_next = place.mixed(ffn_own, 0)
    ffn_last = place.mixed(jnp.stack([ffn_own, ffn_next]), 1)
    small = small.reshape(-1, small_rows, own_columns).transpose(1, 0, 2).reshape(small_rows, D)
    ident_full, gains = after(small[: 2 * LAP].astype(BF), near), small
    start_row = head * tokens
    lens = lax.dynamic_slice_in_dim(lengths.reshape(-1), head * graphs, graphs, 0)
    partner = lax.dynamic_slice_in_dim(
        jnp.concatenate([pairing.reshape(-1)] * 2), head * graphs, graphs, 0
    )
    places = jnp.stack([place.outer, place.inner, place.far, core, 1 - core]).astype(jnp.int32)
    info = jnp.concatenate([places, lens, partner])
    table_rows = lax.dynamic_slice_in_dim(laplacian, head * graphs * NODE, graphs * NODE, 0)
    end_rows = lax.dynamic_slice_in_dim(endpoints, start_row, tokens, 0)
    ident_rows = identifiers(table_rows, end_rows)
    embedded = lax.dynamic_slice_in_dim(features, start_row, tokens, 0).astype(F32)
    embedded = embedded + nn(ident_rows, ident_full)
    normed_one = (normalize(embedded)[0] * gains[GAIN]).astype(BF)

    last_others = place.to_core(last)
    if aligned:
        mine, saved_mine = attend(info, 3, normed_one, [near, last], True)
    else:
        packs = stack_pieces(place, near, last)
        mine, saved_mine = attend(info, 3, normed_one, [packs], True)
    normed_turned = saved_mine[4]
    heads_mine = saved_mine[2]
    ffn_pieces = place.pieces_of(ffn_own, ffn_next, after(ffn_last, heads_mine))
    if aligned:
        others, saved_others = attend(info, 4, normed_one, [near_others, last_others], False)
    else:
        others, saved_others = attend(info, 4, normed_one, [place.to_core(packs)], False)
    ffn_mine = place.whole(ffn_pieces).reshape(D, -1)
    ffn_other = place.to_core(ffn_mine)
    middle, slope, payload, w_up, w_down = forward_rest(
        info,
        embedded,
        gains,
        ffn_mine,
        ffn_other,
        [heads_mine, saved_others[2]],
        [mine, others],
    )

    own_row = (dp * heads + head) * graphs
    if place.n * GRAPHS_DEV <= 128:
        first = place.outer_list(payload)
        first = jnp.stack([first, place.mixed(first, 0)])
        third = place.mixed(first, 1)
        total_loss, d_out, d_hidden, d_rows_low, hidden_sums, gain_three = contrast(
            info, [first, third, place.to_core(first), place.to_core(third)], gains, w_down
        )
        total_loss = total_loss[0, 0]
    else:
        everyone = place.gather_all(payload).reshape(place.n, 2, GRAPHS_DEV, -1)
        total_loss, d_out, d_hidden, d_rows_low, hidden_sums, gain_three = contrast_plain(
            everyone, gains, w_down, own_row, graphs
        )

    own_column = (dp * heads + head) * own_columns
    d_columns = lax.dynamic_slice_in_dim(d_rows_low, own_column, own_columns, 1)
    grad_down = tn(d_columns, hidden_sums)
    (d_middle, grad_up, gain_two), augs, grad_outs = ffn_back(
        info,
        middle,
        slope,
        d_out,
        d_hidden,
        gains,
        w_up,
        [saved_mine[2], saved_others[2]],
        [saved_mine[3], saved_others[3]],
        [mine, others],
    )
    up_sent, up_kept = split_core(place, grad_up)
    up_came = place.to_core(up_sent)
    grad_others, d_others = attend_back(
        normed_turned, saved_others, augs[1], grad_outs[1], 0, 1, heads
    )
    came = place.to_core(grad_others)
    back = functools.partial(attend_back, normed_turned, saved_mine)
    aug = after(augs[0], grad_others)
    grad_even, d_even = back(aug, grad_outs[0], 0, 2, heads // 2)
    even = fold_pieces(place, [grad_even[0], grad_even[1]], [came[0], came[2]], (up_kept, up_came))
    even_kept, even_sent = place.fold_far(even)
    even_came = place.mixed(even_sent, 1)
    more = ([info, came], place.outs) if aligned else ()
    grad_odd, d_odd = back(after(aug, even_sent), grad_outs[0], 1, 2, heads // 2, *more)
    even_kept, even_sent = place.fold_near(even_kept, after(even_came, grad_odd), BF)
    if aligned:
        odd = [[v[0], v[1]] for v in grad_odd]
    else:
        odd = fold_pieces(place, [grad_odd[0], grad_odd[1]], [came[1], came[3]], None)
    odd_kept, odd_sent = place.fold_far(odd)
    odd_came = place.mixed(odd_sent, 1)
    even_came = place.mixed(even_sent, 0)
    d_normed = first_sum([after(d_others, odd_sent)], ((0, (0, 1, 2, 3)),), [others])
    odd_kept, odd_sent = place.fold_near(odd_kept, odd_came, BF)
    odd_sent = after(odd_sent, even_came)
    odd_came = place.mixed(odd_sent, 0)
    even = place.fold_outer(even_kept, even_came, BF)
    rows = first_back(
        embedded, d_middle, ident_rows, gains, d_normed, d_even, after(d_odd, odd_sent), mine
    )
    rows = after(rows, even, odd_came)
    odd = place.fold_outer(odd_kept, odd_came, BF)
    gain_rows = jnp.stack([jnp.sum(rows[2 * LAP :], axis=0), jnp.sum(gain_two, axis=0)])
    rows = jnp.concatenate([rows[: 2 * LAP], gain_rows], axis=0)
    row_count = rows.shape[0]
    rows = rows.T.reshape(devices, own_columns * row_count)
    rows = jnp.sum(lax.all_to_all(rows, ("dp", "head"), 0, 0, tiled=True), axis=0)
    rows = rows.reshape(own_columns, row_count)
    own_gains = lax.dynamic_slice_in_dim(gain_three, own_column, own_columns, 1)
    norm_parts = lax.all_to_all(
        squares([even, odd, grad_down, rows, own_gains], devices),
        ("dp", "head"),
        0,
        0,
        tiled=True,
    )
    own_half, other_half = even[:shard_rows], place.to_core(odd)
    halves = [place.by_core(own_half, other_half), place.by_core(other_half, own_half)]
    columns = lambda j: jnp.concatenate([v[:, j * SW : (j + 1) * SW] for v in halves], axis=1)
    grad_up = even[shard_rows:].reshape(2, own_columns, PACK)
    grads = (
        rows[:, : 2 * LAP],
        jnp.stack([columns(0), columns(1), columns(2)]),
        columns(3).T,
        jnp.stack([jnp.concatenate([grad_up[0], grad_up[1]], axis=1), grad_down]),
        jnp.concatenate([rows[:, 2 * LAP :].T, own_gains], axis=0),
    )
    turns = (lambda v: v.T, lambda v: v.transpose(1, 0, 2)) + (lambda v: v,) * 3
    state = [
        [turn(v) for turn, v in zip(turns, kind)]
        for kind in (
            (ident_weight, qkv_weight, out_weight, ffn_weight, norm_gains),
            (ident_first, qkv_first, out_first, ffn_first, gains_first),
            (ident_second, qkv_second, out_second, ffn_second, gains_second),
        )
    ]
    grad_norm, results = update(norm_parts, grads, state)
    return (grad_norm[0, 0], total_loss) + tuple(
        turn(v) for kind in results for turn, v in zip(turns, kind)
    )


def solution(mesh):
    both = P(None, ("dp", "head"))
    weights = (both, P("dp", None, "head"), P("head", "dp"), P(None, ("dp", "head"), None), both)
    in_specs = (P("dp", None),) * 5 + weights * 3
    out_specs = (P(), P()) + weights * 3
    return jax.shard_map(
        per_device, mesh=mesh, in_specs=in_specs, out_specs=out_specs, check_vma=False
    )
```

```python
import functools

import jax
import jax.numpy as jnp
from jax import lax
from jax.experimental import pallas as pl
from jax.experimental.pallas import tpu as pltpu
from jax.sharding import PartitionSpec as P

D = 768
HEAD_DIM = 24
LAP = 16
LEN = 128
NODE = 32
STEPS = 3
GRAPHS_DEV = 16
GAIN = 2 * LAP

HIGHEST = lax.Precision.HIGHEST
NORM_EPS = 1e-05
CLIP_AT = 5.0
STEP_RATES = (0.08, 0.02, 0.15, 0.02, 0.5)
BETA_ONE = 0.5
BETA_TWO = 0.5
DECAY = 0.01
ADAM_EPS = 1e-08
MASKED = -1e30

BF = jnp.bfloat16
F32 = jnp.float32
SUB = 4
SW = SUB * HEAD_DIM
PACK = 4 * SW
V_AT = 128 - SW
SCALE = HEAD_DIM ** (-0.5)
LENS = 5
VMEM_LIMIT = 49 * 2**20


def nn(a, b):
    return lax.dot_general(a, b, (((1,), (0,)), ((), ())), preferred_element_type=F32)


def nt(a, b):
    return lax.dot_general(a, b, (((1,), (1,)), ((), ())), preferred_element_type=F32)


def tn(a, b):
    return lax.dot_general(a, b, (((0,), (0,)), ((), ())), preferred_element_type=F32)


def lanes():
    return lax.broadcasted_iota(jnp.int32, (1, 128), 1)


def head_lanes(h, at):
    lane = lanes()
    return (lane >= at + h * HEAD_DIM) & (lane < at + (h + 1) * HEAD_DIM)


def by_head(v, at):
    zero = jnp.zeros_like(v)
    return jnp.concatenate([jnp.where(head_lanes(h, at), v, zero) for h in range(SUB)], axis=0)


def stack_heads(v):
    return jnp.concatenate([v[:, h * LEN : (h + 1) * LEN] for h in range(SUB)], axis=0)


def attend_kernel(info_ref, x_ref, *refs, graphs, whole, turn, owner):
    refs, turned = (refs[:-1], refs[-1:]) if turn else (refs, ())
    if whole:
        w_ref, qkv_ref, p_ref, o_ref, rinv_ref = refs
    else:
        first_ref, third_ref, w_ref, qkv_ref, p_ref, o_ref, rinv_ref = refs
        outs, rows = first_ref.shape[1], first_ref.shape[3]
        far, head = pl.program_id(0) // 2, pl.program_id(0) % 2
        outer, inner, gatherer = info_ref[0], info_ref[1], info_ref[owner]
        for i in range(2):
            in_first = (far == 0) if i == 0 else (far == 0) & (gatherer == 0)
            in_first = in_first | ((far == 1) & (gatherer == 1) & (i == 0))
            at = jnp.where(in_first, jnp.where(far + i == 0, 0, 1), jnp.where(far + i == 2, 1, 0))

            def place(source, at=at, i=i):
                for o in range(outs):
                    row = (lax.rem(outer + outs - o, outs) * 2 + (inner + i) % 2) * rows
                    w_ref[0, pl.ds(pl.multiple_of(row, rows), rows), :] = source[at, o, head]

            @pl.when(in_first)
            def _(place=place):
                place(first_ref)

            @pl.when(jnp.logical_not(in_first))
            def _(place=place):
                place(third_ref)

    if turned:

        @pl.when(pl.program_id(0) == 0)
        def _():
            turned[0][...] = x_ref[...].T

    y = nn(x_ref[...], w_ref[0])
    qkv_ref[0, 0] = y[:, :128].astype(BF)
    qkv_ref[0, 1] = pltpu.roll(y, PACK - SW, 1)[:, :128].astype(BF)
    qkv_ref[0, 2] = pltpu.roll(y, SW, 1)[:, 256:].astype(BF)
    col = lanes()
    ones = by_head(jnp.ones((LEN, 128), BF), V_AT)
    for g in range(graphs):
        rows = slice(g * LEN, (g + 1) * LEN)
        query, keys, values = qkv_ref[0, 0, rows, :], qkv_ref[0, 1, rows, :], qkv_ref[0, 2, rows, :]
        live = col < info_ref[LENS + g]
        scores = nt(query, by_head(keys, 0))
        parts = []
        for h in range(SUB):
            own = jnp.where(live, scores[:, h * LEN : (h + 1) * LEN] * SCALE, MASKED)
            parts.append(jnp.exp(own - jnp.max(own, axis=1, keepdims=True)).astype(BF))
        expo = jnp.concatenate(parts, axis=1)
        both = nn(expo, jnp.concatenate([by_head(values, V_AT), ones], axis=1))
        rinv = jnp.where(col >= V_AT, 1.0 / both[:, 128:], 0.0)
        p_ref[0, rows, :] = expo
        rinv_ref[0, rows, :] = rinv
        o_ref[0, rows, :] = jnp.where(col >= V_AT, both[:, :128] * rinv, 0.0).astype(BF)


def attend(info, owner, x, pieces, turn):
    tokens = x.shape[0]
    groups = 4
    whole = len(pieces) == 1
    block = lambda *tail: pl.BlockSpec((1,) + tail, lambda i: (i,) + (0,) * len(tail))
    full = lambda a: pl.BlockSpec(a.shape, lambda i: (0,) * a.ndim)
    out_specs = [block(3, tokens, 128), block(tokens, 512), block(tokens, 128), block(tokens, 128)]
    out_shape = [
        jax.ShapeDtypeStruct((groups, 3, tokens, 128), BF),
        jax.ShapeDtypeStruct((groups, tokens, 512), BF),
        jax.ShapeDtypeStruct((groups, tokens, 128), BF),
        jax.ShapeDtypeStruct((groups, tokens, 128), F32),
    ]
    if not whole:
        out_specs = [block(D, PACK)] + out_specs
        out_shape = [jax.ShapeDtypeStruct((groups, D, PACK), BF)] + out_shape
    if turn:
        out_specs = out_specs + [pl.BlockSpec((D, tokens), lambda i: (0, 0))]
        out_shape = out_shape + [jax.ShapeDtypeStruct((D, tokens), BF)]
    result = pl.pallas_call(
        functools.partial(attend_kernel, graphs=tokens // LEN, whole=whole, turn=turn, owner=owner),
        grid=(groups,),
        in_specs=[pl.BlockSpec(memory_space=pltpu.SMEM)]
        + [full(x)]
        + ([block(D, PACK)] if whole else [full(a) for a in pieces]),
        out_specs=out_specs,
        out_shape=out_shape,
        compiler_params=pltpu.CompilerParams(vmem_limit_bytes=VMEM_LIMIT),
        cost_estimate=pl.CostEstimate(
            flops=groups * 2_500_000_000, bytes_accessed=groups * 3_000_000, transcendentals=0
        ),
        name="attend",
    )(info, x, *pieces)
    return (pieces[0], result) if whole else (result[0], result[1:])


def attend_back_kernel(xt_ref, qkv_ref, p_ref, aug_ref, go_ref, *refs, graphs):
    *more, g_ref, d_ref = refs
    lane = lanes()
    for g in range(graphs):
        rows = slice(g * LEN, (g + 1) * LEN)
        query, keys, values = qkv_ref[0, 0, rows, :], qkv_ref[0, 1, rows, :], qkv_ref[0, 2, rows, :]
        d_rows, expo = aug_ref[0, rows, :], p_ref[0, rows, :]
        one, zero = jnp.ones_like(values), jnp.zeros_like(values)
        spread = jnp.concatenate(
            [
                jnp.where(
                    head_lanes(h, V_AT), values, jnp.where((lane == h) | (lane == SUB + h), one, zero)
                )
                for h in range(SUB)
            ],
            axis=0,
        )
        d_scores = (expo.astype(F32) * nt(d_rows, spread)).astype(BF)
        d_query = nn(d_scores, by_head(keys, 0)) * SCALE
        d_keys = tn(stack_heads(d_scores), by_head(query, 0)) * SCALE
        d_values = tn(stack_heads(expo), by_head(d_rows, V_AT))
        rolled_keys, rolled_values = pltpu.roll(d_keys, SW, 1), pltpu.roll(d_values, V_AT, 1)
        d_ref[0, rows, 0:128] = jnp.where(lane < SW, d_query, rolled_keys).astype(BF)
        d_ref[0, rows, 128:256] = jnp.where(lane < 64, rolled_keys, rolled_values).astype(BF)
        d_ref[0, rows, 256:384] = jnp.where(lane < V_AT, rolled_values, 0.0).astype(BF)
    grad = nn(xt_ref[...], d_ref[0])
    end = jnp.where(lane < V_AT, grad[:, 256:384], go_ref[0].astype(F32))
    if not more:
        g_ref[0, :, 0:256] = grad[:, 0:256].astype(BF)
        g_ref[0, :, 256:384] = end.astype(BF)
        return
    info_ref, came_ref = more
    outs, size = g_ref.shape[2], g_ref.shape[3]
    for o in range(outs):
        for i in range(2):
            rows = slice((o * 2 + i) * size, (o * 2 + i + 1) * size)
            at = lax.rem(i + info_ref[1], 2)
            came = came_ref[0, rows, :].astype(F32)
            g_ref[0, at, o, :, 0:256] = (grad[rows, 0:256] + came[:, 0:256]).astype(BF)
            g_ref[0, at, o, :, 256:384] = (end[rows] + came[:, 256:384]).astype(BF)


def attend_back(xt, saved, aug, grad_out, first, stride, groups, more=(), outs=0):
    qkv, expo = saved[:2]
    tokens = xt.shape[1]
    shape = (2, outs, D // (2 * outs), PACK) if more else (D, PACK)
    block = lambda *tail: pl.BlockSpec(
        (1,) + tail, lambda i: (first + i * stride,) + (0,) * len(tail)
    )
    out = lambda *tail: pl.BlockSpec((1,) + tail, lambda i: (i,) + (0,) * len(tail))
    return pl.pallas_call(
        functools.partial(attend_back_kernel, graphs=tokens // LEN),
        grid=(groups,),
        in_specs=[
            pl.BlockSpec(xt.shape, lambda i: (0, 0)),
            block(3, tokens, 128),
            block(tokens, 512),
            block(tokens, 128),
            block(D, 128),
        ]
        + ([pl.BlockSpec(memory_space=pltpu.SMEM), block(D, PACK)] if more else []),
        out_specs=[out(*shape), out(tokens, PACK)],
        out_shape=[
            jax.ShapeDtypeStruct((groups,) + shape, BF),
            jax.ShapeDtypeStruct((groups, tokens, PACK), BF),
        ],
        compiler_params=pltpu.CompilerParams(vmem_limit_bytes=VMEM_LIMIT),
        cost_estimate=pl.CostEstimate(
            flops=groups * 4_000_000_000, bytes_accessed=groups * 3_000_000, transcendentals=0
        ),
        name="attend_back",
    )(xt, qkv, expo, aug, grad_out, *more)


def first_sum_kernel(*refs, parts):
    d_refs, w_refs, out_ref = refs[: len(parts)], refs[len(parts) : -1], refs[-1]
    total = jnp.zeros(out_ref.shape, F32)
    for d_ref, (which, picks) in zip(d_refs, parts):
        for j in range(0, len(picks), 2):
            pair = range(j, min(j + 2, len(picks)))
            left = jnp.concatenate([d_ref[k] for k in pair], axis=1)
            right = jnp.concatenate([w_refs[which][picks[k]] for k in pair], axis=1)
            total = total + nt(left, right)
    out_ref[...] = total


def first_sum(ds, parts, weights):
    tokens = ds[0].shape[1]
    rows = LEN * min(2, tokens // LEN)
    full = lambda a: pl.BlockSpec(a.shape, lambda i: (0,) * a.ndim)
    return pl.pallas_call(
        functools.partial(first_sum_kernel, parts=parts),
        grid=(tokens // rows,),
        in_specs=[pl.BlockSpec((d.shape[0], rows, PACK), lambda i: (0, i, 0)) for d in ds]
        + [full(w) for w in weights],
        out_specs=pl.BlockSpec((rows, D), lambda i: (i, 0)),
        out_shape=jax.ShapeDtypeStruct((tokens, D), F32),
        compiler_params=pltpu.CompilerParams(vmem_limit_bytes=VMEM_LIMIT),
        cost_estimate=pl.CostEstimate(
            flops=7_000_000_000, bytes_accessed=12_000_000, transcendentals=0
        ),
        name="first_sum",
    )(*ds, *weights)


def first_back_kernel(
    e_ref, dmid_ref, ident_ref, gain_ref, sum_ref, even_ref, odd_ref, w_ref, out_ref, acc
):
    step, steps = pl.program_id(0), pl.num_programs(0)
    d_normed = sum_ref[...]
    for at, d_ref in enumerate((even_ref, odd_ref)):
        left = jnp.concatenate([d_ref[0], d_ref[1]], axis=1)
        d_normed = d_normed + nt(left, jnp.concatenate([w_ref[at], w_ref[at + 2]], axis=1))
    xhat, rstd = normalize(e_ref[...])
    d_emb = dmid_ref[...] + norm_back(d_normed, xhat, rstd, gain_ref[GAIN : GAIN + 1, :])
    part = tn(ident_ref[...], d_emb.astype(BF))
    part_gain = jnp.sum((d_normed * xhat).reshape(-1, 8, D), axis=0)

    @pl.when(step == 0)
    def _():
        acc[0 : 2 * LAP, :] = part
        acc[2 * LAP :, :] = part_gain

    @pl.when(step > 0)
    def _():
        acc[0 : 2 * LAP, :] += part
        acc[2 * LAP :, :] += part_gain

    @pl.when(step == steps - 1)
    def _():
        out_ref[...] = acc[...]


def first_back(embedded, d_middle, ident_rows, gains, total, d_even, d_odd, weights):
    tokens = embedded.shape[0]
    rows = LEN * min(2, tokens // LEN)
    full = lambda a: pl.BlockSpec(a.shape, lambda i: (0,) * a.ndim)
    tile = pl.BlockSpec((rows, D), lambda i: (i, 0))
    return pl.pallas_call(
        first_back_kernel,
        grid=(tokens // rows,),
        in_specs=[tile, tile, pl.BlockSpec((rows, 2 * LAP), lambda i: (i, 0)), full(gains), tile]
        + [pl.BlockSpec((2, rows, PACK), lambda i: (0, i, 0))] * 2
        + [full(weights)],
        out_specs=pl.BlockSpec((2 * LAP + 8, D), lambda i: (0, 0)),
        out_shape=jax.ShapeDtypeStruct((2 * LAP + 8, D), F32),
        scratch_shapes=[pltpu.VMEM((2 * LAP + 8, D), F32)],
        compiler_params=pltpu.CompilerParams(vmem_limit_bytes=VMEM_LIMIT),
        cost_estimate=pl.CostEstimate(
            flops=4_000_000_000, bytes_accessed=10_000_000, transcendentals=0
        ),
        name="first_back",
    )(embedded, d_middle, ident_rows, gains, total, d_even, d_odd, weights)


def normal_parts(x):
    falling = jnp.exp(-0.5 * x * x)
    t = 1.0 / (1.0 + (0.3275911 * 0.5**0.5) * jnp.abs(x))
    tail = 0.5 * 1.061405429
    for c in (-1.453152027, 1.421413741, -0.284496736, 0.254829592):
        tail = tail * t + 0.5 * c
    tail = tail * t * falling
    return jnp.where(x < 0.0, tail, 1.0 - tail), 0.3989422804014327 * falling


def normalize(values):
    centred = values - jnp.mean(values, axis=-1, keepdims=True)
    spread = jnp.mean(centred * centred, axis=-1, keepdims=True)
    rstd = lax.rsqrt(spread + NORM_EPS)
    return centred * rstd, rstd


def two_parts(v):
    high = v.astype(BF)
    return high, (v - high.astype(F32)).astype(BF)


def forward_kernel(
    info_ref, e_ref, gain_ref, ffn_ref, other_ref, *refs, tile_graphs, waves, groups
):
    o_refs, w_refs = refs[:waves], refs[waves : 2 * waves]
    mid_ref, slope_ref, pay_ref, up_ref, down_ref, hsum, msum = refs[2 * waves :]
    step, steps = pl.program_id(0), pl.num_programs(0)
    core = info_ref[3]

    @pl.when((step == 0) & (core == 0))
    def _():
        up_ref[...] = ffn_ref[...]
        down_ref[...] = other_ref[...]

    @pl.when((step == 0) & (core != 0))
    def _():
        up_ref[...] = other_ref[...]
        down_ref[...] = ffn_ref[...]

    middle = e_ref[...]
    for wave in range(waves):
        left = jnp.concatenate([o_refs[wave][j] for j in range(groups)], axis=1)
        right = jnp.concatenate([w_refs[wave][j][:, 256:] for j in range(groups)], axis=1)
        middle = middle + nt(left, right)
    mid_ref[...] = middle
    xhat, _ = normalize(middle)
    up = nn((xhat * gain_ref[GAIN + 1 : GAIN + 2, :]).astype(BF), up_ref[...])
    cdf, density = normal_parts(up)
    hidden = (up * cdf).astype(BF).astype(F32)
    slope_ref[...] = (cdf + up * density).astype(BF)
    place = lax.broadcasted_iota(jnp.int32, (LEN, 1), 0)
    for j in range(tile_graphs):
        g = step * tile_graphs + j
        live = place < info_ref[LENS + g]
        rows = slice(j * LEN, (j + 1) * LEN)
        hsum[pl.ds(g, 1), :] = jnp.sum(jnp.where(live, hidden[rows], 0.0), axis=0, keepdims=True)
        msum[pl.ds(g, 1), :] = jnp.sum(jnp.where(live, middle[rows], 0.0), axis=0, keepdims=True)

    @pl.when(step == steps - 1)
    def _():
        graphs = hsum.shape[0]
        high, low = two_parts(hsum[...])
        which = lax.broadcasted_iota(jnp.int32, (graphs, 1), 0)
        length, partner = jnp.ones((graphs, 1), F32), jnp.zeros((graphs, 1), F32)
        for g in range(graphs):
            length = jnp.where(which == g, info_ref[LENS + g].astype(F32), length)
            partner = jnp.where(which == g, info_ref[LENS + graphs + g].astype(F32), partner)
        pooled = (msum[...] + (nt(high, down_ref[...]) + nt(low, down_ref[...]))) / length
        xhat_pool, rstd = normalize(pooled)
        high, low = two_parts(xhat_pool)
        pay_ref[:, 0:D] = high
        pay_ref[:, D : 2 * D] = low
        pay_ref[:, 2 * D : 3 * D] = hsum[...].astype(BF)
        lane = lanes()
        stats = jnp.zeros((graphs, 128), F32)
        for at, value in enumerate(two_parts(rstd) + two_parts(1.0 / length) + (partner,)):
            stats = jnp.where(lane == at, value.astype(F32), stats)
        pay_ref[:, 3 * D :] = stats.astype(BF)


def forward_rest(info, embedded, gains, w_up, w_down, outs, weights):
    tokens = embedded.shape[0]
    graphs = tokens // LEN
    tile_graphs = min(2, graphs)
    rows = tile_graphs * LEN
    waves, groups = len(outs), outs[0].shape[0]
    full = lambda a: pl.BlockSpec(a.shape, lambda i: (0,) * a.ndim)
    tile = pl.BlockSpec((rows, D), lambda i: (i, 0))
    return pl.pallas_call(
        functools.partial(forward_kernel, tile_graphs=tile_graphs, waves=waves, groups=groups),
        grid=(tokens // rows,),
        in_specs=[pl.BlockSpec(memory_space=pltpu.SMEM)]
        + [tile, full(gains), full(w_up), full(w_down)]
        + [pl.BlockSpec((groups, rows, 128), lambda i: (0, i, 0)) for _ in outs]
        + [full(w) for w in weights],
        out_specs=[
            tile,
            tile,
            pl.BlockSpec((graphs, 3 * D + 128), lambda i: (0, 0)),
            full(w_up),
            full(w_down),
        ],
        out_shape=[
            jax.ShapeDtypeStruct((tokens, D), F32),
            jax.ShapeDtypeStruct((tokens, D), BF),
            jax.ShapeDtypeStruct((graphs, 3 * D + 128), BF),
            jax.ShapeDtypeStruct(w_up.shape, BF),
            jax.ShapeDtypeStruct(w_down.shape, BF),
        ],
        scratch_shapes=[pltpu.VMEM((graphs, D), F32), pltpu.VMEM((graphs, D), F32)],
        compiler_params=pltpu.CompilerParams(vmem_limit_bytes=VMEM_LIMIT),
        cost_estimate=pl.CostEstimate(
            flops=10_000_000_000, bytes_accessed=20_000_000, transcendentals=0
        ),
        name="forward_rest",
    )(info, embedded, gains, w_up, w_down, *outs, *weights)


def norm_back(d_normed, xhat, rstd, gain):
    d_hat = d_normed * gain
    return rstd * (
        d_hat
        - jnp.mean(d_hat, axis=-1, keepdims=True)
        - xhat * jnp.mean(d_hat * xhat, axis=-1, keepdims=True)
    )


def ffn_back_kernel(
    info_ref, mid_ref, slope_ref, dout_ref, dhid_ref, gain_ref, up_ref, *refs, tile_graphs, groups
):
    o_refs, rinv_refs, w_refs = refs[0:2], refs[2:4], refs[4:6]
    dmid_ref, grad_ref, dgain_ref = refs[6:9]
    aug_refs, go_refs = refs[9:11], refs[11:13]
    grad, dgain, grad_out = refs[13:]
    step, steps = pl.program_id(0), pl.num_programs(0)
    xhat, rstd = normalize(mid_ref[...])
    gain = gain_ref[GAIN + 1 : GAIN + 2, :]
    place = lax.broadcasted_iota(jnp.int32, (LEN, 1), 0)
    d_up, d_out = [], []
    for j in range(tile_graphs):
        g = step * tile_graphs + j
        live = place < info_ref[LENS + g]
        rows = slice(j * LEN, (j + 1) * LEN)
        d_hidden = jnp.where(live, dhid_ref[pl.ds(g, 1), :], 0.0)
        d_up.append((slope_ref[rows, :].astype(F32) * d_hidden).astype(BF))
        d_out.append(jnp.where(live, dout_ref[pl.ds(g, 1), :], 0.0))
    d_up, d_out = jnp.concatenate(d_up, axis=0), jnp.concatenate(d_out, axis=0)
    d_normed = nt(d_up, up_ref[...])
    d_mid = d_out + norm_back(d_normed, xhat, rstd, gain)
    dmid_ref[...] = d_mid
    d_attn = d_mid.astype(BF)
    d_turned = d_attn.T
    part = tn((xhat * gain).astype(BF), d_up)
    part_gain = jnp.sum((d_normed * xhat).reshape(-1, 8, D), axis=0)

    lane = lanes()
    row = lax.broadcasted_iota(jnp.int32, (256, 128), 0) & 127
    column = lax.broadcasted_iota(jnp.int32, (256, 128), 1)
    pick = jnp.zeros((256, 128), BF)
    for h in range(SUB):
        inside = (row >= V_AT + h * HEAD_DIM) & (row < V_AT + (h + 1) * HEAD_DIM)
        pick = jnp.where(inside & ((column == h) | (column == SUB + h)), jnp.ones_like(pick), pick)
    parts_out = []
    for half in range(2):
        d_heads = nn(d_attn, jnp.concatenate([w_refs[half][j] for j in range(groups)], axis=1))
        for j in range(groups):
            d_over = d_heads[:, j * 128 : (j + 1) * 128] * rinv_refs[half][j]
            d_over = jnp.where(lane >= V_AT, d_over, 0.0)
            terms = d_over * o_refs[half][j].astype(F32)
            delta = nn(jnp.concatenate(two_parts(terms), axis=1), pick)
            rounded = delta.astype(BF).astype(F32)
            aug_refs[half][j] = jnp.where(
                lane >= V_AT, d_over, jnp.where(lane < SUB, -rounded, rounded - delta)
            ).astype(BF)
        parts_out.append(
            nn(d_turned, jnp.concatenate([o_refs[half][j] for j in range(groups)], axis=1))
        )

    @pl.when(step == 0)
    def _():
        grad[...] = part
        dgain[...] = part_gain
        for half in range(2):
            grad_out[half] = parts_out[half]

    @pl.when(step > 0)
    def _():
        grad[...] += part
        dgain[...] += part_gain
        for half in range(2):
            grad_out[half] += parts_out[half]

    @pl.when(step == steps - 1)
    def _():
        for half in range(2):
            grad_ref[half] = grad[:, half * PACK : (half + 1) * PACK].astype(BF)
            for j in range(groups):
                go_refs[half][j] = grad_out[half, :, j * 128 : (j + 1) * 128].astype(BF)
        dgain_ref[...] = dgain[...]


def ffn_back(info, middle, slope, d_out, d_hidden, gains, w_up, outs, rinvs, weights):
    tokens = middle.shape[0]
    tile_graphs = min(2, tokens // LEN)
    rows = tile_graphs * LEN
    groups = outs[0].shape[0]
    full = lambda a: pl.BlockSpec(a.shape, lambda i: (0,) * a.ndim)
    tile = pl.BlockSpec((rows, D), lambda i: (i, 0))
    sub_tile = pl.BlockSpec((groups, rows, 128), lambda i: (0, i, 0))
    result = pl.pallas_call(
        functools.partial(ffn_back_kernel, tile_graphs=tile_graphs, groups=groups),
        grid=(tokens // rows,),
        in_specs=[pl.BlockSpec(memory_space=pltpu.SMEM), tile, tile]
        + [full(a) for a in (d_out, d_hidden, gains, w_up)]
        + [sub_tile] * 4
        + [pl.BlockSpec((groups, D, 128), lambda i: (0, 0, 2))] * 2,
        out_specs=[
            tile,
            pl.BlockSpec((2, D, PACK), lambda i: (0, 0, 0)),
            pl.BlockSpec((8, D), lambda i: (0, 0)),
        ]
        + [sub_tile] * 2
        + [pl.BlockSpec((groups, D, 128), lambda i: (0, 0, 0))] * 2,
        out_shape=[
            jax.ShapeDtypeStruct((tokens, D), F32),
            jax.ShapeDtypeStruct((2, D, PACK), BF),
            jax.ShapeDtypeStruct((8, D), F32),
        ]
        + [jax.ShapeDtypeStruct((groups, tokens, 128), BF)] * 2
        + [jax.ShapeDtypeStruct((groups, D, 128), BF)] * 2,
        scratch_shapes=[
            pltpu.VMEM((D, D), F32),
            pltpu.VMEM((8, D), F32),
            pltpu.VMEM((2, D, groups * 128), F32),
        ],
        compiler_params=pltpu.CompilerParams(vmem_limit_bytes=VMEM_LIMIT),
        cost_estimate=pl.CostEstimate(
            flops=14_000_000_000, bytes_accessed=20_000_000, transcendentals=0
        ),
        name="ffn_back",
    )(info, middle, slope, d_out, d_hidden, gains, w_up, *outs, *rinvs, *weights)
    return result[:3], result[3:5], result[5:7]


def loss_kernel(
    info_ref, a1_ref, a3_ref, b1_ref, b3_ref, gain_ref, down_ref,
    loss_ref, dout_ref, dhid_ref, dlow_ref, hid_ref, dgain_ref, xhat, stats, rows_ref
):
    outs, graphs = a1_ref.shape[1], a1_ref.shape[2]
    outer, inner, far, core = (info_ref[i] for i in range(4))
    count = outs * 2 * GRAPHS_DEV
    place = lambda f, o, i, c: pl.multiple_of(
        f * count + (o * 2 + i) * GRAPHS_DEV + c * graphs, graphs
    )
    for owner, refs in ((core, (a1_ref, a3_ref)), (1 - core, (b1_ref, b3_ref))):
        for part, ref in enumerate(refs):
            for at in range(2):
                if part == at:
                    f, i = part, part
                else:
                    f, i = (owner, 1 - owner) if part == 0 else (1 - owner, owner)
                for o in range(outs):
                    values = ref[at, o].astype(F32)
                    row = place(
                        lax.rem(far + f, 2), lax.rem(outer + outs - o, outs), lax.rem(inner + i, 2), owner
                    )
                    rows = pl.ds(row, graphs)
                    xhat[rows, :] = values[:, 0:D] + values[:, D : 2 * D]
                    rows_ref[rows, :] = values[:, 2 * D : 3 * D]
                    stats[rows, :] = values[:, 3 * D :]
    hid_ref[...] = rows_ref[...].astype(BF)
    root = D**-0.5
    left, right = xhat[0:count, :] * gain_ref[GAIN + 2 : GAIN + 3, :], xhat[count:, :] * gain_ref[GAIN + 2 : GAIN + 3, :]
    exact = lambda a, b, dims: lax.dot_general(
        a, b, (dims, ((), ())), precision=HIGHEST, preferred_element_type=F32
    )
    logits = exact(left, right, ((1,), (1,))) * root
    row_top, col_top = jnp.max(logits, axis=1, keepdims=True), jnp.max(logits, axis=0, keepdims=True)
    row_expo, col_expo = jnp.exp(logits - row_top), jnp.exp(logits - col_top)
    row_sum, col_sum = jnp.sum(row_expo, axis=1, keepdims=True), jnp.sum(col_expo, axis=0, keepdims=True)
    row_id = lax.broadcasted_iota(jnp.int32, (count, count), 0)
    col_id = lax.broadcasted_iota(jnp.int32, (count, count), 1)
    slot = stats[0:count, 4:5].astype(jnp.int32)
    positive = jnp.where(col_id == (row_id & -GRAPHS_DEV) + slot, 1.0, 0.0)
    loss = (
        jnp.sum(row_top + jnp.log(row_sum), axis=0, keepdims=True)
        + jnp.sum(col_top + jnp.log(col_sum), axis=1, keepdims=True)
        - 2.0 * jnp.sum(jnp.sum(positive * logits, axis=1, keepdims=True), axis=0, keepdims=True)
    )
    loss_ref[...] = loss
    d_logits = row_expo / row_sum + col_expo / col_sum - 2.0 * positive
    rows_ref[0:count, :] = exact(d_logits, right, ((1,), (0,))) * root
    rows_ref[count:, :] = exact(d_logits, left, ((0,), (0,))) * root
    every = xhat[...]
    d_summary = rows_ref[...]
    dgain_ref[...] = jnp.sum(d_summary * every, axis=0, keepdims=True)
    rstd, share = stats[:, 0:1] + stats[:, 1:2], stats[:, 2:3] + stats[:, 3:4]
    d_rows = norm_back(d_summary, every, rstd, gain_ref[GAIN + 2 : GAIN + 3, :]) * share
    rows_ref[...] = d_rows
    dlow_ref[...] = d_rows.astype(BF)
    own = rows_ref[pl.ds(place(far, outer, inner, core), graphs), :]
    dout_ref[...] = own
    dhid_ref[...] = nn(own.astype(BF), down_ref[...])


def contrast(info, pieces, gains, w_down):
    outs, graphs = pieces[0].shape[1], pieces[0].shape[2]
    total = outs * 4 * GRAPHS_DEV
    return pl.pallas_call(
        loss_kernel,
        in_specs=[pl.BlockSpec(memory_space=pltpu.SMEM)]
        + [pl.BlockSpec(memory_space=pltpu.VMEM)] * 6,
        out_specs=[pl.BlockSpec(memory_space=pltpu.VMEM)] * 6,
        out_shape=[
            jax.ShapeDtypeStruct((1, 1), F32),
            jax.ShapeDtypeStruct((graphs, D), F32),
            jax.ShapeDtypeStruct((graphs, D), F32),
            jax.ShapeDtypeStruct((total, D), BF),
            jax.ShapeDtypeStruct((total, D), BF),
            jax.ShapeDtypeStruct((1, D), F32),
        ],
        scratch_shapes=[
            pltpu.VMEM((total, D), F32),
            pltpu.VMEM((total, 128), F32),
            pltpu.VMEM((total, D), F32),
        ],
        compiler_params=pltpu.CompilerParams(vmem_limit_bytes=24 * 2**20),
        cost_estimate=pl.CostEstimate(
            flops=3_000_000_000, bytes_accessed=4_000_000, transcendentals=0
        ),
        name="contrast",
    )(info, *pieces, gains, w_down)


def contrast_plain(everyone, gains, w_down, own_row, graphs):
    n = everyone.shape[0]
    stats = everyone[..., 3 * D :].astype(F32)
    xhat = everyone[..., :D].astype(F32) + everyone[..., D : 2 * D].astype(F32)
    hidden_sums = everyone[..., 2 * D : 3 * D].reshape(-1, D)
    rstd_pool = (stats[..., 0:1] + stats[..., 1:2]).reshape(-1, 1)
    share = (stats[..., 2:3] + stats[..., 3:4]).reshape(-1, 1)
    summaries = xhat * gains[GAIN + 2]
    left, right = summaries[:, 0].reshape(-1, D), summaries[:, 1].reshape(-1, D)
    root_width = D**0.5
    logits = jnp.dot(left, right.T, precision=HIGHEST) / root_width
    row_totals, col_totals = log_total(logits, 1), log_total(logits, 0)
    count = logits.shape[0]
    group = jnp.arange(count, dtype=jnp.int32) // GRAPHS_DEV
    partners = group * GRAPHS_DEV + stats[:, 0, :, 4].reshape(-1).astype(jnp.int32)
    positive = (partners[:, None] == jnp.arange(count, dtype=jnp.int32)[None, :]).astype(F32)
    total_loss = jnp.sum(row_totals) + jnp.sum(col_totals) - 2.0 * jnp.sum(positive * logits)
    d_logits = (
        jnp.exp(logits - row_totals[:, None])
        + jnp.exp(logits - col_totals[None, :])
        - 2.0 * positive
    )
    d_left = jnp.dot(d_logits, right, precision=HIGHEST) / root_width
    d_right = jnp.dot(d_logits.T, left, precision=HIGHEST) / root_width
    d_summary = jnp.stack(
        [d_left.reshape(n, GRAPHS_DEV, D), d_right.reshape(n, GRAPHS_DEV, D)], axis=1
    ).reshape(-1, D)
    xhat = xhat.reshape(-1, D)
    gain_three = jnp.sum(d_summary * xhat, axis=0, keepdims=True)
    d_rows = norm_back(d_summary, xhat, rstd_pool, gains[GAIN + 2]) * share
    d_out = lax.dynamic_slice_in_dim(d_rows, own_row, graphs, 0)
    d_hidden = nn(d_out.astype(BF), w_down)
    return total_loss, d_out, d_hidden, d_rows.astype(BF), hidden_sums, gain_three


class Place:
    def __init__(self):
        self.n, self.heads = lax.axis_size("dp"), lax.axis_size("head")
        self.outs = self.n // 2
        dp, head = lax.axis_index("dp"), lax.axis_index("head")
        self.dp, self.head = dp, head
        self.outer, self.inner, self.far, self.core = dp // 2, dp % 2, head // 2, head % 2

    def move(self, v, to):
        pairs = []
        for i in range(self.n * self.heads):
            outer, inner, far, core = i // 8, (i // 4) % 2, (i // 2) % 2, i % 2
            outer, inner, far, core = to(outer, inner, far, core)
            pairs.append((i, ((outer % self.outs * 2 + inner) * 2 + far) * 2 + core))
        return lax.ppermute(v, ("dp", "head"), pairs)

    def to_core(self, v):
        return self.move(v, lambda o, i, f, c: (o, i, f, 1 - c))

    def to_outer(self, v, by):
        return self.move(v, lambda o, i, f, c: (o + by, i, f, c))

    def mixed(self, v, turn):
        return self.move(
            v, lambda o, i, f, c: (o, 1 - i, f, c) if c == turn else (o, i, 1 - f, c)
        )

    def by_core(self, a, b):
        return jnp.where(self.core == 0, a, b)

    def gather_outer(self, v, *late):
        out = jnp.zeros((self.outs,) + v.shape, v.dtype)
        out = lax.dynamic_update_index_in_dim(out, v, self.outer, 0)
        for by in range(1, self.outs):
            out = lax.dynamic_update_index_in_dim(
                out, after(self.to_outer(v, by), *late), (self.outer - by) % self.outs, 0
            )
        return out

    def outer_list(self, v):
        return jnp.stack([v] + [self.to_outer(v, by) for by in range(1, self.outs)])

    def gather_pieces(self, v):
        return self.gather_near(self.gather_outer(v))

    def gather_near(self, own):
        return self.gather_last(own, self.mixed(own, 0))

    def gather_last(self, own, second):
        return self.pieces_of(own, second, self.mixed(jnp.stack([own, second]), 1))

    def pieces_of(self, own, second, third):
        return [
            [own, self.by_core(second, third[0])],
            [self.by_core(third[0], second), third[1]],
        ]

    def whole(self, pieces):
        rows = [
            [jnp.where(self.far == 0, pieces[f][i], pieces[1 - f][i]) for f in range(2)]
            for i in range(2)
        ]
        ordered = [
            [jnp.where(self.inner == 0, rows[i][f], rows[1 - i][f]) for f in range(2)]
            for i in range(2)
        ]
        return jnp.stack([jnp.stack(pair, axis=1) for pair in ordered], axis=1)

    def both_cores(self, v, axis):
        other = self.to_core(v)
        return jnp.stack([self.by_core(v, other), self.by_core(other, v)], axis=axis)

    def both_cores_of(self, own, sent):
        other = self.to_core(sent)
        return jnp.stack([self.by_core(own, other), self.by_core(other, own)])

    def gather_all(self, v):
        v = self.both_cores(self.whole(self.gather_pieces(v)), 3)
        return v.reshape((self.n, self.heads) + v.shape[4:])

    def fold_far(self, pieces):
        sent = jnp.stack([self.by_core(pieces[1][0], pieces[0][1]), pieces[1][1]])
        kept = jnp.stack([pieces[0][0], self.by_core(pieces[0][1], pieces[1][0])])
        return kept, sent

    def fold_near(self, kept, came, dtype):
        total = kept.astype(F32) + came.astype(F32)
        return total[0], total[1].astype(dtype)

    def fold_outer(self, total, dtype):
        total = total.astype(dtype)
        pick = lambda by: lax.dynamic_index_in_dim(
            total, (self.outer + by) % self.outs, 0, keepdims=False
        )
        result = pick(0).astype(F32)
        for by in range(1, self.outs):
            result = result + self.to_outer(pick(by), by).astype(F32)
        return result

    def total(self, v):
        v = jnp.broadcast_to(v, (self.n * self.heads, 128))
        return jnp.sum(lax.all_to_all(v, ("dp", "head"), 0, 0, tiled=True)[:, 0])

    def split_rows(self, v):
        v = v.reshape((self.outs, 2, -1) + v.shape[1:])
        return [
            lax.dynamic_index_in_dim(v, (self.inner + i) % 2, 1, keepdims=False) for i in range(2)
        ]


def tie(*values):
    return lax.optimization_barrier(values)


def after(value, *others):
    return lax.optimization_barrier((value,) + others)[0]


def log_total(values, axis):
    top = jnp.max(values, axis=axis, keepdims=True)
    return jnp.squeeze(top, axis) + jnp.log(jnp.sum(jnp.exp(values - top), axis=axis))


def identifiers(table, endpoints):
    graphs = endpoints.shape[0] // LEN
    nodes = table.reshape(graphs, NODE, LAP).astype(BF)
    picks = (
        endpoints.reshape(graphs, LEN, 2)[..., None] == jnp.arange(NODE, dtype=jnp.int32)
    ).astype(BF)
    found = jnp.einsum("glan,gnc->glac", picks, nodes, preferred_element_type=F32)
    return found.reshape(graphs * LEN, 2 * LAP).astype(BF)


def stack_pieces(place, near, last):
    pieces = place.pieces_of(near[0], near[1], last)
    packs = []
    for f in range(2):
        for c in range(2):
            rows = [
                jnp.where(place.inner == i, pieces[f][0][:, c], pieces[f][1][:, c]) for i in range(2)
            ]
            packs.append(jnp.stack(rows, axis=1).reshape(D, PACK))
    return jnp.stack(packs)


def split_core(place, grad_up):
    v = grad_up.reshape((2, place.outs, 2, 2, 2, -1, PACK))
    pick = lambda at: lax.dynamic_index_in_dim(v, at, 4, keepdims=False)
    return pick(1 - place.core), pick(place.core)


def fold_pieces(place, own, came, up):
    pieces = []
    for f in range(2):
        total = own[f].astype(F32) + came[f].astype(F32)
        pieces.append([v.astype(BF) for v in place.split_rows(total)])
    if up is None:
        return pieces
    total = (up[0].astype(F32) + up[1].astype(F32)).astype(BF)
    for f in range(2):
        part = lax.dynamic_index_in_dim(total, (place.far + f) % 2, 3, keepdims=False)
        for i in range(2):
            rows = lax.dynamic_index_in_dim(part, (place.inner + i) % 2, 2, keepdims=False)
            pieces[f][i] = jnp.concatenate([pieces[f][i], rows[0], rows[1]], axis=1)
    return pieces


def squares_kernel(*refs):
    *grad_refs, out_ref = refs
    total = jnp.zeros((1, 1), F32)
    for ref in grad_refs:
        v = ref[...]
        total = total + jnp.sum(jnp.sum(v * v, axis=0, keepdims=True), axis=1, keepdims=True)
    out_ref[...] = jnp.broadcast_to(total, out_ref.shape)


def squares(grads, devices):
    return pl.pallas_call(
        squares_kernel,
        out_shape=jax.ShapeDtypeStruct((devices, 128), F32),
        cost_estimate=pl.CostEstimate(flops=1_000_000, bytes_accessed=500_000, transcendentals=0),
        name="squares",
    )(*grads)


def update_kernel(parts_ref, *refs):
    count = len(STEP_RATES)
    grads, weights, firsts, seconds = (refs[k * count : (k + 1) * count] for k in range(4))
    norm_ref, refs = refs[4 * count], refs[4 * count + 1 :]
    new_weights, new_firsts, new_seconds = (refs[k * count : (k + 1) * count] for k in range(3))
    norm = jnp.sqrt(jnp.sum(parts_ref[...], axis=0, keepdims=True)[:, 0:1])
    norm_ref[...] = norm
    factor = CLIP_AT / jnp.maximum(norm, CLIP_AT)
    for k, rate in enumerate(STEP_RATES):
        for at in range(grads[k].shape[0]) if len(grads[k].shape) == 3 else (...,):
            weight = weights[k][at]
            clipped = grads[k][at] * factor
            first = BETA_ONE * firsts[k][at] + (1.0 - BETA_ONE) * clipped
            second = BETA_TWO * seconds[k][at] + (1.0 - BETA_TWO) * clipped * clipped
            first_hat = first / (1.0 - BETA_ONE**STEPS)
            second_hat = second / (1.0 - BETA_TWO**STEPS)
            new_weights[k][at] = weight - rate * (
                first_hat / (jnp.sqrt(second_hat) + ADAM_EPS) + DECAY * weight
            )
            new_firsts[k][at] = first
            new_seconds[k][at] = second


def update(norm_parts, grads, state):
    result = pl.pallas_call(
        update_kernel,
        out_shape=[jax.ShapeDtypeStruct((1, 1), F32)]
        + [jax.ShapeDtypeStruct(v.shape, F32) for kind in state for v in kind],
        cost_estimate=pl.CostEstimate(
            flops=5_000_000, bytes_accessed=6_000_000, transcendentals=0
        ),
        name="update",
    )(norm_parts, *grads, *(v for kind in state for v in kind))
    count = len(grads)
    return result[0], [result[1 + k * count : 1 + (k + 1) * count] for k in range(3)]


def per_device(
    features,
    laplacian,
    endpoints,
    lengths,
    pairing,
    ident_weight,
    qkv_weight,
    out_weight,
    ffn_weight,
    norm_gains,
    ident_first,
    qkv_first,
    out_first,
    ffn_first,
    gains_first,
    ident_second,
    qkv_second,
    out_second,
    ffn_second,
    gains_second,
):
    place = Place()
    heads, head, dp, core = place.heads, place.head, place.dp, place.core
    tokens = features.shape[0] // heads
    devices = place.n * heads
    graphs = tokens // LEN
    own_columns = norm_gains.shape[1]

    small = jnp.concatenate([ident_weight, norm_gains], axis=0)
    small_rows = small.shape[0]

    packed = [qkv_weight[:, 0], qkv_weight[:, 1], qkv_weight[:, 2], out_weight.T]
    shards = jnp.stack(
        [
            jnp.concatenate([m[:, s * SW : (s + 1) * SW] for m in packed], axis=1).astype(BF)
            for s in range(2)
        ]
    )
    pick = lambda v, at: lax.dynamic_index_in_dim(v, at, 0, keepdims=False)
    near = jnp.stack([pick(shards, core), place.to_core(pick(shards, 1 - core))])
    shard_rows = D // place.n
    aligned = shard_rows % 16 == 0
    near_own = (place.outer_list if aligned else place.gather_outer)(near)
    small = jnp.broadcast_to(after(small.reshape(1, -1), near_own), (devices, small.size))
    small = lax.all_to_all(small, ("dp", "head"), 0, 0, tiled=True)
    near = jnp.stack([near_own, place.mixed(near_own, 0)])
    last = place.mixed(near, 1)
    ffn = after(ffn_weight.astype(BF), near_own)
    small = after(small, near)
    ffn_near = place.both_cores_of(pick(ffn, core), pick(ffn, 1 - core))
    ffn_own = place.gather_outer(ffn_near, near)
    near_others = place.to_core(near)
    ffn_next = place.mixed(ffn_own, 0)
    ffn_last = place.mixed(jnp.stack([ffn_own, ffn_next]), 1)
    small = small.reshape(-1, small_rows, own_columns).transpose(1, 0, 2).reshape(small_rows, D)
    ident_full, gains = after(small[: 2 * LAP].astype(BF), near), small
    start_row = head * tokens
    lens = lax.dynamic_slice_in_dim(lengths.reshape(-1), head * graphs, graphs, 0)
    partner = lax.dynamic_slice_in_dim(
        jnp.concatenate([pairing.reshape(-1)] * 2), head * graphs, graphs, 0
    )
    places = jnp.stack([place.outer, place.inner, place.far, core, 1 - core]).astype(jnp.int32)
    info = jnp.concatenate([places, lens, partner])
    table_rows = lax.dynamic_slice_in_dim(laplacian, head * graphs * NODE, graphs * NODE, 0)
    end_rows = lax.dynamic_slice_in_dim(endpoints, start_row, tokens, 0)
    ident_rows = identifiers(table_rows, end_rows)
    embedded = lax.dynamic_slice_in_dim(features, start_row, tokens, 0).astype(F32)
    embedded = embedded + nn(ident_rows, ident_full)
    normed_one = (normalize(embedded)[0] * gains[GAIN]).astype(BF)

    last_others = place.to_core(last)
    if aligned:
        mine, saved_mine = attend(info, 3, normed_one, [near, last], True)
    else:
        packs = stack_pieces(place, near, last)
        mine, saved_mine = attend(info, 3, normed_one, [packs], True)
    normed_turned = saved_mine[4]
    heads_mine = saved_mine[2]
    ffn_pieces = place.pieces_of(ffn_own, ffn_next, after(ffn_last, heads_mine))
    if aligned:
        others, saved_others = attend(info, 4, normed_one, [near_others, last_others], False)
    else:
        others, saved_others = attend(info, 4, normed_one, [place.to_core(packs)], False)
    ffn_mine = place.whole(ffn_pieces).reshape(D, -1)
    ffn_other = place.to_core(ffn_mine)
    middle, slope, payload, w_up, w_down = forward_rest(
        info,
        embedded,
        gains,
        ffn_mine,
        ffn_other,
        [heads_mine, saved_others[2]],
        [mine, others],
    )

    own_row = (dp * heads + head) * graphs
    if place.n * GRAPHS_DEV <= 128:
        first = place.outer_list(payload)
        first = jnp.stack([first, place.mixed(first, 0)])
        third = place.mixed(first, 1)
        total_loss, d_out, d_hidden, d_rows_low, hidden_sums, gain_three = contrast(
            info, [first, third, place.to_core(first), place.to_core(third)], gains, w_down
        )
        total_loss = total_loss[0, 0]
    else:
        everyone = place.gather_all(payload).reshape(place.n, 2, GRAPHS_DEV, -1)
        total_loss, d_out, d_hidden, d_rows_low, hidden_sums, gain_three = contrast_plain(
            everyone, gains, w_down, own_row, graphs
        )

    own_column = (dp * heads + head) * own_columns
    d_columns = lax.dynamic_slice_in_dim(d_rows_low, own_column, own_columns, 1)
    grad_down = tn(d_columns, hidden_sums)
    (d_middle, grad_up, gain_two), augs, grad_outs = ffn_back(
        info,
        middle,
        slope,
        d_out,
        d_hidden,
        gains,
        w_up,
        [saved_mine[2], saved_others[2]],
        [saved_mine[3], saved_others[3]],
        [mine, others],
    )
    up_sent, up_kept = split_core(place, grad_up)
    up_came = place.to_core(up_sent)
    grad_others, d_others = attend_back(
        normed_turned, saved_others, augs[1], grad_outs[1], 0, 1, heads
    )
    came = place.to_core(grad_others)
    back = functools.partial(attend_back, normed_turned, saved_mine)
    aug = after(augs[0], grad_others)
    grad_even, d_even = back(aug, grad_outs[0], 0, 2, heads // 2)
    even = fold_pieces(place, [grad_even[0], grad_even[1]], [came[0], came[2]], (up_kept, up_came))
    even_kept, even_sent = place.fold_far(even)
    even_came = place.mixed(even_sent, 1)
    more = ([info, came], place.outs) if aligned else ()
    grad_odd, d_odd = back(after(aug, even_sent), grad_outs[0], 1, 2, heads // 2, *more)
    even_kept, even_sent = place.fold_near(even_kept, after(even_came, grad_odd), BF)
    if aligned:
        odd = [[v[0], v[1]] for v in grad_odd]
    else:
        odd = fold_pieces(place, [grad_odd[0], grad_odd[1]], [came[1], came[3]], None)
    odd_kept, odd_sent = place.fold_far(odd)
    odd_came = place.mixed(odd_sent, 1)
    even_came = place.mixed(even_sent, 0)
    d_normed = first_sum([after(d_others, odd_sent)], ((0, (0, 1, 2, 3)),), [others])
    odd_kept, odd_sent = place.fold_near(odd_kept, odd_came, BF)
    odd_came = place.mixed(odd_sent, 0)
    rows = first_back(
        embedded, d_middle, ident_rows, gains, d_normed, d_even, after(d_odd, odd_sent), mine
    )
    rows = after(rows, even_came, odd_came)
    total = lambda kept, came: kept.astype(F32) + came.astype(F32)
    both = jnp.concatenate([total(even_kept, even_came), total(odd_kept, odd_came)], axis=1)
    both = place.fold_outer(both, BF)
    even, odd = both[: even_kept.shape[1]], both[even_kept.shape[1] :]
    gain_rows = jnp.stack([jnp.sum(rows[2 * LAP :], axis=0), jnp.sum(gain_two, axis=0)])
    rows = jnp.concatenate([rows[: 2 * LAP], gain_rows], axis=0)
    row_count = rows.shape[0]
    rows = rows.T.reshape(devices, own_columns * row_count)
    rows = jnp.sum(lax.all_to_all(rows, ("dp", "head"), 0, 0, tiled=True), axis=0)
    rows = rows.reshape(own_columns, row_count)
    own_gains = lax.dynamic_slice_in_dim(gain_three, own_column, own_columns, 1)
    norm_parts = lax.all_to_all(
        squares([even, odd, grad_down, rows, own_gains], devices),
        ("dp", "head"),
        0,
        0,
        tiled=True,
    )
    own_half, other_half = even[:shard_rows], place.to_core(odd)
    halves = [place.by_core(own_half, other_half), place.by_core(other_half, own_half)]
    columns = lambda j: jnp.concatenate([v[:, j * SW : (j + 1) * SW] for v in halves], axis=1)
    grad_up = even[shard_rows:].reshape(2, own_columns, PACK)
    grads = (
        rows[:, : 2 * LAP],
        jnp.stack([columns(0), columns(1), columns(2)]),
        columns(3).T,
        jnp.stack([jnp.concatenate([grad_up[0], grad_up[1]], axis=1), grad_down]),
        jnp.concatenate([rows[:, 2 * LAP :].T, own_gains], axis=0),
    )
    turns = (lambda v: v.T, lambda v: v.transpose(1, 0, 2)) + (lambda v: v,) * 3
    state = [
        [turn(v) for turn, v in zip(turns, kind)]
        for kind in (
            (ident_weight, qkv_weight, out_weight, ffn_weight, norm_gains),
            (ident_first, qkv_first, out_first, ffn_first, gains_first),
            (ident_second, qkv_second, out_second, ffn_second, gains_second),
        )
    ]
    grad_norm, results = update(norm_parts, grads, state)
    return (grad_norm[0, 0], total_loss) + tuple(
        turn(v) for kind in results for turn, v in zip(turns, kind)
    )


def solution(mesh):
    both = P(None, ("dp", "head"))
    weights = (both, P("dp", None, "head"), P("head", "dp"), P(None, ("dp", "head"), None), both)
    in_specs = (P("dp", None),) * 5 + weights * 3
    out_specs = (P(), P()) + weights * 3
    return jax.shard_map(
        per_device, mesh=mesh, in_specs=in_specs, out_specs=out_specs, check_vma=False
    )
```

```python
import functools

import jax
import jax.numpy as jnp
from jax import lax
from jax.experimental import pallas as pl
from jax.experimental.pallas import tpu as pltpu
from jax.sharding import PartitionSpec as P

D = 768
HEAD_DIM = 24
LAP = 16
LEN = 128
NODE = 32
STEPS = 3
GRAPHS_DEV = 16
GAIN = 2 * LAP

HIGHEST = lax.Precision.HIGHEST
NORM_EPS = 1e-05
CLIP_AT = 5.0
STEP_RATES = (0.08, 0.02, 0.15, 0.02, 0.5)
BETA_ONE = 0.5
BETA_TWO = 0.5
DECAY = 0.01
ADAM_EPS = 1e-08
MASKED = -1e30

BF = jnp.bfloat16
F32 = jnp.float32
SUB = 4
SW = SUB * HEAD_DIM
PACK = 4 * SW
V_AT = 128 - SW
SCALE = HEAD_DIM ** (-0.5)
LENS = 5
VMEM_LIMIT = 48 * 2**20


def nn(a, b):
    return lax.dot_general(a, b, (((1,), (0,)), ((), ())), preferred_element_type=F32)


def nt(a, b):
    return lax.dot_general(a, b, (((1,), (1,)), ((), ())), preferred_element_type=F32)


def tn(a, b):
    return lax.dot_general(a, b, (((0,), (0,)), ((), ())), preferred_element_type=F32)


def lanes():
    return lax.broadcasted_iota(jnp.int32, (1, 128), 1)


def head_lanes(h, at):
    lane = lanes()
    return (lane >= at + h * HEAD_DIM) & (lane < at + (h + 1) * HEAD_DIM)


def by_head(v, at):
    zero = jnp.zeros_like(v)
    return jnp.concatenate([jnp.where(head_lanes(h, at), v, zero) for h in range(SUB)], axis=0)


def stack_heads(v):
    return jnp.concatenate([v[:, h * LEN : (h + 1) * LEN] for h in range(SUB)], axis=0)


def attend_kernel(info_ref, x_ref, *refs, graphs, whole, turn, owner):
    refs, turned = (refs[:-1], refs[-1:]) if turn else (refs, ())
    if whole:
        w_ref, qkv_ref, p_ref, o_ref, rinv_ref = refs
    else:
        first_ref, third_ref, w_ref, qkv_ref, p_ref, o_ref, rinv_ref = refs
        outs, rows = first_ref.shape[1], first_ref.shape[3]
        far, head = pl.program_id(0) // 2, pl.program_id(0) % 2
        outer, inner, gatherer = info_ref[0], info_ref[1], info_ref[owner]
        for i in range(2):
            in_first = (far == 0) if i == 0 else (far == 0) & (gatherer == 0)
            in_first = in_first | ((far == 1) & (gatherer == 1) & (i == 0))
            at = jnp.where(in_first, jnp.where(far + i == 0, 0, 1), jnp.where(far + i == 2, 1, 0))

            def place(source, at=at, i=i):
                for o in range(outs):
                    row = (lax.rem(outer + outs - o, outs) * 2 + (inner + i) % 2) * rows
                    w_ref[0, pl.ds(pl.multiple_of(row, rows), rows), :] = source[at, o, head]

            @pl.when(in_first)
            def _(place=place):
                place(first_ref)

            @pl.when(jnp.logical_not(in_first))
            def _(place=place):
                place(third_ref)

    if turned:

        @pl.when(pl.program_id(0) == 0)
        def _():
            turned[0][...] = x_ref[...].T

    y = nn(x_ref[...], w_ref[0])
    qkv_ref[0, 0] = y[:, :128].astype(BF)
    qkv_ref[0, 1] = pltpu.roll(y, PACK - SW, 1)[:, :128].astype(BF)
    qkv_ref[0, 2] = pltpu.roll(y, SW, 1)[:, 256:].astype(BF)
    col = lanes()
    ones = by_head(jnp.ones((LEN, 128), BF), V_AT)
    for g in range(graphs):
        rows = slice(g * LEN, (g + 1) * LEN)
        query, keys, values = qkv_ref[0, 0, rows, :], qkv_ref[0, 1, rows, :], qkv_ref[0, 2, rows, :]
        live = col < info_ref[LENS + g]
        scores = nt(query, by_head(keys, 0))
        parts = []
        for h in range(SUB):
            own = jnp.where(live, scores[:, h * LEN : (h + 1) * LEN] * SCALE, MASKED)
            parts.append(jnp.exp(own - jnp.max(own, axis=1, keepdims=True)).astype(BF))
        expo = jnp.concatenate(parts, axis=1)
        both = nn(expo, jnp.concatenate([by_head(values, V_AT), ones], axis=1))
        rinv = jnp.where(col >= V_AT, 1.0 / both[:, 128:], 0.0)
        p_ref[0, rows, :] = expo
        rinv_ref[0, rows, :] = rinv
        o_ref[0, rows, :] = jnp.where(col >= V_AT, both[:, :128] * rinv, 0.0).astype(BF)


def attend(info, owner, x, pieces, turn):
    tokens = x.shape[0]
    groups = 4
    whole = len(pieces) == 1
    block = lambda *tail: pl.BlockSpec((1,) + tail, lambda i: (i,) + (0,) * len(tail))
    full = lambda a: pl.BlockSpec(a.shape, lambda i: (0,) * a.ndim)
    out_specs = [block(3, tokens, 128), block(tokens, 512), block(tokens, 128), block(tokens, 128)]
    out_shape = [
        jax.ShapeDtypeStruct((groups, 3, tokens, 128), BF),
        jax.ShapeDtypeStruct((groups, tokens, 512), BF),
        jax.ShapeDtypeStruct((groups, tokens, 128), BF),
        jax.ShapeDtypeStruct((groups, tokens, 128), F32),
    ]
    if not whole:
        out_specs = [block(D, PACK)] + out_specs
        out_shape = [jax.ShapeDtypeStruct((groups, D, PACK), BF)] + out_shape
    if turn:
        out_specs = out_specs + [pl.BlockSpec((D, tokens), lambda i: (0, 0))]
        out_shape = out_shape + [jax.ShapeDtypeStruct((D, tokens), BF)]
    result = pl.pallas_call(
        functools.partial(attend_kernel, graphs=tokens // LEN, whole=whole, turn=turn, owner=owner),
        grid=(groups,),
        in_specs=[pl.BlockSpec(memory_space=pltpu.SMEM)]
        + [full(x)]
        + ([block(D, PACK)] if whole else [full(a) for a in pieces]),
        out_specs=out_specs,
        out_shape=out_shape,
        compiler_params=pltpu.CompilerParams(vmem_limit_bytes=VMEM_LIMIT),
        cost_estimate=pl.CostEstimate(
            flops=groups * 2_500_000_000, bytes_accessed=groups * 3_000_000, transcendentals=0
        ),
        name="attend",
    )(info, x, *pieces)
    return (pieces[0], result) if whole else (result[0], result[1:])


def attend_back_kernel(xt_ref, qkv_ref, p_ref, aug_ref, go_ref, *refs, graphs):
    *more, g_ref, d_ref = refs
    lane = lanes()
    for g in range(graphs):
        rows = slice(g * LEN, (g + 1) * LEN)
        query, keys, values = qkv_ref[0, 0, rows, :], qkv_ref[0, 1, rows, :], qkv_ref[0, 2, rows, :]
        d_rows, expo = aug_ref[0, rows, :], p_ref[0, rows, :]
        one, zero = jnp.ones_like(values), jnp.zeros_like(values)
        spread = jnp.concatenate(
            [
                jnp.where(
                    head_lanes(h, V_AT), values, jnp.where((lane == h) | (lane == SUB + h), one, zero)
                )
                for h in range(SUB)
            ],
            axis=0,
        )
        d_scores = (expo.astype(F32) * nt(d_rows, spread)).astype(BF)
        d_query = nn(d_scores, by_head(keys, 0)) * SCALE
        d_keys = tn(stack_heads(d_scores), by_head(query, 0)) * SCALE
        d_values = tn(stack_heads(expo), by_head(d_rows, V_AT))
        rolled_keys, rolled_values = pltpu.roll(d_keys, SW, 1), pltpu.roll(d_values, V_AT, 1)
        d_ref[0, rows, 0:128] = jnp.where(lane < SW, d_query, rolled_keys).astype(BF)
        d_ref[0, rows, 128:256] = jnp.where(lane < 64, rolled_keys, rolled_values).astype(BF)
        d_ref[0, rows, 256:384] = jnp.where(lane < V_AT, rolled_values, 0.0).astype(BF)
    grad = nn(xt_ref[...], d_ref[0])
    end = jnp.where(lane < V_AT, grad[:, 256:384], go_ref[0].astype(F32))
    if not more:
        g_ref[0, :, 0:256] = grad[:, 0:256].astype(BF)
        g_ref[0, :, 256:384] = end.astype(BF)
        return
    info_ref, came_ref = more
    outs, size = g_ref.shape[2], g_ref.shape[3]
    for o in range(outs):
        for i in range(2):
            rows = slice((o * 2 + i) * size, (o * 2 + i + 1) * size)
            at = lax.rem(i + info_ref[1], 2)
            came = came_ref[0, rows, :].astype(F32)
            g_ref[0, at, o, :, 0:256] = (grad[rows, 0:256] + came[:, 0:256]).astype(BF)
            g_ref[0, at, o, :, 256:384] = (end[rows] + came[:, 256:384]).astype(BF)


def attend_back(xt, saved, aug, grad_out, first, stride, groups, more=(), outs=0):
    qkv, expo = saved[:2]
    tokens = xt.shape[1]
    shape = (2, outs, D // (2 * outs), PACK) if more else (D, PACK)
    block = lambda *tail: pl.BlockSpec(
        (1,) + tail, lambda i: (first + i * stride,) + (0,) * len(tail)
    )
    out = lambda *tail: pl.BlockSpec((1,) + tail, lambda i: (i,) + (0,) * len(tail))
    return pl.pallas_call(
        functools.partial(attend_back_kernel, graphs=tokens // LEN),
        grid=(groups,),
        in_specs=[
            pl.BlockSpec(xt.shape, lambda i: (0, 0)),
            block(3, tokens, 128),
            block(tokens, 512),
            block(tokens, 128),
            block(D, 128),
        ]
        + ([pl.BlockSpec(memory_space=pltpu.SMEM), block(D, PACK)] if more else []),
        out_specs=[out(*shape), out(tokens, PACK)],
        out_shape=[
            jax.ShapeDtypeStruct((groups,) + shape, BF),
            jax.ShapeDtypeStruct((groups, tokens, PACK), BF),
        ],
        compiler_params=pltpu.CompilerParams(vmem_limit_bytes=VMEM_LIMIT),
        cost_estimate=pl.CostEstimate(
            flops=groups * 4_000_000_000, bytes_accessed=groups * 3_000_000, transcendentals=0
        ),
        name="attend_back",
    )(xt, qkv, expo, aug, grad_out, *more)


def first_sum_kernel(*refs, parts):
    d_refs, w_refs, out_ref = refs[: len(parts)], refs[len(parts) : -1], refs[-1]
    total = jnp.zeros(out_ref.shape, F32)
    for d_ref, (which, picks) in zip(d_refs, parts):
        for j in range(0, len(picks), 2):
            pair = range(j, min(j + 2, len(picks)))
            left = jnp.concatenate([d_ref[k] for k in pair], axis=1)
            right = jnp.concatenate([w_refs[which][picks[k]] for k in pair], axis=1)
            total = total + nt(left, right)
    out_ref[...] = total


def first_sum(ds, parts, weights):
    tokens = ds[0].shape[1]
    rows = LEN * min(2, tokens // LEN)
    full = lambda a: pl.BlockSpec(a.shape, lambda i: (0,) * a.ndim)
    return pl.pallas_call(
        functools.partial(first_sum_kernel, parts=parts),
        grid=(tokens // rows,),
        in_specs=[pl.BlockSpec((d.shape[0], rows, PACK), lambda i: (0, i, 0)) for d in ds]
        + [full(w) for w in weights],
        out_specs=pl.BlockSpec((rows, D), lambda i: (i, 0)),
        out_shape=jax.ShapeDtypeStruct((tokens, D), F32),
        compiler_params=pltpu.CompilerParams(vmem_limit_bytes=VMEM_LIMIT),
        cost_estimate=pl.CostEstimate(
            flops=7_000_000_000, bytes_accessed=12_000_000, transcendentals=0
        ),
        name="first_sum",
    )(*ds, *weights)


def first_back_kernel(
    e_ref, dmid_ref, ident_ref, gain_ref, sum_ref, even_ref, odd_ref, w_ref, out_ref, acc
):
    step, steps = pl.program_id(0), pl.num_programs(0)
    d_normed = sum_ref[...]
    for at, d_ref in enumerate((even_ref, odd_ref)):
        left = jnp.concatenate([d_ref[0], d_ref[1]], axis=1)
        d_normed = d_normed + nt(left, jnp.concatenate([w_ref[at], w_ref[at + 2]], axis=1))
    xhat, rstd = normalize(e_ref[...])
    d_emb = dmid_ref[...] + norm_back(d_normed, xhat, rstd, gain_ref[GAIN : GAIN + 1, :])
    part = tn(ident_ref[...], d_emb.astype(BF))
    part_gain = jnp.sum((d_normed * xhat).reshape(-1, 8, D), axis=0)

    @pl.when(step == 0)
    def _():
        acc[0 : 2 * LAP, :] = part
        acc[2 * LAP :, :] = part_gain

    @pl.when(step > 0)
    def _():
        acc[0 : 2 * LAP, :] += part
        acc[2 * LAP :, :] += part_gain

    @pl.when(step == steps - 1)
    def _():
        out_ref[...] = acc[...]


def first_back(embedded, d_middle, ident_rows, gains, total, d_even, d_odd, weights):
    tokens = embedded.shape[0]
    rows = LEN * min(2, tokens // LEN)
    full = lambda a: pl.BlockSpec(a.shape, lambda i: (0,) * a.ndim)
    tile = pl.BlockSpec((rows, D), lambda i: (i, 0))
    return pl.pallas_call(
        first_back_kernel,
        grid=(tokens // rows,),
        in_specs=[tile, tile, pl.BlockSpec((rows, 2 * LAP), lambda i: (i, 0)), full(gains), tile]
        + [pl.BlockSpec((2, rows, PACK), lambda i: (0, i, 0))] * 2
        + [full(weights)],
        out_specs=pl.BlockSpec((2 * LAP + 8, D), lambda i: (0, 0)),
        out_shape=jax.ShapeDtypeStruct((2 * LAP + 8, D), F32),
        scratch_shapes=[pltpu.VMEM((2 * LAP + 8, D), F32)],
        compiler_params=pltpu.CompilerParams(vmem_limit_bytes=VMEM_LIMIT),
        cost_estimate=pl.CostEstimate(
            flops=4_000_000_000, bytes_accessed=10_000_000, transcendentals=0
        ),
        name="first_back",
    )(embedded, d_middle, ident_rows, gains, total, d_even, d_odd, weights)


def normal_parts(x):
    falling = jnp.exp(-0.5 * x * x)
    t = 1.0 / (1.0 + (0.3275911 * 0.5**0.5) * jnp.abs(x))
    tail = 0.5 * 1.061405429
    for c in (-1.453152027, 1.421413741, -0.284496736, 0.254829592):
        tail = tail * t + 0.5 * c
    tail = tail * t * falling
    return jnp.where(x < 0.0, tail, 1.0 - tail), 0.3989422804014327 * falling


def normalize(values):
    centred = values - jnp.mean(values, axis=-1, keepdims=True)
    spread = jnp.mean(centred * centred, axis=-1, keepdims=True)
    rstd = lax.rsqrt(spread + NORM_EPS)
    return centred * rstd, rstd


def two_parts(v):
    high = v.astype(BF)
    return high, (v - high.astype(F32)).astype(BF)


def forward_kernel(
    info_ref, e_ref, gain_ref, ffn_ref, other_ref, *refs, tile_graphs, waves, groups
):
    o_refs, w_refs = refs[:waves], refs[waves : 2 * waves]
    mid_ref, slope_ref, pay_ref, up_ref, down_ref, hsum, msum = refs[2 * waves :]
    step, steps = pl.program_id(0), pl.num_programs(0)
    core = info_ref[3]

    @pl.when((step == 0) & (core == 0))
    def _():
        up_ref[...] = ffn_ref[...]
        down_ref[...] = other_ref[...]

    @pl.when((step == 0) & (core != 0))
    def _():
        up_ref[...] = other_ref[...]
        down_ref[...] = ffn_ref[...]

    middle = e_ref[...]
    for wave in range(waves):
        left = jnp.concatenate([o_refs[wave][j] for j in range(groups)], axis=1)
        right = jnp.concatenate([w_refs[wave][j][:, 256:] for j in range(groups)], axis=1)
        middle = middle + nt(left, right)
    mid_ref[...] = middle
    xhat, _ = normalize(middle)
    up = nn((xhat * gain_ref[GAIN + 1 : GAIN + 2, :]).astype(BF), up_ref[...])
    cdf, density = normal_parts(up)
    hidden = (up * cdf).astype(BF).astype(F32)
    slope_ref[...] = (cdf + up * density).astype(BF)
    place = lax.broadcasted_iota(jnp.int32, (LEN, 1), 0)
    for j in range(tile_graphs):
        g = step * tile_graphs + j
        live = place < info_ref[LENS + g]
        rows = slice(j * LEN, (j + 1) * LEN)
        hsum[pl.ds(g, 1), :] = jnp.sum(jnp.where(live, hidden[rows], 0.0), axis=0, keepdims=True)
        msum[pl.ds(g, 1), :] = jnp.sum(jnp.where(live, middle[rows], 0.0), axis=0, keepdims=True)

    @pl.when(step == steps - 1)
    def _():
        graphs = hsum.shape[0]
        high, low = two_parts(hsum[...])
        which = lax.broadcasted_iota(jnp.int32, (graphs, 1), 0)
        length, partner = jnp.ones((graphs, 1), F32), jnp.zeros((graphs, 1), F32)
        for g in range(graphs):
            length = jnp.where(which == g, info_ref[LENS + g].astype(F32), length)
            partner = jnp.where(which == g, info_ref[LENS + graphs + g].astype(F32), partner)
        pooled = (msum[...] + (nt(high, down_ref[...]) + nt(low, down_ref[...]))) / length
        xhat_pool, rstd = normalize(pooled)
        high, low = two_parts(xhat_pool)
        pay_ref[:, 0:D] = high
        pay_ref[:, D : 2 * D] = low
        pay_ref[:, 2 * D : 3 * D] = hsum[...].astype(BF)
        lane = lanes()
        stats = jnp.zeros((graphs, 128), F32)
        for at, value in enumerate(two_parts(rstd) + two_parts(1.0 / length) + (partner,)):
            stats = jnp.where(lane == at, value.astype(F32), stats)
        pay_ref[:, 3 * D :] = stats.astype(BF)


def forward_rest(info, embedded, gains, w_up, w_down, outs, weights):
    tokens = embedded.shape[0]
    graphs = tokens // LEN
    tile_graphs = min(4, graphs)
    rows = tile_graphs * LEN
    waves, groups = len(outs), outs[0].shape[0]
    full = lambda a: pl.BlockSpec(a.shape, lambda i: (0,) * a.ndim)
    tile = pl.BlockSpec((rows, D), lambda i: (i, 0))
    return pl.pallas_call(
        functools.partial(forward_kernel, tile_graphs=tile_graphs, waves=waves, groups=groups),
        grid=(tokens // rows,),
        in_specs=[pl.BlockSpec(memory_space=pltpu.SMEM)]
        + [tile, full(gains), full(w_up), full(w_down)]
        + [pl.BlockSpec((groups, rows, 128), lambda i: (0, i, 0)) for _ in outs]
        + [full(w) for w in weights],
        out_specs=[
            tile,
            tile,
            pl.BlockSpec((graphs, 3 * D + 128), lambda i: (0, 0)),
            full(w_up),
            full(w_down),
        ],
        out_shape=[
            jax.ShapeDtypeStruct((tokens, D), F32),
            jax.ShapeDtypeStruct((tokens, D), BF),
            jax.ShapeDtypeStruct((graphs, 3 * D + 128), BF),
            jax.ShapeDtypeStruct(w_up.shape, BF),
            jax.ShapeDtypeStruct(w_down.shape, BF),
        ],
        scratch_shapes=[pltpu.VMEM((graphs, D), F32), pltpu.VMEM((graphs, D), F32)],
        compiler_params=pltpu.CompilerParams(vmem_limit_bytes=VMEM_LIMIT),
        cost_estimate=pl.CostEstimate(
            flops=10_000_000_000, bytes_accessed=20_000_000, transcendentals=0
        ),
        name="forward_rest",
    )(info, embedded, gains, w_up, w_down, *outs, *weights)


def norm_back(d_normed, xhat, rstd, gain):
    d_hat = d_normed * gain
    return rstd * (
        d_hat
        - jnp.mean(d_hat, axis=-1, keepdims=True)
        - xhat * jnp.mean(d_hat * xhat, axis=-1, keepdims=True)
    )


def ffn_back_kernel(
    info_ref, mid_ref, slope_ref, dout_ref, dhid_ref, gain_ref, up_ref, *refs, tile_graphs, groups
):
    o_refs, rinv_refs, w_refs = refs[0:2], refs[2:4], refs[4:6]
    dmid_ref, grad_ref, dgain_ref = refs[6:9]
    aug_refs, go_refs = refs[9:11], refs[11:13]
    grad, dgain, grad_out = refs[13:]
    step, steps = pl.program_id(0), pl.num_programs(0)
    xhat, rstd = normalize(mid_ref[...])
    gain = gain_ref[GAIN + 1 : GAIN + 2, :]
    place = lax.broadcasted_iota(jnp.int32, (LEN, 1), 0)
    d_up, d_out = [], []
    for j in range(tile_graphs):
        g = step * tile_graphs + j
        live = place < info_ref[LENS + g]
        rows = slice(j * LEN, (j + 1) * LEN)
        d_hidden = jnp.where(live, dhid_ref[pl.ds(g, 1), :], 0.0)
        d_up.append((slope_ref[rows, :].astype(F32) * d_hidden).astype(BF))
        d_out.append(jnp.where(live, dout_ref[pl.ds(g, 1), :], 0.0))
    d_up, d_out = jnp.concatenate(d_up, axis=0), jnp.concatenate(d_out, axis=0)
    d_normed = nt(d_up, up_ref[...])
    d_mid = d_out + norm_back(d_normed, xhat, rstd, gain)
    dmid_ref[...] = d_mid
    d_attn = d_mid.astype(BF)
    d_turned = d_attn.T
    part = tn((xhat * gain).astype(BF), d_up)
    part_gain = jnp.sum((d_normed * xhat).reshape(-1, 8, D), axis=0)

    lane = lanes()
    row = lax.broadcasted_iota(jnp.int32, (256, 128), 0) & 127
    column = lax.broadcasted_iota(jnp.int32, (256, 128), 1)
    pick = jnp.zeros((256, 128), BF)
    for h in range(SUB):
        inside = (row >= V_AT + h * HEAD_DIM) & (row < V_AT + (h + 1) * HEAD_DIM)
        pick = jnp.where(inside & ((column == h) | (column == SUB + h)), jnp.ones_like(pick), pick)
    parts_out = []
    for half in range(2):
        d_heads = nn(d_attn, jnp.concatenate([w_refs[half][j] for j in range(groups)], axis=1))
        for j in range(groups):
            d_over = d_heads[:, j * 128 : (j + 1) * 128] * rinv_refs[half][j]
            d_over = jnp.where(lane >= V_AT, d_over, 0.0)
            terms = d_over * o_refs[half][j].astype(F32)
            delta = nn(jnp.concatenate(two_parts(terms), axis=1), pick)
            rounded = delta.astype(BF).astype(F32)
            aug_refs[half][j] = jnp.where(
                lane >= V_AT, d_over, jnp.where(lane < SUB, -rounded, rounded - delta)
            ).astype(BF)
        parts_out.append(
            nn(d_turned, jnp.concatenate([o_refs[half][j] for j in range(groups)], axis=1))
        )

    @pl.when(step == 0)
    def _():
        grad[...] = part
        dgain[...] = part_gain
        for half in range(2):
            grad_out[half] = parts_out[half]

    @pl.when(step > 0)
    def _():
        grad[...] += part
        dgain[...] += part_gain
        for half in range(2):
            grad_out[half] += parts_out[half]

    @pl.when(step == steps - 1)
    def _():
        for half in range(2):
            grad_ref[half] = grad[:, half * PACK : (half + 1) * PACK].astype(BF)
            for j in range(groups):
                go_refs[half][j] = grad_out[half, :, j * 128 : (j + 1) * 128].astype(BF)
        dgain_ref[...] = dgain[...]


def ffn_back(info, middle, slope, d_out, d_hidden, gains, w_up, outs, rinvs, weights):
    tokens = middle.shape[0]
    tile_graphs = min(2, tokens // LEN)
    rows = tile_graphs * LEN
    groups = outs[0].shape[0]
    full = lambda a: pl.BlockSpec(a.shape, lambda i: (0,) * a.ndim)
    tile = pl.BlockSpec((rows, D), lambda i: (i, 0))
    sub_tile = pl.BlockSpec((groups, rows, 128), lambda i: (0, i, 0))
    result = pl.pallas_call(
        functools.partial(ffn_back_kernel, tile_graphs=tile_graphs, groups=groups),
        grid=(tokens // rows,),
        in_specs=[pl.BlockSpec(memory_space=pltpu.SMEM), tile, tile]
        + [full(a) for a in (d_out, d_hidden, gains, w_up)]
        + [sub_tile] * 4
        + [pl.BlockSpec((groups, D, 128), lambda i: (0, 0, 2))] * 2,
        out_specs=[
            tile,
            pl.BlockSpec((2, D, PACK), lambda i: (0, 0, 0)),
            pl.BlockSpec((8, D), lambda i: (0, 0)),
        ]
        + [sub_tile] * 2
        + [pl.BlockSpec((groups, D, 128), lambda i: (0, 0, 0))] * 2,
        out_shape=[
            jax.ShapeDtypeStruct((tokens, D), F32),
            jax.ShapeDtypeStruct((2, D, PACK), BF),
            jax.ShapeDtypeStruct((8, D), F32),
        ]
        + [jax.ShapeDtypeStruct((groups, tokens, 128), BF)] * 2
        + [jax.ShapeDtypeStruct((groups, D, 128), BF)] * 2,
        scratch_shapes=[
            pltpu.VMEM((D, D), F32),
            pltpu.VMEM((8, D), F32),
            pltpu.VMEM((2, D, groups * 128), F32),
        ],
        compiler_params=pltpu.CompilerParams(vmem_limit_bytes=VMEM_LIMIT),
        cost_estimate=pl.CostEstimate(
            flops=14_000_000_000, bytes_accessed=20_000_000, transcendentals=0
        ),
        name="ffn_back",
    )(info, middle, slope, d_out, d_hidden, gains, w_up, *outs, *rinvs, *weights)
    return result[:3], result[3:5], result[5:7]


def loss_kernel(
    info_ref, a1_ref, a3_ref, b1_ref, b3_ref, gain_ref, down_ref,
    loss_ref, dout_ref, dhid_ref, dlow_ref, hid_ref, dgain_ref, xhat, stats, rows_ref
):
    outs, graphs = a1_ref.shape[1], a1_ref.shape[2]
    outer, inner, far, core = (info_ref[i] for i in range(4))
    count = outs * 2 * GRAPHS_DEV
    place = lambda f, o, i, c: pl.multiple_of(
        f * count + (o * 2 + i) * GRAPHS_DEV + c * graphs, graphs
    )
    for owner, refs in ((core, (a1_ref, a3_ref)), (1 - core, (b1_ref, b3_ref))):
        for part, ref in enumerate(refs):
            for at in range(2):
                if part == at:
                    f, i = part, part
                else:
                    f, i = (owner, 1 - owner) if part == 0 else (1 - owner, owner)
                for o in range(outs):
                    values = ref[at, o].astype(F32)
                    row = place(
                        lax.rem(far + f, 2), lax.rem(outer + outs - o, outs), lax.rem(inner + i, 2), owner
                    )
                    rows = pl.ds(row, graphs)
                    xhat[rows, :] = values[:, 0:D] + values[:, D : 2 * D]
                    rows_ref[rows, :] = values[:, 2 * D : 3 * D]
                    stats[rows, :] = values[:, 3 * D :]
    hid_ref[...] = rows_ref[...].astype(BF)
    root = D**-0.5
    left, right = xhat[0:count, :] * gain_ref[GAIN + 2 : GAIN + 3, :], xhat[count:, :] * gain_ref[GAIN + 2 : GAIN + 3, :]
    exact = lambda a, b, dims: lax.dot_general(
        a, b, (dims, ((), ())), precision=HIGHEST, preferred_element_type=F32
    )
    logits = exact(left, right, ((1,), (1,))) * root
    row_top, col_top = jnp.max(logits, axis=1, keepdims=True), jnp.max(logits, axis=0, keepdims=True)
    row_expo, col_expo = jnp.exp(logits - row_top), jnp.exp(logits - col_top)
    row_sum, col_sum = jnp.sum(row_expo, axis=1, keepdims=True), jnp.sum(col_expo, axis=0, keepdims=True)
    row_id = lax.broadcasted_iota(jnp.int32, (count, count), 0)
    col_id = lax.broadcasted_iota(jnp.int32, (count, count), 1)
    slot = stats[0:count, 4:5].astype(jnp.int32)
    positive = jnp.where(col_id == (row_id & -GRAPHS_DEV) + slot, 1.0, 0.0)
    loss = (
        jnp.sum(row_top + jnp.log(row_sum), axis=0, keepdims=True)
        + jnp.sum(col_top + jnp.log(col_sum), axis=1, keepdims=True)
        - 2.0 * jnp.sum(jnp.sum(positive * logits, axis=1, keepdims=True), axis=0, keepdims=True)
    )
    loss_ref[...] = loss
    d_logits = row_expo / row_sum + col_expo / col_sum - 2.0 * positive
    rows_ref[0:count, :] = exact(d_logits, right, ((1,), (0,))) * root
    rows_ref[count:, :] = exact(d_logits, left, ((0,), (0,))) * root
    every = xhat[...]
    d_summary = rows_ref[...]
    dgain_ref[...] = jnp.sum(d_summary * every, axis=0, keepdims=True)
    rstd, share = stats[:, 0:1] + stats[:, 1:2], stats[:, 2:3] + stats[:, 3:4]
    d_rows = norm_back(d_summary, every, rstd, gain_ref[GAIN + 2 : GAIN + 3, :]) * share
    rows_ref[...] = d_rows
    dlow_ref[...] = d_rows.astype(BF)
    own = rows_ref[pl.ds(place(far, outer, inner, core), graphs), :]
    dout_ref[...] = own
    dhid_ref[...] = nn(own.astype(BF), down_ref[...])


def contrast(info, pieces, gains, w_down):
    outs, graphs = pieces[0].shape[1], pieces[0].shape[2]
    total = outs * 4 * GRAPHS_DEV
    return pl.pallas_call(
        loss_kernel,
        in_specs=[pl.BlockSpec(memory_space=pltpu.SMEM)]
        + [pl.BlockSpec(memory_space=pltpu.VMEM)] * 6,
        out_specs=[pl.BlockSpec(memory_space=pltpu.VMEM)] * 6,
        out_shape=[
            jax.ShapeDtypeStruct((1, 1), F32),
            jax.ShapeDtypeStruct((graphs, D), F32),
            jax.ShapeDtypeStruct((graphs, D), F32),
            jax.ShapeDtypeStruct((total, D), BF),
            jax.ShapeDtypeStruct((total, D), BF),
            jax.ShapeDtypeStruct((1, D), F32),
        ],
        scratch_shapes=[
            pltpu.VMEM((total, D), F32),
            pltpu.VMEM((total, 128), F32),
            pltpu.VMEM((total, D), F32),
        ],
        compiler_params=pltpu.CompilerParams(vmem_limit_bytes=24 * 2**20),
        cost_estimate=pl.CostEstimate(
            flops=3_000_000_000, bytes_accessed=4_000_000, transcendentals=0
        ),
        name="contrast",
    )(info, *pieces, gains, w_down)


def contrast_plain(everyone, gains, w_down, own_row, graphs):
    n = everyone.shape[0]
    stats = everyone[..., 3 * D :].astype(F32)
    xhat = everyone[..., :D].astype(F32) + everyone[..., D : 2 * D].astype(F32)
    hidden_sums = everyone[..., 2 * D : 3 * D].reshape(-1, D)
    rstd_pool = (stats[..., 0:1] + stats[..., 1:2]).reshape(-1, 1)
    share = (stats[..., 2:3] + stats[..., 3:4]).reshape(-1, 1)
    summaries = xhat * gains[GAIN + 2]
    left, right = summaries[:, 0].reshape(-1, D), summaries[:, 1].reshape(-1, D)
    root_width = D**0.5
    logits = jnp.dot(left, right.T, precision=HIGHEST) / root_width
    row_totals, col_totals = log_total(logits, 1), log_total(logits, 0)
    count = logits.shape[0]
    group = jnp.arange(count, dtype=jnp.int32) // GRAPHS_DEV
    partners = group * GRAPHS_DEV + stats[:, 0, :, 4].reshape(-1).astype(jnp.int32)
    positive = (partners[:, None] == jnp.arange(count, dtype=jnp.int32)[None, :]).astype(F32)
    total_loss = jnp.sum(row_totals) + jnp.sum(col_totals) - 2.0 * jnp.sum(positive * logits)
    d_logits = (
        jnp.exp(logits - row_totals[:, None])
        + jnp.exp(logits - col_totals[None, :])
        - 2.0 * positive
    )
    d_left = jnp.dot(d_logits, right, precision=HIGHEST) / root_width
    d_right = jnp.dot(d_logits.T, left, precision=HIGHEST) / root_width
    d_summary = jnp.stack(
        [d_left.reshape(n, GRAPHS_DEV, D), d_right.reshape(n, GRAPHS_DEV, D)], axis=1
    ).reshape(-1, D)
    xhat = xhat.reshape(-1, D)
    gain_three = jnp.sum(d_summary * xhat, axis=0, keepdims=True)
    d_rows = norm_back(d_summary, xhat, rstd_pool, gains[GAIN + 2]) * share
    d_out = lax.dynamic_slice_in_dim(d_rows, own_row, graphs, 0)
    d_hidden = nn(d_out.astype(BF), w_down)
    return total_loss, d_out, d_hidden, d_rows.astype(BF), hidden_sums, gain_three


class Place:
    def __init__(self):
        self.n, self.heads = lax.axis_size("dp"), lax.axis_size("head")
        self.outs = self.n // 2
        dp, head = lax.axis_index("dp"), lax.axis_index("head")
        self.dp, self.head = dp, head
        self.outer, self.inner, self.far, self.core = dp // 2, dp % 2, head // 2, head % 2

    def move(self, v, to):
        pairs = []
        for i in range(self.n * self.heads):
            outer, inner, far, core = i // 8, (i // 4) % 2, (i // 2) % 2, i % 2
            outer, inner, far, core = to(outer, inner, far, core)
            pairs.append((i, ((outer % self.outs * 2 + inner) * 2 + far) * 2 + core))
        return lax.ppermute(v, ("dp", "head"), pairs)

    def to_core(self, v):
        return self.move(v, lambda o, i, f, c: (o, i, f, 1 - c))

    def to_outer(self, v, by):
        return self.move(v, lambda o, i, f, c: (o + by, i, f, c))

    def mixed(self, v, turn):
        return self.move(
            v, lambda o, i, f, c: (o, 1 - i, f, c) if c == turn else (o, i, 1 - f, c)
        )

    def by_core(self, a, b):
        return jnp.where(self.core == 0, a, b)

    def gather_outer(self, v, *late):
        out = jnp.zeros((self.outs,) + v.shape, v.dtype)
        out = lax.dynamic_update_index_in_dim(out, v, self.outer, 0)
        for by in range(1, self.outs):
            out = lax.dynamic_update_index_in_dim(
                out, after(self.to_outer(v, by), *late), (self.outer - by) % self.outs, 0
            )
        return out

    def outer_list(self, v):
        return jnp.stack([v] + [self.to_outer(v, by) for by in range(1, self.outs)])

    def gather_pieces(self, v):
        return self.gather_near(self.gather_outer(v))

    def gather_near(self, own):
        return self.gather_last(own, self.mixed(own, 0))

    def gather_last(self, own, second):
        return self.pieces_of(own, second, self.mixed(jnp.stack([own, second]), 1))

    def pieces_of(self, own, second, third):
        return [
            [own, self.by_core(second, third[0])],
            [self.by_core(third[0], second), third[1]],
        ]

    def whole(self, pieces):
        rows = [
            [jnp.where(self.far == 0, pieces[f][i], pieces[1 - f][i]) for f in range(2)]
            for i in range(2)
        ]
        ordered = [
            [jnp.where(self.inner == 0, rows[i][f], rows[1 - i][f]) for f in range(2)]
            for i in range(2)
        ]
        return jnp.stack([jnp.stack(pair, axis=1) for pair in ordered], axis=1)

    def both_cores(self, v, axis):
        other = self.to_core(v)
        return jnp.stack([self.by_core(v, other), self.by_core(other, v)], axis=axis)

    def both_cores_of(self, own, sent):
        other = self.to_core(sent)
        return jnp.stack([self.by_core(own, other), self.by_core(other, own)])

    def gather_all(self, v):
        v = self.both_cores(self.whole(self.gather_pieces(v)), 3)
        return v.reshape((self.n, self.heads) + v.shape[4:])

    def fold_far(self, pieces):
        sent = jnp.stack([self.by_core(pieces[1][0], pieces[0][1]), pieces[1][1]])
        kept = jnp.stack([pieces[0][0], self.by_core(pieces[0][1], pieces[1][0])])
        return kept, sent

    def fold_near(self, kept, came, dtype):
        total = kept.astype(F32) + came.astype(F32)
        return total[0], total[1].astype(dtype)

    def fold_outer(self, total, dtype):
        total = total.astype(dtype)
        pick = lambda by: lax.dynamic_index_in_dim(
            total, (self.outer + by) % self.outs, 0, keepdims=False
        )
        result = pick(0).astype(F32)
        for by in range(1, self.outs):
            result = result + self.to_outer(pick(by), by).astype(F32)
        return result

    def total(self, v):
        v = jnp.broadcast_to(v, (self.n * self.heads, 128))
        return jnp.sum(lax.all_to_all(v, ("dp", "head"), 0, 0, tiled=True)[:, 0])

    def split_rows(self, v):
        v = v.reshape((self.outs, 2, -1) + v.shape[1:])
        return [
            lax.dynamic_index_in_dim(v, (self.inner + i) % 2, 1, keepdims=False) for i in range(2)
        ]


def tie(*values):
    return lax.optimization_barrier(values)


def after(value, *others):
    return lax.optimization_barrier((value,) + others)[0]


def log_total(values, axis):
    top = jnp.max(values, axis=axis, keepdims=True)
    return jnp.squeeze(top, axis) + jnp.log(jnp.sum(jnp.exp(values - top), axis=axis))


def identifiers(table, endpoints):
    graphs = endpoints.shape[0] // LEN
    nodes = table.reshape(graphs, NODE, LAP).astype(BF)
    picks = (
        endpoints.reshape(graphs, LEN, 2)[..., None] == jnp.arange(NODE, dtype=jnp.int32)
    ).astype(BF)
    found = jnp.einsum("glan,gnc->glac", picks, nodes, preferred_element_type=F32)
    return found.reshape(graphs * LEN, 2 * LAP).astype(BF)


def stack_pieces(place, near, last):
    pieces = place.pieces_of(near[0], near[1], last)
    packs = []
    for f in range(2):
        for c in range(2):
            rows = [
                jnp.where(place.inner == i, pieces[f][0][:, c], pieces[f][1][:, c]) for i in range(2)
            ]
            packs.append(jnp.stack(rows, axis=1).reshape(D, PACK))
    return jnp.stack(packs)


def split_core(place, grad_up):
    v = grad_up.reshape((2, place.outs, 2, 2, 2, -1, PACK))
    pick = lambda at: lax.dynamic_index_in_dim(v, at, 4, keepdims=False)
    return pick(1 - place.core), pick(place.core)


def fold_pieces(place, own, came, up):
    pieces = []
    for f in range(2):
        total = own[f].astype(F32) + came[f].astype(F32)
        pieces.append([v.astype(BF) for v in place.split_rows(total)])
    if up is None:
        return pieces
    total = (up[0].astype(F32) + up[1].astype(F32)).astype(BF)
    for f in range(2):
        part = lax.dynamic_index_in_dim(total, (place.far + f) % 2, 3, keepdims=False)
        for i in range(2):
            rows = lax.dynamic_index_in_dim(part, (place.inner + i) % 2, 2, keepdims=False)
            pieces[f][i] = jnp.concatenate([pieces[f][i], rows[0], rows[1]], axis=1)
    return pieces


def squares_kernel(*refs):
    *grad_refs, out_ref = refs
    total = jnp.zeros((1, 1), F32)
    for ref in grad_refs:
        v = ref[...]
        total = total + jnp.sum(jnp.sum(v * v, axis=0, keepdims=True), axis=1, keepdims=True)
    out_ref[...] = jnp.broadcast_to(total, out_ref.shape)


def squares(grads, devices):
    return pl.pallas_call(
        squares_kernel,
        out_shape=jax.ShapeDtypeStruct((devices, 128), F32),
        cost_estimate=pl.CostEstimate(flops=1_000_000, bytes_accessed=500_000, transcendentals=0),
        name="squares",
    )(*grads)


def update_kernel(parts_ref, *refs):
    count = len(STEP_RATES)
    grads, weights, firsts, seconds = (refs[k * count : (k + 1) * count] for k in range(4))
    norm_ref, refs = refs[4 * count], refs[4 * count + 1 :]
    new_weights, new_firsts, new_seconds = (refs[k * count : (k + 1) * count] for k in range(3))
    norm = jnp.sqrt(jnp.sum(parts_ref[...], axis=0, keepdims=True)[:, 0:1])
    norm_ref[...] = norm
    factor = CLIP_AT / jnp.maximum(norm, CLIP_AT)
    for k, rate in enumerate(STEP_RATES):
        for at in range(grads[k].shape[0]) if len(grads[k].shape) == 3 else (...,):
            weight = weights[k][at]
            clipped = grads[k][at] * factor
            first = BETA_ONE * firsts[k][at] + (1.0 - BETA_ONE) * clipped
            second = BETA_TWO * seconds[k][at] + (1.0 - BETA_TWO) * clipped * clipped
            first_hat = first / (1.0 - BETA_ONE**STEPS)
            second_hat = second / (1.0 - BETA_TWO**STEPS)
            new_weights[k][at] = weight - rate * (
                first_hat / (jnp.sqrt(second_hat) + ADAM_EPS) + DECAY * weight
            )
            new_firsts[k][at] = first
            new_seconds[k][at] = second


def update(norm_parts, grads, state):
    result = pl.pallas_call(
        update_kernel,
        out_shape=[jax.ShapeDtypeStruct((1, 1), F32)]
        + [jax.ShapeDtypeStruct(v.shape, F32) for kind in state for v in kind],
        cost_estimate=pl.CostEstimate(
            flops=5_000_000, bytes_accessed=6_000_000, transcendentals=0
        ),
        name="update",
    )(norm_parts, *grads, *(v for kind in state for v in kind))
    count = len(grads)
    return result[0], [result[1 + k * count : 1 + (k + 1) * count] for k in range(3)]


def per_device(
    features,
    laplacian,
    endpoints,
    lengths,
    pairing,
    ident_weight,
    qkv_weight,
    out_weight,
    ffn_weight,
    norm_gains,
    ident_first,
    qkv_first,
    out_first,
    ffn_first,
    gains_first,
    ident_second,
    qkv_second,
    out_second,
    ffn_second,
    gains_second,
):
    place = Place()
    heads, head, dp, core = place.heads, place.head, place.dp, place.core
    tokens = features.shape[0] // heads
    devices = place.n * heads
    graphs = tokens // LEN
    own_columns = norm_gains.shape[1]

    small = jnp.concatenate([ident_weight, norm_gains], axis=0)
    small_rows = small.shape[0]

    packed = [qkv_weight[:, 0], qkv_weight[:, 1], qkv_weight[:, 2], out_weight.T]
    shards = jnp.stack(
        [
            jnp.concatenate([m[:, s * SW : (s + 1) * SW] for m in packed], axis=1).astype(BF)
            for s in range(2)
        ]
    )
    pick = lambda v, at: lax.dynamic_index_in_dim(v, at, 0, keepdims=False)
    near = jnp.stack([pick(shards, core), place.to_core(pick(shards, 1 - core))])
    shard_rows = D // place.n
    aligned = shard_rows % 16 == 0
    near_own = (place.outer_list if aligned else place.gather_outer)(near)
    small = jnp.broadcast_to(after(small.reshape(1, -1), near_own), (devices, small.size))
    small = lax.all_to_all(small, ("dp", "head"), 0, 0, tiled=True)
    near = jnp.stack([near_own, place.mixed(near_own, 0)])
    last = place.mixed(near, 1)
    ffn = after(ffn_weight.astype(BF), near_own)
    small = after(small, near)
    ffn_near = place.both_cores_of(pick(ffn, core), pick(ffn, 1 - core))
    ffn_own = place.gather_outer(ffn_near, near)
    near_others = place.to_core(near)
    ffn_next = place.mixed(ffn_own, 0)
    ffn_last = place.mixed(jnp.stack([ffn_own, ffn_next]), 1)
    small = small.reshape(-1, small_rows, own_columns).transpose(1, 0, 2).reshape(small_rows, D)
    ident_full, gains = after(small[: 2 * LAP].astype(BF), near), small
    start_row = head * tokens
    lens = lax.dynamic_slice_in_dim(lengths.reshape(-1), head * graphs, graphs, 0)
    partner = lax.dynamic_slice_in_dim(
        jnp.concatenate([pairing.reshape(-1)] * 2), head * graphs, graphs, 0
    )
    places = jnp.stack([place.outer, place.inner, place.far, core, 1 - core]).astype(jnp.int32)
    info = jnp.concatenate([places, lens, partner])
    table_rows = lax.dynamic_slice_in_dim(laplacian, head * graphs * NODE, graphs * NODE, 0)
    end_rows = lax.dynamic_slice_in_dim(endpoints, start_row, tokens, 0)
    ident_rows = identifiers(table_rows, end_rows)
    embedded = lax.dynamic_slice_in_dim(features, start_row, tokens, 0).astype(F32)
    embedded = embedded + nn(ident_rows, ident_full)
    normed_one = (normalize(embedded)[0] * gains[GAIN]).astype(BF)

    last_others = place.to_core(last)
    if aligned:
        mine, saved_mine = attend(info, 3, normed_one, [near, last], True)
    else:
        packs = stack_pieces(place, near, last)
        mine, saved_mine = attend(info, 3, normed_one, [packs], True)
    normed_turned = saved_mine[4]
    heads_mine = saved_mine[2]
    ffn_pieces = place.pieces_of(ffn_own, ffn_next, after(ffn_last, heads_mine))
    if aligned:
        others, saved_others = attend(info, 4, normed_one, [near_others, last_others], False)
    else:
        others, saved_others = attend(info, 4, normed_one, [place.to_core(packs)], False)
    ffn_mine = place.whole(ffn_pieces).reshape(D, -1)
    ffn_other = place.to_core(ffn_mine)
    middle, slope, payload, w_up, w_down = forward_rest(
        info,
        embedded,
        gains,
        ffn_mine,
        ffn_other,
        [heads_mine, saved_others[2]],
        [mine, others],
    )

    own_row = (dp * heads + head) * graphs
    if place.n * GRAPHS_DEV <= 128:
        first = place.outer_list(payload)
        first = jnp.stack([first, place.mixed(first, 0)])
        third = place.mixed(first, 1)
        total_loss, d_out, d_hidden, d_rows_low, hidden_sums, gain_three = contrast(
            info, [first, third, place.to_core(first), place.to_core(third)], gains, w_down
        )
        total_loss = total_loss[0, 0]
    else:
        everyone = place.gather_all(payload).reshape(place.n, 2, GRAPHS_DEV, -1)
        total_loss, d_out, d_hidden, d_rows_low, hidden_sums, gain_three = contrast_plain(
            everyone, gains, w_down, own_row, graphs
        )

    own_column = (dp * heads + head) * own_columns
    d_columns = lax.dynamic_slice_in_dim(d_rows_low, own_column, own_columns, 1)
    grad_down = tn(d_columns, hidden_sums)
    (d_middle, grad_up, gain_two), augs, grad_outs = ffn_back(
        info,
        middle,
        slope,
        d_out,
        d_hidden,
        gains,
        w_up,
        [saved_mine[2], saved_others[2]],
        [saved_mine[3], saved_others[3]],
        [mine, others],
    )
    up_sent, up_kept = split_core(place, grad_up)
    up_came = place.to_core(up_sent)
    grad_others, d_others = attend_back(
        normed_turned, saved_others, augs[1], grad_outs[1], 0, 1, heads
    )
    came = place.to_core(grad_others)
    back = functools.partial(attend_back, normed_turned, saved_mine)
    aug = after(augs[0], grad_others)
    grad_even, d_even = back(aug, grad_outs[0], 0, 2, heads // 2)
    even = fold_pieces(place, [grad_even[0], grad_even[1]], [came[0], came[2]], (up_kept, up_came))
    even_kept, even_sent = place.fold_far(even)
    even_came = place.mixed(even_sent, 1)
    more = ([info, came], place.outs) if aligned else ()
    grad_odd, d_odd = back(after(aug, even_sent), grad_outs[0], 1, 2, heads // 2, *more)
    even_kept, even_sent = place.fold_near(even_kept, after(even_came, grad_odd), BF)
    if aligned:
        odd = [[v[0], v[1]] for v in grad_odd]
    else:
        odd = fold_pieces(place, [grad_odd[0], grad_odd[1]], [came[1], came[3]], None)
    odd_kept, odd_sent = place.fold_far(odd)
    odd_came = place.mixed(odd_sent, 1)
    even_came = place.mixed(even_sent, 0)
    d_normed = first_sum([after(d_others, odd_sent)], ((0, (0, 1, 2, 3)),), [others])
    odd_kept, odd_sent = place.fold_near(odd_kept, odd_came, BF)
    odd_came = place.mixed(odd_sent, 0)
    rows = first_back(
        embedded, d_middle, ident_rows, gains, d_normed, d_even, after(d_odd, odd_sent), mine
    )
    rows = after(rows, even_came, odd_came)
    total = lambda kept, came: kept.astype(F32) + came.astype(F32)
    both = jnp.concatenate([total(even_kept, even_came), total(odd_kept, odd_came)], axis=1)
    both = place.fold_outer(both, BF)
    even, odd = both[: even_kept.shape[1]], both[even_kept.shape[1] :]
    gain_rows = jnp.stack([jnp.sum(rows[2 * LAP :], axis=0), jnp.sum(gain_two, axis=0)])
    rows = jnp.concatenate([rows[: 2 * LAP], gain_rows], axis=0)
    row_count = rows.shape[0]
    rows = rows.T.reshape(devices, own_columns * row_count)
    rows = jnp.sum(lax.all_to_all(rows, ("dp", "head"), 0, 0, tiled=True), axis=0)
    rows = rows.reshape(own_columns, row_count)
    own_gains = lax.dynamic_slice_in_dim(gain_three, own_column, own_columns, 1)
    norm_parts = lax.all_to_all(
        squares([even, odd, grad_down, rows, own_gains], devices),
        ("dp", "head"),
        0,
        0,
        tiled=True,
    )
    own_half, other_half = even[:shard_rows], place.to_core(odd)
    halves = [place.by_core(own_half, other_half), place.by_core(other_half, own_half)]
    columns = lambda j: jnp.concatenate([v[:, j * SW : (j + 1) * SW] for v in halves], axis=1)
    grad_up = even[shard_rows:].reshape(2, own_columns, PACK)
    grads = (
        rows[:, : 2 * LAP],
        jnp.stack([columns(0), columns(1), columns(2)]),
        columns(3).T,
        jnp.stack([jnp.concatenate([grad_up[0], grad_up[1]], axis=1), grad_down]),
        jnp.concatenate([rows[:, 2 * LAP :].T, own_gains], axis=0),
    )
    turns = (lambda v: v.T, lambda v: v.transpose(1, 0, 2)) + (lambda v: v,) * 3
    state = [
        [turn(v) for turn, v in zip(turns, kind)]
        for kind in (
            (ident_weight, qkv_weight, out_weight, ffn_weight, norm_gains),
            (ident_first, qkv_first, out_first, ffn_first, gains_first),
            (ident_second, qkv_second, out_second, ffn_second, gains_second),
        )
    ]
    grad_norm, results = update(norm_parts, grads, state)
    return (grad_norm[0, 0], total_loss) + tuple(
        turn(v) for kind in results for turn, v in zip(turns, kind)
    )


def solution(mesh):
    both = P(None, ("dp", "head"))
    weights = (both, P("dp", None, "head"), P("head", "dp"), P(None, ("dp", "head"), None), both)
    in_specs = (P("dp", None),) * 5 + weights * 3
    out_specs = (P(), P()) + weights * 3
    return jax.shard_map(
        per_device, mesh=mesh, in_specs=in_specs, out_specs=out_specs, check_vma=False
    )
```
